32 devices in a mesh: cells: 16 (over z, y, core), spots: 2 (over x).
Axes of the slice: x: 2, y: 2, z: 4, core: 2. Of those that a mesh axis runs over, the one named last changes fastest.
Arguments:
- logits: bfloat16 [16384, 1024], P('cells', 'spots'), may hold values from -12 to 12
- expression: float32 [16384, 2048], P('cells'), may hold values from 0.1 to 10
- spatial: float32 [2, 512, 2048], P('spots', 'cells'), may hold values from 0.1 to 10
- slide_ids: int32 [2, 512], P('spots'), may hold values from 0 to 1
- spot_counts: int32 [2, 512], P('spots'), may hold values from 1 to 15
Outputs:
- predicted: float32 [2, 512, 2048], P('spots', 'cells')
- loss: float32 [], replicated
- logit_grad: float32 [16384, 1024], P('cells', 'spots')
- expr_grad: float32 [16384, 2048], P('cells')
The draws below stay inside these ranges and needn't reach their ends.
All inputs are finite; a program needn't handle non-finite values.
Results may differ from the reference program's by a relative error of at most 0.0046.
Values may be sent and summed in bfloat16 or wider, within the bound.
A program may use at most 128 MiB of HBM per device.

```python
import math
import jax
import jax.numpy as jnp
from jax import lax

GENES = 2048
CELLS = 16384
PH = 512
SPOTS = 1024
N_SPOTS = 2


def draw_logits(key, part):
    key = jax.random.fold_in(key, 11)
    kind_key, cell_key, noise_key = jax.random.split(key, 3)
    kinds = jax.random.randint(kind_key, (1, SPOTS), 0, 4)
    planted = jax.random.randint(cell_key, (1, SPOTS), 0, CELLS)
    rows = lax.broadcasted_iota(jnp.int32, (CELLS, SPOTS), 0)
    noise = jax.random.normal(noise_key, (CELLS, SPOTS), jnp.float32)
    broad = jnp.clip(3.0 * noise, -12.0, 12.0)
    flat = jnp.clip(noise, -12.0, 12.0)
    background = 1.5 + 0.5 * noise
    spiked = jnp.where(rows == planted, jnp.float32(12.0), background)
    values = jnp.where(kinds < 2, flat, jnp.where(kinds == 2, spiked, broad))
    return values.astype(jnp.bfloat16)


def set_ends(drawn, rng, smallest, largest):
    longest = drawn.shape.index(max(drawn.shape))
    spots = []
    for shift in (0, 1):
        where = [jax.random.randint(jax.random.fold_in(rng, axis), (), 0, length) for axis, length in enumerate(drawn.shape)]
        where[longest] = (where[longest] + shift) % drawn.shape[longest]
        spots.append(tuple(where))
    return drawn.at[spots[0]].set(smallest).at[spots[1]].set(largest)


def shard_levels(own_key, dims, pieces, smallest, high):
    loudness = 1.0
    for position, parts in pieces:
        steps = jax.random.uniform(jax.random.fold_in(jax.random.fold_in(own_key, 6), position), (parts,), jnp.float32, smallest / len(pieces), high / len(pieces))
        loudness = loudness * jnp.repeat(jnp.exp(steps), dims[position] // parts).reshape((-1,) + (1,) * (len(dims) - 1 - position))
    return loudness


def setup_inputs(seed: int = 0) -> dict:
    arg_keys = jax.random.split(jax.random.key(seed), 6)
    logits = draw_logits(jax.random.fold_in(arg_keys[5], 71), 0)
    expression = jnp.clip(jnp.exp(math.log(10.0) - 4.6051702 * jax.random.uniform(arg_keys[1], (CELLS, GENES), jnp.float32) ** shard_levels(arg_keys[1], (CELLS, GENES), ((0, 16),), -0.2, 0.2)), 0.1, 10.0)
    spatial = jnp.clip(jnp.exp(math.log(10.0) - 4.6051702 * jax.random.uniform(arg_keys[2], (N_SPOTS, PH, GENES), jnp.float32) ** shard_levels(arg_keys[2], (N_SPOTS, PH, GENES), ((0, 2), (1, 16)), -0.2, 0.2)), 0.1, 10.0)
    slide_ids = set_ends(jax.random.randint(arg_keys[3], (N_SPOTS, PH), 0, 2), jax.random.fold_in(arg_keys[3], 1), 0, 1).astype(jnp.int32)
    spot_counts = set_ends(jax.random.randint(arg_keys[4], (N_SPOTS, PH), 1, 16), jax.random.fold_in(arg_keys[4], 1), 1, 15).astype(jnp.int32)
    return dict(logits=logits, expression=expression, spatial=spatial, slide_ids=slide_ids, spot_counts=spot_counts)


EPSILON = 1e-06

@jax.custom_vjp
def low(v):
    return lax.optimization_barrier(v.astype(jnp.bfloat16)).astype(jnp.float32)

@jax.custom_vjp
def low_back(v):
    return v

def low_keep(v):
    return (low(v), None)

def low_pass(kept, grad):
    return (grad,)

def back_keep(v):
    return (v, None)

def back_low(kept, grad):
    return (low(grad),)
low.defvjp(low_keep, low_pass)
low_back.defvjp(back_keep, back_low)

def forward(scores, expression, spatial, slide_ids, spot_counts):
    highest = lax.Precision.HIGHEST
    width = math.gcd(SPOTS, 512)
    nblocks = SPOTS // width
    expr_low = low(expression)
    blocks = scores.reshape(CELLS, nblocks, width).transpose(1, 0, 2)

    def column_block(part):
        peak = lax.optimization_barrier(jnp.max(part, axis=0))
        shifted = jnp.exp(part - peak)
        total = lax.optimization_barrier(jnp.sum(shifted, axis=0))
        weights = low(shifted / total)
        block_pred = jnp.dot(weights.T, expr_low, precision=highest)
        return (block_pred, peak + jnp.log(total))
    preds, masses = lax.map(jax.checkpoint(column_block), blocks)
    predicted = low_back(preds.reshape(SPOTS, GENES))
    log_mass = masses.reshape(SPOTS)
    target = spatial.reshape(SPOTS, GENES)
    slide_flat = slide_ids.reshape(SPOTS)
    counts_real = spot_counts.reshape(SPOTS).astype(jnp.float32)
    member = (slide_flat[:, None] == jnp.arange(2, dtype=jnp.int32)[None, :]).astype(jnp.float32)
    gene_inner = jnp.dot(member.T, predicted * target, precision=highest)
    gene_pred = jnp.dot(member.T, predicted * predicted, precision=highest)
    gene_true = jnp.dot(member.T, target * target, precision=highest)
    gene_cos = gene_inner * lax.rsqrt(gene_pred + EPSILON) * lax.rsqrt(gene_true + EPSILON)
    spot_cos = lax.optimization_barrier(jnp.sum(predicted * target, axis=1)) * lax.rsqrt(lax.optimization_barrier(jnp.sum(predicted * predicted, axis=1)) + EPSILON) * lax.rsqrt(lax.optimization_barrier(jnp.sum(target * target, axis=1)) + EPSILON)
    slide_mass = jnp.dot(member.T, jnp.exp(log_mass), precision=highest)
    slide_count = jnp.dot(member.T, counts_real, precision=highest)
    share = counts_real / jnp.dot(member, slide_count, precision=highest)
    log_density = log_mass - jnp.log(jnp.dot(member, slide_mass, precision=highest))
    kl_value = jnp.sum(share * (jnp.log(share) - log_density))
    loss = -jnp.mean(gene_cos) - jnp.mean(spot_cos) + kl_value
    return (loss, predicted)

def reference(logits, expression, spatial, slide_ids, spot_counts):
    scores = logits.astype(jnp.float32)

    def wrapped(first, second):
        return forward(first, second, spatial, slide_ids, spot_counts)
    loss, pullback, predicted = jax.vjp(wrapped, scores, expression, has_aux=True)
    logit_grad, expr_grad = pullback(jnp.ones_like(loss))
    return (predicted.reshape(N_SPOTS, PH, GENES), loss, logit_grad, expr_grad)
```

```python
import functools

import jax
import jax.numpy as jnp
from jax import lax
from jax.experimental import pallas as pl
from jax.experimental.pallas import tpu as pltpu
from jax.sharding import PartitionSpec as P

EPSILON = 1e-06
MESH = pl.DeviceIdType.MESH
F32 = jnp.float32
BF16 = jnp.bfloat16
YK = 4


def forward_kernel(
    nz,
    nx,
    lg_hbm, ex_hbm, sp_hbm, ids_ref, cnt_ref,
    w_out, xl_out, g_out, p_out, vec_out, loss_out,
    lgv, lgo, et, exv, xl, pf, psib, ysend, yrecv, zsend, zrecv, g, wv, tgt, prd,
    s_own, s_sib, s_pair, s_y, s_quad, s_z, aux, gb, gsum, st, ssum, st1, st2,
    loc, snd, rcv,
):
    cells = lgv.shape[0]
    cols = lgv.shape[1]
    rows = cols // nz
    wide = exv.shape[2]
    part = rows // YK
    c = lax.axis_index("cells")
    x = lax.axis_index("spots")
    z = c // YK
    yk = c % YK
    y = yk // 2
    k = yk % 2
    sib_b = y * 2 + 1 - k
    y_b = (1 - y) * 2 + k
    dia_b = (1 - y) * 2 + 1 - k
    xo = (x + 1) % nx

    def dev(zz, bb, xx):
        return (zz * YK + bb, xx)

    sib, yp, dia, xp = dev(z, sib_b, x), dev(z, y_b, x), dev(z, dia_b, x), dev(z, yk, xo)
    yk_peers = ((sib, sib_b), (yp, y_b), (dia, dia_b))
    xz_peers = [
        (dev((z + dz) % nz, yk, (x + dx) % nx)) for dx in range(nx) for dz in range(nz) if dx or dz
    ]
    me_xz = x * nz + z

    count = [0]
    started = []

    def remote(src, dst, device):
        i = count[0]
        count[0] += 1
        cp = pltpu.make_async_remote_copy(
            src_ref=src, dst_ref=dst, send_sem=snd.at[i], recv_sem=rcv.at[i],
            device_id=device, device_id_type=MESH,
        )
        cp.start()
        started.append(cp)
        return cp

    nloc = [0]

    def local(src, dst):
        cp = pltpu.make_async_copy(src, dst, loc.at[nloc[0]])
        nloc[0] += 1
        cp.start()
        return cp

    barrier = pltpu.get_barrier_semaphore()
    for d in [p[0] for p in yk_peers] + xz_peers:
        pl.semaphore_signal(barrier, inc=1, device_id=d, device_id_type=MESH)

    lg_copy = local(lg_hbm, lgv)
    blocks = (dia_b, y_b, sib_b, yk)
    ex_copies = [
        local(ex_hbm.at[:, pl.ds(pl.multiple_of(b * wide, wide), wide)], exv.at[i])
        for i, b in enumerate(blocks)
    ]
    t_copy = local(sp_hbm.at[0, :, pl.ds(pl.multiple_of(yk * wide, wide), wide)], tgt.at[yk])

    lg_copy.wait()
    piece = 128
    total = jnp.zeros((1, cols), F32)
    total_low = jnp.zeros((1, cols), F32)
    for i in range(cells // piece):
        e = jnp.exp(lgv[pl.ds(i * piece, piece), :].astype(F32))
        low = e.astype(BF16).astype(F32)
        total = total + jnp.sum(e, axis=0, keepdims=True)
        total_low = total_low + jnp.sum(low, axis=0, keepdims=True)
        et[:, pl.ds(i * piece, piece)] = low.T.astype(BF16)
    s_own[0:1, :] = total
    s_own[1:2, :] = total_low

    pl.semaphore_wait(barrier, len(yk_peers) + len(xz_peers))
    t_in = [
        remote(sp_hbm.at[0, :, pl.ds(pl.multiple_of(b * wide, wide), wide)], tgt.at[yk], d)
        for d, b in yk_peers
    ]
    quarter = cells // 4
    lg_in = [
        remote(lg_hbm.at[pl.ds(i * quarter, quarter)], lgo.at[pl.ds(i * quarter, quarter)], xp)
        for i in range(4)
    ]
    s_sib_in = remote(s_own, s_sib, sib)

    half = wide // 2

    def forward(i):
        ex_copies[i].wait()
        for n in range(2):
            lanes = pl.ds(n * half, half)
            low = exv[i, :, lanes].astype(BF16)
            xl[blocks[i], :, lanes] = low
            pf[i, :, :, lanes] = jnp.dot(et[...], low, preferred_element_type=F32).reshape(
                nz, rows, half
            )

    order = [(z + r) % nz for r in range(1, nz)] + [z]
    forward(0)
    sib_in0 = [remote(pf.at[0, q], psib.at[0, q], sib) for q in order]
    forward(1)
    y_in = []
    for cp, q in zip(sib_in0, order, strict=True):
        cp.wait_recv()
        ysend[q] = (pf[1, q] + psib[0, q]).astype(BF16)
        y_in.append(remote(ysend.at[q], yrecv.at[q], yp))
    s_sib_in.wait_recv()
    s_pair[...] = s_own[...] + s_sib[...]
    s_y_in = remote(s_pair, s_y, yp)
    forward(2)
    sib_in1 = [remote(pf.at[2, q], psib.at[1, q], sib) for q in order]
    forward(3)
    s_y_in.wait_recv()
    s_quad[...] = s_pair[...] + s_y[...]
    s_z[z] = s_quad[...]
    s_z_in = [remote(s_quad, s_z.at[z], dev((z + r) % nz, yk, x)) for r in range(1, nz)]

    xl_copy = local(xl, xl_out)

    t_copy.wait()
    for cp in t_in:
        cp.wait_recv()
    here = pl.ds(pl.multiple_of(z * rows, rows), rows)
    eye = lax.broadcasted_iota(jnp.int32, (rows, rows), 0) == lax.broadcasted_iota(
        jnp.int32, (rows, rows), 1
    )

    def to_col(v):
        return jnp.sum(jnp.where(eye, jnp.broadcast_to(v, (rows, rows)), 0.0), axis=1, keepdims=True)

    def to_row(v):
        return jnp.sum(jnp.where(eye, jnp.broadcast_to(v, (rows, rows)), 0.0), axis=0, keepdims=True)

    slide = to_col(ids_ref[:, here].astype(F32))
    second = jnp.broadcast_to(slide > 0.5, (rows, wide))

    def by_slide(v):
        a = jnp.sum(jnp.where(second, 0.0, v), axis=0, keepdims=True)
        b = jnp.sum(jnp.where(second, v, 0.0), axis=0, keepdims=True)
        return a, b

    target = tgt[...].reshape(rows, wide)
    square = target * target
    b0, b1 = by_slide(square)
    gb[me_xz, 0:1, :] = b0
    gb[me_xz, 1:2, :] = b1
    st[yk] = to_row(jnp.sum(square, axis=1, keepdims=True))
    gb_in = [remote(gb.at[me_xz], gb.at[me_xz], d) for d in xz_peers]
    st_in = [remote(st.at[yk], st.at[yk], d) for d, _ in yk_peers]

    z_in = []
    for r, q in enumerate(order):
        sib_in1[r].wait_recv()
        y_in[r].wait_recv()
        term = pf[3, q] + psib[1, q] + yrecv[q].astype(F32)
        if r < nz - 1:
            zsend[q] = term.astype(BF16)
            z_in.append(remote(zsend.at[q], zrecv.at[z], dev(q, yk, x)))
        else:
            pred = term

    for cp in s_z_in:
        cp.wait_recv()
    sums = s_z[0]
    for q in range(1, nz):
        sums = sums + s_z[q]
    mass = sums[0:1, :]
    slides = ids_ref[...].astype(F32)
    counts = cnt_ref[...].astype(F32)
    aux[x, 0:1, :] = mass
    aux[x, 1:2, :] = slides
    aux[x, 2:3, :] = counts
    aux[x, 3:4, :] = jnp.zeros((1, cols), F32)
    aux_in = remote(aux.at[x], aux.at[x], xp)
    low_sum = s_z[0, 1:2, here]
    for q in range(1, nz):
        low_sum = low_sum + s_z[q, 1:2, here]
    low_col = to_col(low_sum)

    for r, cp in enumerate(z_in):
        cp.wait_recv()
        pred = pred + zrecv[(z + nz - 1 - r) % nz].astype(F32)
    inv_low = 1.0 / low_col
    pred = pred * inv_low
    prd[...] = pred.reshape(YK, part, wide)
    both = pred * target
    pair = pred * pred
    i0, i1 = by_slide(both)
    a0, a1 = by_slide(pair)
    for r, v in enumerate((i0, i1, a0, a1)):
        gsum[me_xz, r : r + 1, :] = v
    g_in = [remote(gsum.at[me_xz], gsum.at[me_xz], d) for d in xz_peers]
    ssum[yk, 0:1, :] = to_row(jnp.sum(both, axis=1, keepdims=True))
    ssum[yk, 1:2, :] = to_row(jnp.sum(pair, axis=1, keepdims=True))
    ss_in = [remote(ssum.at[yk], ssum.at[yk], d) for d, _ in yk_peers]
    p_in = [remote(prd.at[b], p_out.at[yk], d) for d, b in yk_peers]
    p_out[yk] = prd[yk]

    for cp in gb_in + st_in + ss_in + g_in:
        cp.wait_recv()

    def added(ref, n):
        v = ref[0]
        for q in range(1, n):
            v = v + ref[q]
        return v

    genes = YK * wide
    spots = nx * cols
    gene_step = -1.0 / (2 * genes)
    spot_step = -1.0 / spots
    gs = added(gsum, nx * nz)
    gt = added(gb, nx * nz)
    gene_a = lax.rsqrt(gs[2:4] + EPSILON)
    gene_b = lax.rsqrt(gt + EPSILON)
    gene_cos = gs[0:2] * gene_a * gene_b
    t_gene = gene_step * gene_a * gene_b
    p_gene = -gene_step * gs[0:2] * gene_b * gene_a * gene_a * gene_a
    ss = added(ssum, YK)
    pred_scale = lax.rsqrt(ss[1:2] + EPSILON)
    true_scale = lax.rsqrt(added(st, YK) + EPSILON)
    spot_cos = ss[0:1] * pred_scale * true_scale
    t_spot = to_col(spot_step * pred_scale * true_scale)
    p_spot = to_col(-spot_step * ss[0:1] * pred_scale * pred_scale * pred_scale * true_scale)
    t_row = jnp.where(
        second, jnp.broadcast_to(t_gene[1:2], (rows, wide)), jnp.broadcast_to(t_gene[0:1], (rows, wide))
    )
    p_row = jnp.where(
        second, jnp.broadcast_to(p_gene[1:2], (rows, wide)), jnp.broadcast_to(p_gene[0:1], (rows, wide))
    )
    grad = (t_row + t_spot) * target + (p_row + p_spot) * pred
    low = grad.astype(BF16)
    for h in range(2):
        g[me_xz, yk, h] = low[:, h * half : (h + 1) * half]

    own = g.at[me_xz, yk]
    y_first = [remote(own, own, yp)]
    x_first = [remote(own, own, xp)]
    g_z_in = [remote(own, own, dev((z + r) % nz, yk, x)) for r in range(1, nz)]
    sib_all = [remote(own, own, sib)]

    inner = to_row(jnp.sum(low.astype(F32) * pred, axis=1, keepdims=True))
    lane = lax.broadcasted_iota(jnp.int32, (1, rows), 1)
    st1[yk, 0:1, :] = inner
    st1[yk, 1:2, :] = jnp.where(lane == 0, jnp.sum(gene_cos), 0.0)
    st1_in = [remote(st1.at[yk], st1.at[yk], d) for d, _ in yk_peers]

    def weights(src, scale, to):
        for i in range(cells // piece):
            r = pl.ds(i * piece, piece)
            wv[to, r, :] = (jnp.exp(src[r, :].astype(F32)) * scale).astype(BF16)

    inv_mass = 1.0 / mass
    weights(lgv, inv_mass, x)

    diag_x, diag_y = [], []
    for r in range(nz):
        zr = (z + nz - r) % nz
        if r:
            g_z_in[r - 1].wait_recv()
            shard = g.at[x * nz + zr, yk]
            y_first.append(remote(shard, shard, yp))
            x_first.append(remote(shard, shard, xp))
            sib_all.append(remote(shard, shard, sib))
        if r == 1:
            for cp in st1_in:
                cp.wait_recv()
            whole = added(st1, YK)
            st2[me_xz, 0:1, :] = whole[0:1]
            st2[me_xz, 1:2, :] = jnp.where(
                lane == 0, whole[1:2], jnp.where(lane == 1, jnp.sum(spot_cos), 0.0)
            )
            st2_in = [remote(st2.at[me_xz], st2.at[me_xz], d) for d in xz_peers]
            aux_in.wait_recv()
            for cp in lg_in:
                cp.wait_recv()
            weights(lgo, 1.0 / aux[xo, 0:1, :], xo)
            w_copy = local(wv, w_out)
        y_first[r].wait_recv()
        shard = g.at[x * nz + zr, y_b]
        diag_x.append(remote(shard.at[0], shard.at[0], xp))
        sib_all.append(remote(shard, shard, sib))
        x_first[r].wait_recv()
        shard = g.at[xo * nz + zr, yk]
        diag_y.append(remote(shard.at[1], shard.at[1], yp))
        sib_all.append(remote(shard, shard, sib))

    for cp in st2_in:
        cp.wait_recv()
    kl = 0.0
    slide_mass, slide_count = [], []
    for s in range(2):
        m = n = cl = cm = 0.0
        for q in range(nx):
            mine = jnp.abs(aux[q, 1:2, :] - s) < 0.5
            n_q = jnp.where(mine, aux[q, 2:3, :], 0.0)
            m = m + jnp.sum(jnp.where(mine, aux[q, 0:1, :], 0.0))
            n = n + jnp.sum(n_q)
            cl = cl + jnp.sum(n_q * jnp.log(aux[q, 2:3, :]))
            cm = cm + jnp.sum(n_q * jnp.log(aux[q, 0:1, :]))
        some = n > 0.5
        m = jnp.full((1, 128), jnp.where(some, m, 1.0), F32)
        n = jnp.full((1, 128), jnp.where(some, n, 1.0), F32)
        kl = kl + jnp.where(some, (cl - cm) / n - jnp.log(n) + jnp.log(m), 0.0)
        slide_mass.append(m[:, 0:1])
        slide_count.append(n[:, 0:1])
    gene_total = whole[1:2]
    spot_total = added(st2, nx * nz)[1:2]
    loss_out[...] = (
        -jnp.sum(jnp.where(lane == 0, gene_total, 0.0)) / (2 * genes)
        - jnp.sum(jnp.where(lane == 1, spot_total, 0.0)) / spots
        + kl
    )
    is_second = slides > 0.5
    mass_grad = mass / jnp.where(is_second, slide_mass[1], slide_mass[0]) - counts / jnp.where(
        is_second, slide_count[1], slide_count[0]
    )
    vec_out[0:1, :] = inv_mass
    for q in range(nz):
        lanes = pl.ds(q * rows, rows)
        vec_out[1:2, lanes] = mass_grad[:, q * rows : (q + 1) * rows] - st2[x * nz + q, 0:1, :]

    for r in range(nz):
        zr = (z + nz - r) % nz
        shard = g.at[xo * nz + zr, y_b]
        diag_x[r].wait_recv()
        sib_all.append(remote(shard.at[0], shard.at[0], sib))
        diag_y[r].wait_recv()
        sib_all.append(remote(shard.at[1], shard.at[1], sib))
    for cp in sib_all + p_in:
        cp.wait_recv()
    g_copy = local(g, g_out)
    for cp in started:
        cp.wait_send()
    xl_copy.wait()
    w_copy.wait()
    g_copy.wait()


def backward_kernel(
    nz, w_ref, xl_ref, g_ref, lg_ref, vec_ref, p_ref, loss_ref, eg_ref, lgrad_ref, pred_ref, total_ref, acc
):
    i = pl.program_id(0)
    x = lax.axis_index("spots")
    nx = w_ref.shape[0]
    cols = lg_ref.shape[1]
    wide = g_ref.shape[4]
    out = jnp.zeros(eg_ref.shape, F32)
    for q in range(nx):
        block = g_ref[q * nz : (q + 1) * nz, 0, 0].reshape(cols, wide)
        out = out + jnp.dot(w_ref[q], block, preferred_element_type=F32)
    eg_ref[...] = out
    mine = g_ref[pl.ds(x * nz, nz), 0, 0].reshape(cols, wide)
    term = lax.dot_general(
        xl_ref[0], mine, (((1,), (1,)), ((), ())), preferred_element_type=F32
    )

    @pl.when(i == 0)
    def _():
        acc[...] = term
        total_ref[...] = loss_ref[:, 0:1]
        for b in range(YK):
            w = p_ref.shape[2]
            pred_ref[:, b * w : (b + 1) * w] = p_ref[b]

    @pl.when(i > 0)
    def _():
        acc[...] += term

    @pl.when(i == pl.num_programs(0) - 1)
    def _():
        e = jnp.exp(lg_ref[...].astype(F32)) * vec_ref[0:1, :]
        lgrad_ref[...] = e * (acc[...] + vec_ref[1:2, :])


def step(ncells, nx, logits, expression, spatial, slide_ids, spot_counts):
    cells, cols = logits.shape
    genes = expression.shape[1]
    nz = ncells // YK
    rows = cols // nz
    wide = genes // YK
    part = rows // YK
    half = wide // 2
    copies = 320
    anywhere = pl.BlockSpec(memory_space=pl.ANY)
    whole = pl.BlockSpec(memory_space=pltpu.VMEM)
    w, xl, g, p, vec, loss = pl.pallas_call(
        functools.partial(forward_kernel, nz, nx),
        out_shape=(
            jax.ShapeDtypeStruct((nx, cells, cols), BF16),
            jax.ShapeDtypeStruct((YK, cells, wide), BF16),
            jax.ShapeDtypeStruct((nx * nz, YK, 2, rows, half), BF16),
            jax.ShapeDtypeStruct((YK, part, wide), F32),
            jax.ShapeDtypeStruct((8, cols), F32),
            jax.ShapeDtypeStruct((1, 128), F32),
        ),
        in_specs=[anywhere, anywhere, anywhere, whole, whole],
        out_specs=(anywhere, anywhere, anywhere, whole, whole, whole),
        scratch_shapes=[
            pltpu.VMEM((cells, cols), BF16),
            pltpu.VMEM((cells, cols), BF16),
            pltpu.VMEM((cols, cells), BF16),
            pltpu.VMEM((YK, cells, wide), F32),
            pltpu.VMEM((YK, cells, wide), BF16),
            pltpu.VMEM((YK, nz, rows, wide), F32),
            pltpu.VMEM((2, nz, rows, wide), F32),
            pltpu.VMEM((nz, rows, wide), BF16),
            pltpu.VMEM((nz, rows, wide), BF16),
            pltpu.VMEM((nz, rows, wide), BF16),
            pltpu.VMEM((nz, rows, wide), BF16),
            pltpu.VMEM((nx * nz, YK, 2, rows, half), BF16),
            pltpu.VMEM((nx, cells, cols), BF16),
            pltpu.VMEM((YK, part, wide), F32),
            pltpu.VMEM((YK, part, wide), F32),
            pltpu.VMEM((2, cols), F32),
            pltpu.VMEM((2, cols), F32),
            pltpu.VMEM((2, cols), F32),
            pltpu.VMEM((2, cols), F32),
            pltpu.VMEM((2, cols), F32),
            pltpu.VMEM((nz, 2, cols), F32),
            pltpu.VMEM((nx, 4, cols), F32),
            pltpu.VMEM((nx * nz, 2, wide), F32),
            pltpu.VMEM((nx * nz, 4, wide), F32),
            pltpu.VMEM((YK, 1, rows), F32),
            pltpu.VMEM((YK, 2, rows), F32),
            pltpu.VMEM((YK, 2, rows), F32),
            pltpu.VMEM((nx * nz, 2, rows), F32),
            pltpu.SemaphoreType.DMA((16,)),
            pltpu.SemaphoreType.DMA((copies,)),
            pltpu.SemaphoreType.DMA((copies,)),
        ],
        compiler_params=pltpu.CompilerParams(
            collective_id=0, has_side_effects=True, vmem_limit_bytes=56 << 20
        ),
        name="forward_and_gather",
    )(logits, expression, spatial, slide_ids, spot_counts)

    return pl.pallas_call(
        functools.partial(backward_kernel, nz),
        grid=(genes // half,),
        out_shape=(
            jax.ShapeDtypeStruct((cells, genes), F32),
            jax.ShapeDtypeStruct((cells, cols), F32),
            jax.ShapeDtypeStruct((part, genes), F32),
            jax.ShapeDtypeStruct((1, 1), F32),
        ),
        in_specs=[
            pl.BlockSpec((nx, cells, cols), lambda i: (0, 0, 0)),
            pl.BlockSpec((1, cells, half), lambda i: (i // 2, 0, i % 2)),
            pl.BlockSpec((nx * nz, 1, 1, rows, half), lambda i: (0, i // 2, i % 2, 0, 0)),
            pl.BlockSpec((cells, cols), lambda i: (0, 0)),
            pl.BlockSpec((8, cols), lambda i: (0, 0)),
            pl.BlockSpec((YK, part, wide), lambda i: (0, 0, 0)),
            pl.BlockSpec((1, 128), lambda i: (0, 0)),
        ],
        out_specs=(
            pl.BlockSpec((cells, half), lambda i: (0, i)),
            pl.BlockSpec((cells, cols), lambda i: (0, 0)),
            pl.BlockSpec((part, genes), lambda i: (0, 0)),
            pl.BlockSpec((1, 1), lambda i: (0, 0)),
        ),
        scratch_shapes=[pltpu.VMEM((cells, cols), F32)],
        compiler_params=pltpu.CompilerParams(vmem_limit_bytes=56 << 20),
        name="backward",
    )(w, xl, g, logits, vec, p, loss)


def kernel_step(ncells, nx, *args):
    grad_expr, grad_logits, predicted, loss = step(ncells, nx, *args)
    return (predicted[None], loss[0, 0], grad_logits, grad_expr)


def fits(ncells, nx, logits, expression, spatial):
    cells, cols = logits.shape
    genes = expression.shape[1]
    if ncells % YK or nx != 2 or cols % (ncells // YK) or genes % (YK * 256):
        return False
    rows = cols // (ncells // YK)
    held = (cells + rows) * genes * 8 + cells * cols * 16 + cols * genes * 16
    return rows % 128 == 0 and cells % 128 == 0 and held < 50 << 20


def plain_step(logits, expression, spatial, slide_ids, spot_counts):
    highest = lax.Precision.HIGHEST
    ncells = lax.axis_size("cells")
    nspots = lax.axis_size("spots")
    columns = logits.shape[1]
    genes = expression.shape[1]
    out_rows = columns // ncells
    scores = logits.astype(F32)
    col_peak = lax.pmax(jnp.max(scores, axis=0), "cells")
    shifted = jnp.exp(scores - col_peak)
    col_total = lax.psum(jnp.sum(shifted, axis=0), "cells")
    weights = shifted / col_total
    log_mass = col_peak + jnp.log(col_total)
    weights_low = weights.astype(BF16)
    expr_low = expression.astype(BF16)
    contract_first = (((0,), (0,)), ((), ()))
    predicted = lax.psum_scatter(
        lax.dot_general(weights_low, expr_low, contract_first, preferred_element_type=F32),
        "cells",
        scatter_dimension=0,
        tiled=True,
    )
    target = spatial[0]
    member_all = (slide_ids[0][:, None] == jnp.arange(2, dtype=jnp.int32)[None, :]).astype(F32)
    first_row = lax.axis_index("cells") * out_rows
    member_rows = lax.dynamic_slice_in_dim(member_all, first_row, out_rows, 0)
    gene_inner = jnp.dot(member_rows.T, predicted * target, precision=highest)
    gene_pred = jnp.dot(member_rows.T, predicted * predicted, precision=highest)
    gene_true = jnp.dot(member_rows.T, target * target, precision=highest)
    spot_inner = jnp.sum(predicted * target, axis=1)
    pred_scale = lax.rsqrt(jnp.sum(predicted * predicted, axis=1) + EPSILON)
    true_scale = lax.rsqrt(jnp.sum(target * target, axis=1) + EPSILON)
    spot_sum = jnp.sum(spot_inner * pred_scale * true_scale)
    counts_real = spot_counts[0].astype(F32)
    exp_mass = jnp.exp(log_mass)
    local_mass = jnp.dot(member_all.T, exp_mass, precision=highest)
    local_count = jnp.dot(member_all.T, counts_real, precision=highest)
    local_clog = jnp.dot(member_all.T, counts_real * jnp.log(counts_real), precision=highest)
    local_clse = jnp.dot(member_all.T, counts_real * log_mass, precision=highest)
    slide_mass, slide_count, count_log, count_lse = lax.psum(
        (local_mass, local_count, local_clog, local_clse), "spots"
    )
    gene_inner, gene_pred, gene_true, spot_total = lax.psum(
        (gene_inner, gene_pred, gene_true, spot_sum), ("cells", "spots")
    )
    gene_a = lax.rsqrt(gene_pred + EPSILON)
    gene_b = lax.rsqrt(gene_true + EPSILON)
    gene_cos = gene_inner * gene_a * gene_b
    total_spots = columns * nspots
    some = slide_count > 0.5
    slide_count = jnp.where(some, slide_count, 1.0)
    slide_mass = jnp.where(some, slide_mass, 1.0)
    kl_value = jnp.sum(
        jnp.where(
            some,
            (count_log - count_lse) / slide_count - jnp.log(slide_count) + jnp.log(slide_mass),
            0.0,
        )
    )
    loss = -jnp.mean(gene_cos) - spot_total / total_spots + kl_value
    gene_step = -1.0 / (2 * genes)
    inner_grad = gene_step * gene_a * gene_b
    square_grad = -0.5 * gene_step * gene_inner * gene_b * gene_a * gene_a * gene_a
    pred_grad = jnp.dot(member_rows, inner_grad, precision=highest) * target
    pred_grad = pred_grad + 2.0 * jnp.dot(member_rows, square_grad, precision=highest) * predicted
    spot_step = -1.0 / total_spots
    pred_grad = pred_grad + (spot_step * pred_scale * true_scale)[:, None] * target
    pred_grad = (
        pred_grad
        - (spot_step * spot_inner * pred_scale * pred_scale * pred_scale * true_scale)[:, None]
        * predicted
    )
    grad_low = pred_grad.astype(BF16)
    mass_grad = exp_mass / jnp.dot(
        member_all, slide_mass, precision=highest
    ) - counts_real / jnp.dot(member_all, slide_count, precision=highest)
    contract_genes = (((1,), (1,)), ((), ()))
    grad_all = lax.all_gather(grad_low, "cells", axis=0, tiled=True)
    expr_part = jnp.dot(weights_low, grad_all, preferred_element_type=F32)
    weight_grad = lax.dot_general(
        expr_low, grad_all, contract_genes, preferred_element_type=F32
    )
    col_inner = lax.psum(jnp.sum(weights * weight_grad, axis=0), "cells")
    logit_grad = weights * (weight_grad - col_inner + mass_grad)
    expr_grad = lax.psum(expr_part, "spots")
    return (predicted[None], loss, logit_grad, expr_grad)


def solution(mesh):
    ncells, nx = mesh.shape["cells"], mesh.shape["spots"]

    def per_device(*args):
        if fits(ncells, nx, *args[:3]):
            return kernel_step(ncells, nx, *args)
        return plain_step(*args)

    return jax.shard_map(
        per_device,
        mesh=mesh,
        in_specs=(
            P("cells", "spots"),
            P("cells", None),
            P("spots", "cells", None),
            P("spots", None),
            P("spots", None),
        ),
        out_specs=(P("spots", "cells", None), P(), P("cells", "spots"), P("cells", None)),
        check_vma=False,
    )
```

```python
import functools

import jax
import jax.numpy as jnp
from jax import lax
from jax.experimental import pallas as pl
from jax.experimental.pallas import tpu as pltpu
from jax.sharding import PartitionSpec as P

EPSILON = 1e-06
MESH = pl.DeviceIdType.MESH
F32 = jnp.float32
BF16 = jnp.bfloat16
YK = 4


def forward_kernel(
    nz,
    nx,
    lg_hbm, ex_hbm, sp_hbm, ids_hbm, cnt_hbm,
    wv, xl, g, p_out, vec_out, loss_out,
    lgv, lgo, et, exv, pf, psib, ysend, yrecv, zsend, zrecv, tgt, prd,
    s_own, s_sib, s_pair, s_y, s_quad, s_z, aux, gsum, ssum, st1, st2, ids_ref, cnt_ref,
    loc, snd, rcv,
):
    cells, cols = lgv.shape
    rows, half = pf.shape[3:]
    wide = 2 * half
    part = rows // YK
    c = lax.axis_index("cells")
    x = lax.axis_index("spots")
    z = c // YK
    yk = c % YK
    y = yk // 2
    k = yk % 2
    sib_b = y * 2 + 1 - k
    y_b = (1 - y) * 2 + k
    dia_b = (1 - y) * 2 + 1 - k
    xo = (x + 1) % nx
    me = x * nz + z

    def dev(zz, bb, xx):
        return (zz * YK + bb, xx)

    sib, yp, dia, xp = dev(z, sib_b, x), dev(z, y_b, x), dev(z, dia_b, x), dev(z, yk, xo)
    yk_peers = ((sib, sib_b), (yp, y_b), (dia, dia_b))
    xz_peers = [
        dev((z + dz) % nz, yk, (x + dx) % nx) for dx in range(nx) for dz in range(nz) if dx or dz
    ]

    taken = [0, 0]
    started = []

    def sems(n):
        taken[0] += n
        return taken[0] - n

    def describe(src, dst, device, send, recv):
        return pltpu.make_async_remote_copy(
            src_ref=src, dst_ref=dst, send_sem=snd.at[send], recv_sem=rcv.at[recv],
            device_id=device, device_id_type=MESH,
        )

    def remote(src, dst, device):
        i = sems(1)
        cp = describe(src, dst, device, i, i)
        cp.start()
        started.append(cp)
        return cp

    def local(src, dst):
        cp = pltpu.make_async_copy(src, dst, loc.at[taken[1]])
        taken[1] += 1
        cp.start()
        return cp

    barrier = pltpu.get_barrier_semaphore()
    for d in [p[0] for p in yk_peers] + xz_peers:
        pl.semaphore_signal(barrier, inc=1, device_id=d, device_id_type=MESH)

    def genes_of(ref, b):
        return ref.at[..., pl.ds(pl.multiple_of(b * wide, wide), wide)]

    blocks = (dia_b, y_b, sib_b, yk)
    lg_copy = local(lg_hbm, lgv)
    ex_copies = [local(genes_of(ex_hbm, b), exv.at[i]) for i, b in enumerate(blocks)]
    late = [
        local(genes_of(sp_hbm.at[0], yk), tgt.at[yk]),
        local(ids_hbm, ids_ref),
        local(cnt_hbm, cnt_ref),
    ]

    lg_copy.wait()
    piece = 128
    total = jnp.zeros((1, cols), F32)
    total_low = jnp.zeros((1, cols), F32)
    for i in range(cells // piece):
        e = jnp.exp(lgv[pl.ds(i * piece, piece), :].astype(F32))
        low = e.astype(BF16).astype(F32)
        total = total + jnp.sum(e, axis=0, keepdims=True)
        total_low = total_low + jnp.sum(low, axis=0, keepdims=True)
        et[:, pl.ds(i * piece, piece)] = low.T.astype(BF16)
    s_own[0:1, :] = total
    s_own[1:2, :] = total_low

    def forward(i):
        ex_copies[i].wait()
        for n in range(2):
            lanes = pl.ds(n * half, half)
            low = exv[i, :, lanes].astype(BF16)
            xl[blocks[i], :, lanes] = low
            pf[i, n] = jnp.dot(et[...], low, preferred_element_type=F32).reshape(nz, rows, half)

    forward(0)
    forward(1)

    pl.semaphore_wait(barrier, len(yk_peers) + len(xz_peers))
    s_sib_in = remote(s_own, s_sib, sib)
    others = [(z + r) % nz for r in range(1, nz)]
    others = others[1:2] + others[:1] + others[2:]
    to_y = [(n, q) for n in range(2) for q in others] + [(0, z), (1, z)]
    sib_in = {}
    for n, q in to_y:
        sib_in[0, n, id(q)] = remote(pf.at[0, n, q], psib.at[0, n, q], sib)
    lg_in = remote(lg_hbm, lgo, xp)
    s_sib_in.wait_recv()
    s_pair[...] = s_own[...] + s_sib[...]
    s_y_in = remote(s_pair, s_y, yp)
    y_in = {}

    def send_y(n, q):
        sib_in[0, n, id(q)].wait_recv()
        ysend[n, q] = (pf[1, n, q] + psib[0, n, q]).astype(BF16)
        y_in[n, id(q)] = remote(ysend.at[n, q], yrecv.at[n, q], yp)

    for n, q in to_y[:-2]:
        send_y(n, q)
    t_in = [remote(genes_of(sp_hbm.at[0], b), tgt.at[yk], d) for d, b in yk_peers]
    for n, q in to_y[-2:]:
        send_y(n, q)
    forward(2)
    for n in range(2):
        sib_in[1, n] = remote(pf.at[2, n], psib.at[1, n], sib)
    forward(3)
    s_y_in.wait_recv()
    s_quad[...] = s_pair[...] + s_y[...]
    s_z[z] = s_quad[...]
    s_z_in = [remote(s_quad, s_z.at[z], dev(q, yk, x)) for q in others]

    z_in = []
    mine = []
    for i, (n, q) in enumerate(to_y):
        if i in (0, nz - 1):
            sib_in[1, i // (nz - 1)].wait_recv()
        y_in[n, id(q)].wait_recv()
        term = pf[3, n, q] + psib[1, n, q] + yrecv[n, q].astype(F32)
        if q is z:
            mine.append(term)
        else:
            zsend[n, q] = term.astype(BF16)
            z_in.append(remote(zsend.at[n, q], zrecv.at[n, z], dev(q, yk, x)))

    for cp in late:
        cp.wait()
    for cp in s_z_in:
        cp.wait_recv()
    sums = s_z[0]
    for q in range(1, nz):
        sums = sums + s_z[q]
    mass = sums[0:1, :]
    inv_mass = 1.0 / mass
    slides = ids_ref[...].astype(F32)
    counts = cnt_ref[...].astype(F32)
    aux[x, 0:1, :] = mass
    aux[x, 1:2, :] = slides
    aux[x, 2:3, :] = counts
    aux[x, 3:4, :] = jnp.zeros((1, cols), F32)
    aux_in = remote(aux.at[x], aux.at[x], xp)

    here = pl.ds(pl.multiple_of(z * rows, rows), rows)
    eye = lax.broadcasted_iota(jnp.int32, (rows, rows), 0) == lax.broadcasted_iota(
        jnp.int32, (rows, rows), 1
    )

    def to_col(v):
        return jnp.sum(jnp.where(eye, jnp.broadcast_to(v, (rows, rows)), 0.0), axis=1, keepdims=True)

    def to_row(v):
        return jnp.sum(jnp.where(eye, jnp.broadcast_to(v, (rows, rows)), 0.0), axis=0, keepdims=True)

    slide = to_col(ids_ref[:, here].astype(F32))
    second = jnp.broadcast_to(slide > 0.5, (rows, wide))
    low_sum = s_z[0, 1:2, here]
    for q in range(1, nz):
        low_sum = low_sum + s_z[q, 1:2, here]
    inv_low = 1.0 / to_col(low_sum)

    def by_slide(v):
        a = jnp.sum(jnp.where(second, 0.0, v), axis=0, keepdims=True)
        b = jnp.sum(jnp.where(second, v, 0.0), axis=0, keepdims=True)
        return a, b

    for cp in t_in:
        cp.wait_recv()
    target = tgt[...].reshape(rows, wide)
    square = target * target

    for cp in z_in:
        cp.wait_recv()
    for n in range(2):
        for r in range(1, nz):
            mine[n] = mine[n] + zrecv[n, (z + r) % nz].astype(F32)
    pred = jnp.concatenate(mine, axis=1) * inv_low
    both = pred * target
    pair = pred * pred
    for r, v in enumerate((both, pair, square)):
        a, b = by_slide(v)
        gsum[me, 2 * r : 2 * r + 1, :] = a
        gsum[me, 2 * r + 1 : 2 * r + 2, :] = b
        ssum[yk, r : r + 1, :] = to_row(jnp.sum(v, axis=1, keepdims=True))
    sum_in = [remote(gsum.at[me], gsum.at[me], d) for d in xz_peers]
    sum_in += [remote(ssum.at[yk], ssum.at[yk], d) for d, _ in yk_peers]
    prd[...] = pred.reshape(YK, part, wide)
    p_in = [remote(prd.at[b], p_out.at[yk], d) for d, b in yk_peers]
    p_out[yk] = prd[yk]

    def weights(src, scale, to):
        for i in range(cells // piece):
            r = pl.ds(i * piece, piece)
            wv[to, r, :] = (jnp.exp(src[r, :].astype(F32)) * scale).astype(BF16)

    weights(lgv, inv_mass, x)
    for cp in sum_in:
        cp.wait_recv()

    def added(ref, n):
        v = ref[0]
        for q in range(1, n):
            v = v + ref[q]
        return v

    genes = YK * wide
    spots = nx * cols
    gene_step = -1.0 / (2 * genes)
    spot_step = -1.0 / spots
    gs = added(gsum, nx * nz)
    gene_a = lax.rsqrt(gs[2:4] + EPSILON)
    gene_b = lax.rsqrt(gs[4:6] + EPSILON)
    gene_cos = gs[0:2] * gene_a * gene_b
    t_gene = gene_step * gene_a * gene_b
    p_gene = -gene_step * gs[0:2] * gene_b * gene_a * gene_a * gene_a
    ss = added(ssum, YK)
    pred_scale = lax.rsqrt(ss[1:2] + EPSILON)
    true_scale = lax.rsqrt(ss[2:3] + EPSILON)
    spot_cos = ss[0:1] * pred_scale * true_scale
    t_spot = to_col(spot_step * pred_scale * true_scale)
    p_spot = to_col(-spot_step * ss[0:1] * pred_scale * pred_scale * pred_scale * true_scale)

    def of_slide(v):
        return jnp.where(
            second, jnp.broadcast_to(v[1:2], (rows, wide)), jnp.broadcast_to(v[0:1], (rows, wide))
        )

    grad = (of_slide(t_gene) + t_spot) * target + (of_slide(p_gene) + p_spot) * pred
    low = grad.astype(BF16)
    for h in range(2):
        g[me, yk, h] = low[:, h * half : (h + 1) * half]

    up, down, along_z, over_y, over_x = (sems(nz) for _ in range(5))
    diag_x, diag_y, core_own, core_y, core_x, core_a, core_b = (sems(nz) for _ in range(7))

    def put(shard, device, send, recv=None):
        describe(shard, shard, device, send, send if recv is None else recv).start()

    def arrived(shard, recv):
        describe(shard, shard, sib, recv, recv).wait_recv()

    def sent(shard, send):
        describe(shard, shard, sib, send, send).wait_send()

    def spread(q):
        shard = g.at[x * nz + q, yk]
        put(shard, yp, over_y + q)
        put(shard, xp, over_x + q)
        put(shard, sib, core_own + q)

    def take_z(q, above):
        shard = g.at[x * nz + q, yk]
        arrived(shard, along_z + q)

        if above:

            @pl.when(z > 0)
            def _():
                put(shard, dev(z - 1, yk, x), down + q, along_z + q)

        else:

            @pl.when(z < nz - 1)
            def _():
                put(shard, dev(z + 1, yk, x), up + q, along_z + q)

        spread(q)

    def take_yx(q):
        shard = g.at[x * nz + q, y_b]
        arrived(shard, over_y + q)
        put(shard.at[0], xp, diag_x + q)
        put(shard, sib, core_y + q)
        shard = g.at[xo * nz + q, yk]
        arrived(shard, over_x + q)
        put(shard.at[1], yp, diag_y + q)
        put(shard, sib, core_x + q)

    spread(z)

    @pl.when(z > 0)
    def _():
        own = g.at[me, yk]
        put(own, dev(z - 1, yk, x), down + z, along_z + z)

    @pl.when(z < nz - 1)
    def _():
        own = g.at[me, yk]
        put(own, dev(z + 1, yk, x), up + z, along_z + z)

    inner = to_row(jnp.sum(low.astype(F32) * pred, axis=1, keepdims=True))
    lane = lax.broadcasted_iota(jnp.int32, (1, rows), 1)
    st1[yk, 0:1, :] = inner
    st1[yk, 1:2, :] = jnp.where(lane == 0, jnp.sum(gene_cos), 0.0)
    st1_in = [remote(st1.at[yk], st1.at[yk], d) for d, _ in yk_peers]

    for d in range(1, nz + 1):
        if d < nz:

            @pl.when(z >= d)
            def _():
                take_z(z - d, False)

            @pl.when(z < nz - d)
            def _():
                take_z(z + d, True)

        if d == 1:
            take_yx(z)
        else:

            @pl.when(z >= d - 1)
            def _():
                take_yx(z - d + 1)

            @pl.when(z < nz - d + 1)
            def _():
                take_yx(z + d - 1)

    for cp in st1_in:
        cp.wait_recv()
    whole = added(st1, YK)
    st2[me, 0:1, :] = whole[0:1]
    st2[me, 1:2, :] = jnp.where(lane == 0, whole[1:2], jnp.where(lane == 1, jnp.sum(spot_cos), 0.0))
    st2_in = [remote(st2.at[me], st2.at[me], d) for d in xz_peers]
    aux_in.wait_recv()
    lg_in.wait_recv()
    weights(lgo, 1.0 / aux[xo, 0:1, :], xo)

    kl = 0.0
    slide_mass, slide_count = [], []
    for s in range(2):
        m = n = cl = cm = 0.0
        for q in range(nx):
            of_s = jnp.abs(aux[q, 1:2, :] - s) < 0.5
            n_q = jnp.where(of_s, aux[q, 2:3, :], 0.0)
            m = m + jnp.sum(jnp.where(of_s, aux[q, 0:1, :], 0.0))
            n = n + jnp.sum(n_q)
            cl = cl + jnp.sum(n_q * jnp.log(aux[q, 2:3, :]))
            cm = cm + jnp.sum(n_q * jnp.log(aux[q, 0:1, :]))
        some = n > 0.5
        m = jnp.full((1, 128), jnp.where(some, m, 1.0), F32)
        n = jnp.full((1, 128), jnp.where(some, n, 1.0), F32)
        kl = kl + jnp.where(some, (cl - cm) / n - jnp.log(n) + jnp.log(m), 0.0)
        slide_mass.append(m[:, 0:1])
        slide_count.append(n[:, 0:1])
    is_second = slides > 0.5
    mass_grad = mass / jnp.where(is_second, slide_mass[1], slide_mass[0]) - counts / jnp.where(
        is_second, slide_count[1], slide_count[0]
    )

    for q in range(nz):
        shard = g.at[xo * nz + q, y_b]
        arrived(shard.at[0], diag_x + q)
        put(shard.at[0], sib, core_a + q)
        arrived(shard.at[1], diag_y + q)
        put(shard.at[1], sib, core_b + q)

    for cp in st2_in:
        cp.wait_recv()
    gene_total = whole[1:2]
    spot_total = added(st2, nx * nz)[1:2]
    loss_out[...] = (
        -jnp.sum(jnp.where(lane == 0, gene_total, 0.0)) / (2 * genes)
        - jnp.sum(jnp.where(lane == 1, spot_total, 0.0)) / spots
        + kl
    )
    vec_out[0:1, :] = inv_mass
    for q in range(nz):
        lanes = pl.ds(q * rows, rows)
        vec_out[1:2, lanes] = mass_grad[:, q * rows : (q + 1) * rows] - st2[x * nz + q, 0:1, :]

    for cp in p_in:
        cp.wait_recv()
    for q in range(nz):
        arrived(g.at[x * nz + q, sib_b], core_own + q)
        arrived(g.at[x * nz + q, dia_b], core_y + q)
        arrived(g.at[xo * nz + q, sib_b], core_x + q)
        arrived(g.at[xo * nz + q, dia_b, 0], core_a + q)
        arrived(g.at[xo * nz + q, dia_b, 1], core_b + q)
    for cp in started:
        cp.wait_send()
    assert taken[0] == snd.shape[0], taken
    for q in range(nz):
        shard = g.at[x * nz + q, yk]
        for s in (over_y, over_x, core_own, core_y, core_x):
            sent(shard, s + q)
        for s in (diag_x, diag_y, core_a, core_b):
            sent(shard.at[0], s + q)

        @pl.when((z >= q) & (z < nz - 1))
        def _():
            sent(shard, up + q)

        @pl.when((z <= q) & (z > 0))
        def _():
            sent(shard, down + q)


def backward_kernel(
    nz, w_ref, xl_ref, g_ref, lg_ref, vec_ref, p_ref, loss_ref, eg_hbm, lgrad_hbm, pred_ref, total_ref,
    eg, lgrad, done,
):
    x = lax.axis_index("spots")
    nx, cells, cols = w_ref.shape
    half = g_ref.shape[4]
    tiles = 4
    m = cells // tiles
    copies = []

    def out(src, dst):
        cp = pltpu.make_async_copy(src, dst, done.at[len(copies)])
        cp.start()
        copies.append(cp)

    total_ref[...] = loss_ref[:, 0:1]
    for b in range(YK):
        pred_ref[:, b * 2 * half : (b + 1) * 2 * half] = p_ref[b]
    for i in range(tiles):
        r = pl.ds(i * m, m)
        acc = jnp.zeros((m, cols), F32)
        for b in range(YK):
            for h in range(2):
                acc = acc + lax.dot_general(
                    xl_ref[b, r, h * half : (h + 1) * half],
                    g_ref[pl.ds(x * nz, nz), b, h].reshape(cols, half),
                    (((1,), (1,)), ((), ())),
                    preferred_element_type=F32,
                )
        e = jnp.exp(lg_ref[r, :].astype(F32)) * vec_ref[0:1, :]
        lgrad[r, :] = e * (acc + vec_ref[1:2, :])
        out(lgrad.at[r], lgrad_hbm.at[r])
    for b in range(YK):
        for h in range(2):
            i = b * 2 + h
            acc = jnp.zeros((cells, half), F32)
            for q in range(nx):
                acc = acc + jnp.dot(
                    w_ref[q],
                    g_ref[q * nz : (q + 1) * nz, b, h].reshape(cols, half),
                    preferred_element_type=F32,
                )
            eg[i] = acc
            out(eg.at[i], eg_hbm.at[:, pl.ds(i * half, half)])
    for cp in copies:
        cp.wait()


def step(ncells, nx, logits, expression, spatial, slide_ids, spot_counts):
    cells, cols = logits.shape
    genes = expression.shape[1]
    nz = ncells // YK
    rows = cols // nz
    wide = genes // YK
    part = rows // YK
    half = wide // 2
    copies = 105
    anywhere = pl.BlockSpec(memory_space=pl.ANY)
    whole = pl.BlockSpec(memory_space=pltpu.VMEM)
    w, xl, g, p, vec, loss = pl.pallas_call(
        functools.partial(forward_kernel, nz, nx),
        out_shape=(
            pltpu.VMEM((nx, cells, cols), BF16),
            pltpu.VMEM((YK, cells, wide), BF16),
            pltpu.VMEM((nx * nz, YK, 2, rows, half), BF16),
            pltpu.VMEM((YK, part, wide), F32),
            pltpu.VMEM((8, cols), F32),
            pltpu.VMEM((1, 128), F32),
        ),
        in_specs=[anywhere] * 5,
        out_specs=(whole,) * 6,
        scratch_shapes=[
            pltpu.VMEM((cells, cols), BF16),
            pltpu.VMEM((cells, cols), BF16),
            pltpu.VMEM((cols, cells), BF16),
            pltpu.VMEM((YK, cells, wide), F32),
            pltpu.VMEM((YK, 2, nz, rows, half), F32),
            pltpu.VMEM((2, 2, nz, rows, half), F32),
            pltpu.VMEM((2, nz, rows, half), BF16),
            pltpu.VMEM((2, nz, rows, half), BF16),
            pltpu.VMEM((2, nz, rows, half), BF16),
            pltpu.VMEM((2, nz, rows, half), BF16),
            pltpu.VMEM((YK, part, wide), F32),
            pltpu.VMEM((YK, part, wide), F32),
            pltpu.VMEM((2, cols), F32),
            pltpu.VMEM((2, cols), F32),
            pltpu.VMEM((2, cols), F32),
            pltpu.VMEM((2, cols), F32),
            pltpu.VMEM((2, cols), F32),
            pltpu.VMEM((nz, 2, cols), F32),
            pltpu.VMEM((nx, 4, cols), F32),
            pltpu.VMEM((nx * nz, 6, wide), F32),
            pltpu.VMEM((YK, 3, rows), F32),
            pltpu.VMEM((YK, 2, rows), F32),
            pltpu.VMEM((nx * nz, 2, rows), F32),
            pltpu.VMEM((1, cols), jnp.int32),
            pltpu.VMEM((1, cols), jnp.int32),
            pltpu.SemaphoreType.DMA((8,)),
            pltpu.SemaphoreType.DMA((copies,)),
            pltpu.SemaphoreType.DMA((copies,)),
        ],
        compiler_params=pltpu.CompilerParams(
            collective_id=0, has_side_effects=True, vmem_limit_bytes=40 << 20
        ),
        name="forward_and_gather",
    )(
        *(
            pltpu.with_memory_space_constraint(v, pltpu.HBM)
            for v in (logits, expression, spatial, slide_ids, spot_counts)
        )
    )

    held = [pltpu.with_memory_space_constraint(v, pltpu.VMEM) for v in (w, xl, g)]
    return pl.pallas_call(
        functools.partial(backward_kernel, nz),
        out_shape=(
            jax.ShapeDtypeStruct((cells, genes), F32),
            jax.ShapeDtypeStruct((cells, cols), F32),
            jax.ShapeDtypeStruct((part, genes), F32),
            jax.ShapeDtypeStruct((1, 1), F32),
        ),
        in_specs=[whole] * 7,
        out_specs=(anywhere, anywhere, whole, whole),
        scratch_shapes=[
            pltpu.VMEM((2 * YK, cells, half), F32),
            pltpu.VMEM((cells, cols), F32),
            pltpu.SemaphoreType.DMA((12,)),
        ],
        compiler_params=pltpu.CompilerParams(vmem_limit_bytes=40 << 20),
        name="backward",
    )(*held, logits, vec, p, loss)


def kernel_step(ncells, nx, *args):
    grad_expr, grad_logits, predicted, loss = step(ncells, nx, *args)
    return (predicted[None], loss[0, 0], grad_logits, grad_expr)


def fits(ncells, nx, logits, expression, spatial):
    cells, cols = logits.shape
    genes = expression.shape[1]
    if ncells % YK or nx != 2 or cols % (ncells // YK) or genes % (YK * 256):
        return False
    rows = cols // (ncells // YK)
    held = (cells + rows) * genes * 8 + cells * cols * 16 + cols * genes * 16
    return rows % 128 == 0 and cells % 128 == 0 and held < 50 << 20


def plain_step(logits, expression, spatial, slide_ids, spot_counts):
    highest = lax.Precision.HIGHEST
    ncells = lax.axis_size("cells")
    nspots = lax.axis_size("spots")
    columns = logits.shape[1]
    genes = expression.shape[1]
    out_rows = columns // ncells
    scores = logits.astype(F32)
    col_peak = lax.pmax(jnp.max(scores, axis=0), "cells")
    shifted = jnp.exp(scores - col_peak)
    col_total = lax.psum(jnp.sum(shifted, axis=0), "cells")
    weights = shifted / col_total
    log_mass = col_peak + jnp.log(col_total)
    weights_low = weights.astype(BF16)
    expr_low = expression.astype(BF16)
    contract_first = (((0,), (0,)), ((), ()))
    predicted = lax.psum_scatter(
        lax.dot_general(weights_low, expr_low, contract_first, preferred_element_type=F32),
        "cells",
        scatter_dimension=0,
        tiled=True,
    )
    target = spatial[0]
    member_all = (slide_ids[0][:, None] == jnp.arange(2, dtype=jnp.int32)[None, :]).astype(F32)
    first_row = lax.axis_index("cells") * out_rows
    member_rows = lax.dynamic_slice_in_dim(member_all, first_row, out_rows, 0)
    gene_inner = jnp.dot(member_rows.T, predicted * target, precision=highest)
    gene_pred = jnp.dot(member_rows.T, predicted * predicted, precision=highest)
    gene_true = jnp.dot(member_rows.T, target * target, precision=highest)
    spot_inner = jnp.sum(predicted * target, axis=1)
    pred_scale = lax.rsqrt(jnp.sum(predicted * predicted, axis=1) + EPSILON)
    true_scale = lax.rsqrt(jnp.sum(target * target, axis=1) + EPSILON)
    spot_sum = jnp.sum(spot_inner * pred_scale * true_scale)
    counts_real = spot_counts[0].astype(F32)
    exp_mass = jnp.exp(log_mass)
    local_mass = jnp.dot(member_all.T, exp_mass, precision=highest)
    local_count = jnp.dot(member_all.T, counts_real, precision=highest)
    local_clog = jnp.dot(member_all.T, counts_real * jnp.log(counts_real), precision=highest)
    local_clse = jnp.dot(member_all.T, counts_real * log_mass, precision=highest)
    slide_mass, slide_count, count_log, count_lse = lax.psum(
        (local_mass, local_count, local_clog, local_clse), "spots"
    )
    gene_inner, gene_pred, gene_true, spot_total = lax.psum(
        (gene_inner, gene_pred, gene_true, spot_sum), ("cells", "spots")
    )
    gene_a = lax.rsqrt(gene_pred + EPSILON)
    gene_b = lax.rsqrt(gene_true + EPSILON)
    gene_cos = gene_inner * gene_a * gene_b
    total_spots = columns * nspots
    some = slide_count > 0.5
    slide_count = jnp.where(some, slide_count, 1.0)
    slide_mass = jnp.where(some, slide_mass, 1.0)
    kl_value = jnp.sum(
        jnp.where(
            some,
            (count_log - count_lse) / slide_count - jnp.log(slide_count) + jnp.log(slide_mass),
            0.0,
        )
    )
    loss = -jnp.mean(gene_cos) - spot_total / total_spots + kl_value
    gene_step = -1.0 / (2 * genes)
    inner_grad = gene_step * gene_a * gene_b
    square_grad = -0.5 * gene_step * gene_inner * gene_b * gene_a * gene_a * gene_a
    pred_grad = jnp.dot(member_rows, inner_grad, precision=highest) * target
    pred_grad = pred_grad + 2.0 * jnp.dot(member_rows, square_grad, precision=highest) * predicted
    spot_step = -1.0 / total_spots
    pred_grad = pred_grad + (spot_step * pred_scale * true_scale)[:, None] * target
    pred_grad = (
        pred_grad
        - (spot_step * spot_inner * pred_scale * pred_scale * pred_scale * true_scale)[:, None]
        * predicted
    )
    grad_low = pred_grad.astype(BF16)
    mass_grad = exp_mass / jnp.dot(
        member_all, slide_mass, precision=highest
    ) - counts_real / jnp.dot(member_all, slide_count, precision=highest)
    contract_genes = (((1,), (1,)), ((), ()))
    grad_all = lax.all_gather(grad_low, "cells", axis=0, tiled=True)
    expr_part = jnp.dot(weights_low, grad_all, preferred_element_type=F32)
    weight_grad = lax.dot_general(
        expr_low, grad_all, contract_genes, preferred_element_type=F32
    )
    col_inner = lax.psum(jnp.sum(weights * weight_grad, axis=0), "cells")
    logit_grad = weights * (weight_grad - col_inner + mass_grad)
    expr_grad = lax.psum(expr_part, "spots")
    return (predicted[None], loss, logit_grad, expr_grad)


def solution(mesh):
    ncells, nx = mesh.shape["cells"], mesh.shape["spots"]

    def per_device(*args):
        if fits(ncells, nx, *args[:3]):
            return kernel_step(ncells, nx, *args)
        return plain_step(*args)

    return jax.shard_map(
        per_device,
        mesh=mesh,
        in_specs=(
            P("cells", "spots"),
            P("cells", None),
            P("spots", "cells", None),
            P("spots", None),
            P("spots", None),
        ),
        out_specs=(P("spots", "cells", None), P(), P("cells", "spots"), P("cells", None)),
        check_vma=False,
    )
```

```python
import functools

import jax
import jax.numpy as jnp
from jax import lax
from jax.experimental import pallas as pl
from jax.experimental.pallas import tpu as pltpu
from jax.sharding import PartitionSpec as P

EPSILON = 1e-06
MESH = pl.DeviceIdType.MESH
F32 = jnp.float32
BF16 = jnp.bfloat16
YK = 4


def forward_kernel(
    nz,
    nx,
    lg_hbm, ex_hbm, sp_hbm, ids_hbm, cnt_hbm,
    wv, g, eg, lgrad, xl, lgv, vec, p_out, loss_out,
    lgo, et, exv, pf, psib, ysend, yrecv, zsend, zrecv, fsend, frecv, fysend, fyrecv, tgt, prd,
    s_own, s_sib, s_pair, s_y, s_quad, s_z, aux, gtrue, strue, gsum, ssum, st1, st2, ids_ref, cnt_ref,
    loc, snd, rcv,
):
    cells, cols = lgv.shape
    rows, wide = pf.shape[2:]
    part = rows // YK
    c = lax.axis_index("cells")
    x = lax.axis_index("spots")
    z = c // YK
    yk = c % YK
    y = yk // 2
    k = yk % 2
    yo, ko, xo = 1 - y, 1 - k, (x + 1) % nx
    me = x * nz + z
    here, there = pl.ds(x * nz, nz), pl.ds(xo * nz, nz)

    def dev(zz, yy, kk, xx):
        return (zz * YK + yy * 2 + kk, xx)

    sib, yp, dia, xp = dev(z, y, ko, x), dev(z, yo, k, x), dev(z, yo, ko, x), dev(z, y, k, xo)
    yk_peers = ((sib, y * 2 + ko), (yp, yo * 2 + k), (dia, yo * 2 + ko))
    others = [(z + r) % nz for r in range(1, nz)]
    others = others[1:2] + others[:1] + others[2:]
    z_peers = [dev(q, y, k, x) for q in others]
    xz_peers = [dev(q, y, k, xo) for q in others] + z_peers + [xp]

    taken = {"send": 0, "recv": 0, "local": 0}
    sends = []

    def sems(kind, n=1):
        taken[kind] += n
        return taken[kind] - n

    def put(src, dst, device, send, recv):
        pltpu.make_async_remote_copy(
            src_ref=src, dst_ref=dst, send_sem=snd.at[send], recv_sem=rcv.at[recv],
            device_id=device, device_id_type=MESH,
        ).start()

    def landed(ref, recv):
        pltpu.make_async_remote_copy(
            src_ref=ref, dst_ref=ref, send_sem=snd.at[0], recv_sem=rcv.at[recv],
            device_id=sib, device_id_type=MESH,
        ).wait_recv()

    def left(ref, send):
        pltpu.make_async_remote_copy(
            src_ref=ref, dst_ref=ref, send_sem=snd.at[send], recv_sem=rcv.at[0],
            device_id=sib, device_id_type=MESH,
        ).wait_send()

    def remote(src, dst, device):
        i, j = sems("send"), sems("recv")
        put(src, dst, device, i, j)
        sends.append((src, i))
        return lambda: landed(dst, j)

    def spread_to(pairs, size):
        i, j = sems("send"), sems("recv")
        for src, dst, device in pairs:
            put(src, dst, device, i, j)
        sends.append((size(len(pairs)), i))
        return lambda: landed(size(len(pairs)), j)

    def local(src, dst):
        cp = pltpu.make_async_copy(src, dst, loc.at[sems("local")])
        cp.start()
        return cp

    barrier = pltpu.get_barrier_semaphore()
    for d in [p[0] for p in yk_peers] + xz_peers:
        pl.semaphore_signal(barrier, inc=1, device_id=d, device_id_type=MESH)

    def genes_of(ref, b):
        return ref.at[..., pl.ds(pl.multiple_of(b * wide, wide), wide)]

    blocks = (yo * 2 + ko, yo * 2 + k, y * 2 + ko, yk)
    lg_copy = local(lg_hbm, lgv)
    ex_copies = [local(genes_of(ex_hbm, b), exv.at[i]) for i, b in enumerate(blocks)]
    late = [
        local(genes_of(sp_hbm.at[0], yk), tgt.at[yk]),
        local(ids_hbm, ids_ref),
        local(cnt_hbm, cnt_ref),
    ]

    lg_copy.wait()
    piece = 128
    total = jnp.zeros((1, cols), F32)
    total_low = jnp.zeros((1, cols), F32)
    for i in range(cells // piece):
        e = jnp.exp(lgv[pl.ds(i * piece, piece), :].astype(F32))
        low = e.astype(BF16).astype(F32)
        total = total + jnp.sum(e, axis=0, keepdims=True)
        total_low = total_low + jnp.sum(low, axis=0, keepdims=True)
        et[:, pl.ds(i * piece, piece)] = low.T.astype(BF16)
    s_own[0:1, :] = total
    s_own[1:2, :] = total_low

    half = wide // 2
    for i, b in enumerate(blocks):
        ex_copies[i].wait()
        for n in range(2):
            lanes = pl.ds(n * half, half)
            low = exv[i, :, lanes].astype(BF16)
            xl[b, :, lanes] = low
            pf[i, :, :, lanes] = jnp.dot(et[...], low, preferred_element_type=F32).reshape(
                nz, rows, half
            )

    first = rows // 8
    middle = rows // 2
    r0, r1, r2 = pl.ds(0, first), pl.ds(first, middle - first), pl.ds(middle, rows - middle)
    rest = pl.ds(first, rows - first)

    def dest(r):
        return pl.ds(r.start - first, r.size)

    pl.semaphore_wait(barrier, len(yk_peers) + len(xz_peers))
    s_sib_in = remote(s_own, s_sib, sib)
    f_sib_in = spread_to(
        [(pf.at[2 * i, :, r0], psib.at[i, :, r0], sib) for i in range(2)], lambda n: psib.at[:, :, r0]
    )
    t_in = spread_to(
        [(genes_of(sp_hbm.at[0], b), tgt.at[yk], d) for d, b in yk_peers],
        lambda n: tgt.at[pl.ds(0, n)],
    )
    sib_r1 = [remote(pf.at[0, q, r1], psib.at[0, q, r1], sib) for q in others + [z]]
    sib_r2 = remote(pf.at[0, :, r2], psib.at[0, :, r2], sib)
    sib_rest = remote(pf.at[2, :, rest], psib.at[1, :, rest], sib)
    most = cells * 7 // 8
    early, last = pl.ds(0, most), pl.ds(most, cells - most)
    lg_in = [remote(lg_hbm.at[early], lgo.at[early], xp)]

    s_sib_in()
    s_pair[...] = s_own[...] + s_sib[...]
    s_y_in = remote(s_pair, s_y, yp)
    f_sib_in()
    for q in others:
        for i in range(2):
            fsend[q, i] = (pf[1 + 2 * i, q, r0] + psib[i, q, r0]).astype(BF16)
    f_in = spread_to(
        [(fsend.at[q], frecv.at[z], d) for q, d in zip(others, z_peers, strict=True)],
        lambda n: frecv.at[pl.ds(0, n)],
    )

    y_send = sems("send")
    y_in = {}

    def send_y(i, r, q):
        ysend[q, dest(r)] = (pf[1, q, r] + psib[0, q, r]).astype(BF16)
        y_in[r.start, i] = sems("recv")
        put(ysend.at[q, dest(r)], yrecv.at[q, dest(r)], yp, y_send, y_in[r.start, i])

    for i, q in enumerate(others):
        sib_r1[i]()
        send_y(i, r1, q)
    sib_r2()
    for i, q in enumerate(others):
        send_y(i, r2, q)
    sib_r1[nz - 1]()
    send_y(nz - 1, r1, z)
    send_y(nz - 1, r2, z)
    sends.append((ysend, y_send))

    s_y_in()
    s_quad[...] = s_pair[...] + s_y[...]
    s_z[z] = s_quad[...]
    s_z_in = spread_to(
        [(s_quad, s_z.at[z], d) for d in z_peers], lambda n: s_z.at[pl.ds(0, n)]
    )

    for cp in late:
        cp.wait()
    t_in()
    eye = lax.broadcasted_iota(jnp.int32, (rows, rows), 0) == lax.broadcasted_iota(
        jnp.int32, (rows, rows), 1
    )

    def to_col(v):
        return jnp.sum(jnp.where(eye, jnp.broadcast_to(v, (rows, rows)), 0.0), axis=1, keepdims=True)

    def to_row(v):
        return jnp.sum(jnp.where(eye, jnp.broadcast_to(v, (rows, rows)), 0.0), axis=0, keepdims=True)

    mine_cols = pl.ds(pl.multiple_of(z * rows, rows), rows)
    slide = to_col(ids_ref[:, mine_cols].astype(F32))
    second = jnp.broadcast_to(slide > 0.5, (rows, wide))

    def by_slide(v):
        a = jnp.sum(jnp.where(second, 0.0, v), axis=0, keepdims=True)
        b = jnp.sum(jnp.where(second, v, 0.0), axis=0, keepdims=True)
        return a, b

    target = tgt[...].reshape(rows, wide)
    square = target * target
    for s, v in enumerate(by_slide(square)):
        gtrue[me, s : s + 1, :] = v
    strue[yk] = to_row(jnp.sum(square, axis=1, keepdims=True))

    def share(by_gene, by_spot):
        a = spread_to([(by_gene.at[me], by_gene.at[me], d) for d in xz_peers], lambda n: by_gene.at[pl.ds(0, n)])
        b = spread_to([(by_spot.at[yk], by_spot.at[yk], d) for d, _ in yk_peers], lambda n: by_spot.at[pl.ds(0, n)])
        return a, b

    true_in = share(gtrue, strue)

    z_send, z_recv = sems("send"), sems("recv")

    def add_y(i, r, q):
        landed(yrecv.at[q, dest(r)], y_in[r.start, i])
        return pf[3, q, r] + psib[1, q, r] + yrecv[q, dest(r)].astype(F32)

    sib_rest()
    for j, r in enumerate((r1, r2)):
        for i, q in enumerate(others):
            zsend[q, dest(r)] = add_y(i, r, q).astype(BF16)
            put(zsend.at[q, dest(r)], zrecv.at[z, dest(r)], z_peers[i], z_send, z_recv)
        if j == 0:
            f_in()
            sums = [pf[1 + 2 * i, z, r0] + psib[i, z, r0] for i in range(2)]
            for q in others:
                for i in range(2):
                    sums[i] = sums[i] + frecv[q, i].astype(F32)
            fysend[...] = sums[0].astype(BF16)
            fy_in = remote(fysend, fyrecv, yp)
    sends.append((zsend.at[pl.ds(0, nz - 1)], z_send))
    own_1 = add_y(nz - 1, r1, z)
    own_2 = add_y(nz - 1, r2, z)

    s_z_in()
    whole_sum = s_z[0]
    for q in range(1, nz):
        whole_sum = whole_sum + s_z[q]
    mass = whole_sum[0:1, :]
    inv_mass = 1.0 / mass
    slides = ids_ref[...].astype(F32)
    counts = cnt_ref[...].astype(F32)
    aux[x, 0:1, :] = mass
    aux[x, 1:2, :] = slides
    aux[x, 2:3, :] = counts
    aux[x, 3:4, :] = jnp.zeros((1, cols), F32)
    aux_in = remote(aux.at[x], aux.at[x], xp)
    low_sum = s_z[0, 1:2, mine_cols]
    for q in range(1, nz):
        low_sum = low_sum + s_z[q, 1:2, mine_cols]
    inv_low = 1.0 / to_col(low_sum)

    fy_in()
    own_0 = sums[1] + fyrecv[...].astype(F32)
    landed(zrecv.at[pl.ds(0, nz - 1)], z_recv)
    own_rest = jnp.concatenate([own_1, own_2], axis=0)
    for q in others:
        own_rest = own_rest + zrecv[q].astype(F32)
    pred = jnp.concatenate([own_0, own_rest], axis=0) * inv_low
    both = pred * target
    pair = pred * pred
    for r, v in enumerate((both, pair)):
        for s, w in enumerate(by_slide(v)):
            gsum[me, 2 * r + s : 2 * r + s + 1, :] = w
        ssum[yk, r : r + 1, :] = to_row(jnp.sum(v, axis=1, keepdims=True))
    sum_in = share(gsum, ssum)
    lg_in.append(remote(lg_hbm.at[last], lgo.at[last], xp))
    prd[...] = pred.reshape(YK, part, wide)
    p_in = spread_to([(prd.at[b], p_out.at[yk], d) for d, b in yk_peers], lambda n: p_out.at[pl.ds(0, n)])
    p_out[yk] = prd[yk]

    def weights(src, scale, to):
        for i in range(cells // piece):
            r = pl.ds(i * piece, piece)
            wv[to, r, :] = (jnp.exp(src[r, :].astype(F32)) * scale).astype(BF16)

    weights(lgv, inv_mass, x)
    for wait in true_in + sum_in:
        wait()

    def added(ref, n):
        v = ref[0]
        for q in range(1, n):
            v = v + ref[q]
        return v

    genes = YK * wide
    spots = nx * cols
    gene_step = -1.0 / (2 * genes)
    spot_step = -1.0 / spots
    gs = added(gsum, nx * nz)
    gene_a = lax.rsqrt(gs[2:4] + EPSILON)
    gene_b = lax.rsqrt(added(gtrue, nx * nz) + EPSILON)
    gene_cos = gs[0:2] * gene_a * gene_b
    t_gene = gene_step * gene_a * gene_b
    p_gene = -gene_step * gs[0:2] * gene_b * gene_a * gene_a * gene_a
    ss = added(ssum, YK)
    pred_scale = lax.rsqrt(ss[1:2] + EPSILON)
    true_scale = lax.rsqrt(added(strue, YK) + EPSILON)
    spot_cos = ss[0:1] * pred_scale * true_scale
    t_spot = to_col(spot_step * pred_scale * true_scale)
    p_spot = to_col(-spot_step * ss[0:1] * pred_scale * pred_scale * pred_scale * true_scale)

    def of_slide(v):
        return jnp.where(
            second, jnp.broadcast_to(v[1:2], (rows, wide)), jnp.broadcast_to(v[0:1], (rows, wide))
        )

    grad = (of_slide(t_gene) + t_spot) * target + (of_slide(p_gene) + p_spot) * pred
    low = grad.astype(BF16)
    g[me, y, k] = low

    cut = rows * 3 // 8
    part_a, part_b, part_c = pl.ds(0, cut), pl.ds(cut, cut), pl.ds(2 * cut, rows - 2 * cut)
    part_ab, four_c = pl.ds(0, 2 * cut), pl.ds(0, 4 * (rows - 2 * cut))
    up, down, c_up, c_down = (sems("send", nz) for _ in range(4))
    y_out, x_out, cy_out, cx_out, cd_out, a_out, b_out, core_out = (sems("send") for _ in range(8))
    from_z, from_y, from_x = (sems("recv", 2 * nz) for _ in range(3))
    from_a, from_b = (sems("recv", nz) for _ in range(2))
    cy_in, cx_in, cd_in = (sems("recv") for _ in range(3))
    from_c, core_in = sems("recv", 4 * nz), sems("recv", 4)
    kinds = ((x, y, 0), (xo, y, 2), (x, yo, 1), (xo, yo, 3))

    def to_core(shard, region):
        put(shard, shard, sib, core_out, core_in + region)

    def pass_on(shard, upward, send, recv):
        @pl.when(z < nz - 1 if upward else z > 0)
        def _():
            put(shard, shard, dev(z + 1 if upward else z - 1, y, k, x), send, recv)

    def own_z():
        for h, r in enumerate((part_a, part_b)):
            shard = g.at[me, y, k, r]
            pass_on(shard, True, up + z, from_z + 2 * z + h)
            pass_on(shard, False, down + z, from_z + 2 * z + h)

    def own_c():
        shard = g.at[me, y, k, part_c]
        put(shard, shard, yp, cy_out, cy_in)
        put(shard, shard, xp, cx_out, cx_in)

    def own_y():
        for h, r in enumerate((part_a, part_b)):
            shard = g.at[me, y, k, r]
            put(shard, shard, yp, y_out, from_y + 2 * z + h)

    def own_x():
        for h, r in ((1, part_b), (0, part_a)):
            shard = g.at[me, y, k, r]
            put(shard, shard, xp, x_out, from_x + 2 * z + h)

    def own_core():
        to_core(g.at[me, y, k], 0)

    def start_c(kind):
        plane, yy, _ = kinds[kind]
        shard = g.at[plane * nz + z, yy, k, part_c]
        pass_on(shard, True, c_up + z, from_c + 4 * z + kind)
        pass_on(shard, False, c_down + z, from_c + 4 * z + kind)

    def wait_cy():
        shard = g.at[me, yo, k, part_c]
        landed(shard, cy_in)
        put(shard, shard, xp, cd_out, cd_in)
        to_core(shard, 1)

    def wait_cx():
        shard = g.at[xo * nz + z, y, k, part_c]
        landed(shard, cx_in)
        to_core(shard, 2)

    def wait_cd():
        shard = g.at[xo * nz + z, yo, k, part_c]
        landed(shard, cd_in)
        to_core(shard, 3)

    def at_distance(d, act):
        if d == 0:
            act(z, False)
            return

        @pl.when(z >= d)
        def _():
            act(z - d, False)

        @pl.when(z < nz - d)
        def _():
            act(z + d, True)

    def take_z(q, above):
        for h, r in enumerate((part_a, part_b)):
            shard = g.at[x * nz + q, y, k, r]
            landed(shard, from_z + 2 * q + h)
            pass_on(shard, not above, (down if above else up) + q, from_z + 2 * q + h)
            put(shard, shard, yp, y_out, from_y + 2 * q + h)
            put(shard, shard, xp, x_out, from_x + 2 * q + h)
            to_core(shard, 0)

    def take_c(kind):
        def act(q, above):
            plane, yy, region = kinds[kind]
            shard = g.at[plane * nz + q, yy, k, part_c]
            landed(shard, from_c + 4 * q + kind)
            pass_on(shard, not above, (c_down if above else c_up) + q, from_c + 4 * q + kind)
            to_core(shard, region)

        return act

    def take_y(q, above):
        for h, r in enumerate((part_a, part_b)):
            shard = g.at[x * nz + q, yo, k, r]
            landed(shard, from_y + 2 * q + h)
            if h == 0:
                put(shard, shard, xp, a_out, from_a + q)
            to_core(shard, 1)

    def take_x(q, above):
        for h, r in ((1, part_b), (0, part_a)):
            shard = g.at[xo * nz + q, y, k, r]
            landed(shard, from_x + 2 * q + h)
            if h == 1:
                put(shard, shard, yp, b_out, from_b + q)
            to_core(shard, 2)

    def take_d(q, above):
        for recv, r in ((from_a, part_a), (from_b, part_b)):
            shard = g.at[xo * nz + q, yo, k, r]
            landed(shard, recv + q)
            to_core(shard, 3)

    def grad_of(plane, yy, kk):
        return g[plane, yy, kk].reshape(cols, wide)

    def unit(yy, kk, start=False):
        term = lax.dot_general(
            xl[yy * 2 + kk], grad_of(here, yy, kk), (((1,), (1,)), ((), ())), preferred_element_type=F32
        )
        lgrad[...] = term if start else lgrad[...] + term
        eg[yy, kk] = jnp.dot(wv[x], grad_of(here, yy, kk), preferred_element_type=F32)

    lane = lax.broadcasted_iota(jnp.int32, (1, rows), 1)

    own_z()
    own_c()
    own_x()
    start_c(0)
    own_y()
    st1[yk, 0:1, :] = to_row(jnp.sum(low.astype(F32) * pred, axis=1, keepdims=True))
    st1[yk, 1:2, :] = jnp.where(lane == 0, jnp.sum(gene_cos), 0.0)
    st1_in = spread_to([(st1.at[yk], st1.at[yk], d) for d, _ in yk_peers], lambda n: st1.at[pl.ds(0, n)])
    aux_in()
    for wait in lg_in:
        wait()
    weights(lgo, 1.0 / aux[xo, 0:1, :], xo)
    wait_cx()
    start_c(1)
    wait_cy()
    start_c(2)
    at_distance(1, take_z)
    at_distance(1, take_c(0))
    at_distance(2, take_z)
    own_core()
    wait_cd()
    start_c(3)
    at_distance(2, take_c(0))
    take_x(z, False)
    take_y(z, False)
    at_distance(3, take_z)
    at_distance(1, take_c(2))
    at_distance(1, take_c(1))
    at_distance(1, take_y)
    at_distance(1, take_x)
    at_distance(1, take_c(3))
    at_distance(3, take_c(0))
    at_distance(2, take_x)
    at_distance(2, take_y)
    st1_in()
    whole = added(st1, YK)
    st2[me, 0:1, :] = whole[0:1]
    st2[me, 1:2, :] = jnp.where(lane == 0, whole[1:2], jnp.where(lane == 1, jnp.sum(spot_cos), 0.0))
    st2_in = spread_to([(st2.at[me], st2.at[me], d) for d in xz_peers], lambda n: st2.at[pl.ds(0, n)])
    unit(y, k, True)
    at_distance(2, take_c(2))
    at_distance(2, take_c(1))
    at_distance(3, take_y)
    at_distance(3, take_x)
    landed(g.at[here, y, ko], core_in)
    unit(y, ko)
    at_distance(2, take_c(3))
    at_distance(3, take_c(2))
    unit(yo, k)
    take_d(z, False)
    at_distance(2, take_d)
    at_distance(3, take_c(1))
    at_distance(1, take_d)
    at_distance(3, take_c(3))
    at_distance(3, take_d)

    kl = 0.0
    slide_mass, slide_count = [], []
    for s in range(2):
        m = n = cl = cm = 0.0
        for q in range(nx):
            of_s = jnp.abs(aux[q, 1:2, :] - s) < 0.5
            n_q = jnp.where(of_s, aux[q, 2:3, :], 0.0)
            m = m + jnp.sum(jnp.where(of_s, aux[q, 0:1, :], 0.0))
            n = n + jnp.sum(n_q)
            cl = cl + jnp.sum(n_q * jnp.log(aux[q, 2:3, :]))
            cm = cm + jnp.sum(n_q * jnp.log(aux[q, 0:1, :]))
        some = n > 0.5
        m = jnp.full((1, 128), jnp.where(some, m, 1.0), F32)
        n = jnp.full((1, 128), jnp.where(some, n, 1.0), F32)
        kl = kl + jnp.where(some, (cl - cm) / n - jnp.log(n) + jnp.log(m), 0.0)
        slide_mass.append(m[:, 0:1])
        slide_count.append(n[:, 0:1])
    is_second = slides > 0.5
    mass_grad = mass / jnp.where(is_second, slide_mass[1], slide_mass[0]) - counts / jnp.where(
        is_second, slide_count[1], slide_count[0]
    )
    st2_in()
    gene_total = whole[1:2]
    spot_total = added(st2, nx * nz)[1:2]
    loss_out[...] = (
        -jnp.sum(jnp.where(lane == 0, gene_total, 0.0)) / (2 * genes)
        - jnp.sum(jnp.where(lane == 1, spot_total, 0.0)) / spots
        + kl
    )
    vec[0:1, :] = inv_mass
    vec[1:2, :] = mass_grad - jnp.concatenate([st2[x * nz + q, 0:1, :] for q in range(nz)], axis=1)

    p_in()
    landed(g.at[here, yo, ko], core_in + 1)
    landed(g.at[there, y, ko], core_in + 2)
    landed(g.at[there, yo, ko], core_in + 3)
    for ref, i in sends:
        left(ref, i)
    left(g.at[here, y, k, part_ab], y_out)
    left(g.at[here, y, k, part_ab], x_out)
    for i in (cy_out, cx_out, cd_out):
        left(g.at[me, y, k, part_c], i)
    left(g.at[here, yo, k, part_a], a_out)
    left(g.at[there, y, k, part_b], b_out)
    left(g.at[:, :, k], core_out)
    for q in range(nz):
        for some, ab_sem, c_sem in (
            ((z >= q) & (z < nz - 1), up, c_up),
            ((z <= q) & (z > 0), down, c_down),
        ):

            @pl.when(some)
            def _():
                left(g.at[x * nz + q, y, k, part_ab], ab_sem + q)
                left(g.at[x * nz + q, y, k, four_c], c_sem + q)

    assert (taken["send"], taken["recv"]) == (snd.shape[0], rcv.shape[0]), taken


def backward_kernel(
    nz, w_ref, g_ref, part_ref, lgrad_ref, xl_ref, lg_ref, vec_ref, p_ref, loss_ref,
    eg_hbm, lgrad_hbm, pred_ref, total_ref, eg, lgrad, done,
):
    c = lax.axis_index("cells")
    x = lax.axis_index("spots")
    y, k = (c % YK) // 2, c % 2
    nx, cells, cols = w_ref.shape
    wide = g_ref.shape[4]
    half = wide // 2
    xo = (x + 1) % nx
    copies = []

    def out(src, dst):
        cp = pltpu.make_async_copy(src, dst, done.at[len(copies)])
        cp.start()
        copies.append(cp)

    def term(q, yy, kk, lanes):
        block = g_ref[pl.ds(q * nz, nz), yy, kk, :, lanes].reshape(cols, half)
        return jnp.dot(w_ref[q], block, preferred_element_type=F32)

    for i, (yy, kk) in enumerate(((y, k), (y, 1 - k), (1 - y, k), (1 - y, 1 - k))):
        for h in range(2):
            lanes = pl.ds(h * half, half)
            mine = part_ref[yy, kk, :, lanes] if i < 3 else term(x, yy, kk, lanes)
            eg[2 * i + h] = mine + term(xo, yy, kk, lanes)
            at = (yy * 2 + kk) * wide + h * half
            out(eg.at[2 * i + h], eg_hbm.at[:, pl.ds(pl.multiple_of(at, half), half)])
    last = g_ref[pl.ds(x * nz, nz), 1 - y, 1 - k].reshape(cols, wide)
    tiles = 4
    m = cells // tiles
    for i in range(tiles):
        r = pl.ds(i * m, m)
        acc = lgrad_ref[r, :] + lax.dot_general(
            xl_ref[(1 - y) * 2 + 1 - k, r, :], last, (((1,), (1,)), ((), ())), preferred_element_type=F32
        )
        e = jnp.exp(lg_ref[r, :].astype(F32)) * vec_ref[0:1, :]
        lgrad[r, :] = e * (acc + vec_ref[1:2, :])
        out(lgrad.at[r], lgrad_hbm.at[r])
    total_ref[...] = loss_ref[:, 0:1]
    for b in range(YK):
        pred_ref[:, b * wide : (b + 1) * wide] = p_ref[b]
    for cp in copies:
        cp.wait()


def step(ncells, nx, logits, expression, spatial, slide_ids, spot_counts):
    cells, cols = logits.shape
    genes = expression.shape[1]
    nz = ncells // YK
    rows = cols // nz
    wide = genes // YK
    part = rows // YK
    half = wide // 2
    first = rows // 8
    anywhere = pl.BlockSpec(memory_space=pl.ANY)
    whole = pl.BlockSpec(memory_space=pltpu.VMEM)
    *held, p, loss = pl.pallas_call(
        functools.partial(forward_kernel, nz, nx),
        out_shape=(
            pltpu.VMEM((nx, cells, cols), BF16),
            pltpu.VMEM((nx * nz, 2, 2, rows, wide), BF16),
            pltpu.VMEM((2, 2, cells, wide), F32),
            pltpu.VMEM((cells, cols), F32),
            pltpu.VMEM((YK, cells, wide), BF16),
            pltpu.VMEM((cells, cols), BF16),
            pltpu.VMEM((2, cols), F32),
            pltpu.VMEM((YK, part, wide), F32),
            pltpu.VMEM((1, 128), F32),
        ),
        in_specs=[anywhere] * 5,
        out_specs=(whole,) * 9,
        scratch_shapes=[
            pltpu.VMEM((cells, cols), BF16),
            pltpu.VMEM((cols, cells), BF16),
            pltpu.VMEM((YK, cells, wide), F32),
            pltpu.VMEM((YK, nz, rows, wide), F32),
            pltpu.VMEM((2, nz, rows, wide), F32),
            pltpu.VMEM((nz, rows - first, wide), BF16),
            pltpu.VMEM((nz, rows - first, wide), BF16),
            pltpu.VMEM((nz, rows - first, wide), BF16),
            pltpu.VMEM((nz, rows - first, wide), BF16),
            pltpu.VMEM((nz, 2, first, wide), BF16),
            pltpu.VMEM((nz, 2, first, wide), BF16),
            pltpu.VMEM((first, wide), BF16),
            pltpu.VMEM((first, wide), BF16),
            pltpu.VMEM((YK, part, wide), F32),
            pltpu.VMEM((YK, part, wide), F32),
            pltpu.VMEM((2, cols), F32),
            pltpu.VMEM((2, cols), F32),
            pltpu.VMEM((2, cols), F32),
            pltpu.VMEM((2, cols), F32),
            pltpu.VMEM((2, cols), F32),
            pltpu.VMEM((nz, 2, cols), F32),
            pltpu.VMEM((nx, 4, cols), F32),
            pltpu.VMEM((nx * nz, 2, wide), F32),
            pltpu.VMEM((YK, 1, rows), F32),
            pltpu.VMEM((nx * nz, 4, wide), F32),
            pltpu.VMEM((YK, 2, rows), F32),
            pltpu.VMEM((YK, 2, rows), F32),
            pltpu.VMEM((nx * nz, 2, rows), F32),
            pltpu.VMEM((1, cols), jnp.int32),
            pltpu.VMEM((1, cols), jnp.int32),
            pltpu.SemaphoreType.DMA((8,)),
            pltpu.SemaphoreType.DMA((29 + 5 * nz,)),
            pltpu.SemaphoreType.DMA((27 + 15 * nz,)),
        ],
        compiler_params=pltpu.CompilerParams(
            collective_id=0, has_side_effects=True, vmem_limit_bytes=24 << 20
        ),
        name="forward_and_gather",
    )(
        *(
            pltpu.with_memory_space_constraint(v, pltpu.HBM)
            for v in (logits, expression, spatial, slide_ids, spot_counts)
        )
    )

    held = [pltpu.with_memory_space_constraint(v, pltpu.VMEM) for v in held]
    return pl.pallas_call(
        functools.partial(backward_kernel, nz),
        out_shape=(
            jax.ShapeDtypeStruct((cells, genes), F32),
            jax.ShapeDtypeStruct((cells, cols), F32),
            jax.ShapeDtypeStruct((part, genes), F32),
            jax.ShapeDtypeStruct((1, 1), F32),
        ),
        in_specs=[whole] * 9,
        out_specs=(anywhere, anywhere, whole, whole),
        scratch_shapes=[
            pltpu.VMEM((2 * YK, cells, half), F32),
            pltpu.VMEM((cells, cols), F32),
            pltpu.SemaphoreType.DMA((12,)),
        ],
        compiler_params=pltpu.CompilerParams(vmem_limit_bytes=24 << 20),
        name="backward",
    )(*held, p, loss)


def kernel_step(ncells, nx, *args):
    grad_expr, grad_logits, predicted, loss = step(ncells, nx, *args)
    return (predicted[None], loss[0, 0], grad_logits, grad_expr)


def fits(ncells, nx, logits, expression, spatial):
    cells, cols = logits.shape
    genes = expression.shape[1]
    if ncells != 4 * YK or nx != 2 or cols % (ncells // YK) or genes % (YK * 256):
        return False
    rows = cols // (ncells // YK)
    held = (cells + rows) * genes * 8 + cells * cols * 16 + cols * genes * 16
    return rows % 128 == 0 and cells % 128 == 0 and held < 50 << 20


def plain_step(logits, expression, spatial, slide_ids, spot_counts):
    highest = lax.Precision.HIGHEST
    ncells = lax.axis_size("cells")
    nspots = lax.axis_size("spots")
    columns = logits.shape[1]
    genes = expression.shape[1]
    out_rows = columns // ncells
    scores = logits.astype(F32)
    col_peak = lax.pmax(jnp.max(scores, axis=0), "cells")
    shifted = jnp.exp(scores - col_peak)
    col_total = lax.psum(jnp.sum(shifted, axis=0), "cells")
    weights = shifted / col_total
    log_mass = col_peak + jnp.log(col_total)
    weights_low = weights.astype(BF16)
    expr_low = expression.astype(BF16)
    contract_first = (((0,), (0,)), ((), ()))
    predicted = lax.psum_scatter(
        lax.dot_general(weights_low, expr_low, contract_first, preferred_element_type=F32),
        "cells",
        scatter_dimension=0,
        tiled=True,
    )
    target = spatial[0]
    member_all = (slide_ids[0][:, None] == jnp.arange(2, dtype=jnp.int32)[None, :]).astype(F32)
    first_row = lax.axis_index("cells") * out_rows
    member_rows = lax.dynamic_slice_in_dim(member_all, first_row, out_rows, 0)
    gene_inner = jnp.dot(member_rows.T, predicted * target, precision=highest)
    gene_pred = jnp.dot(member_rows.T, predicted * predicted, precision=highest)
    gene_true = jnp.dot(member_rows.T, target * target, precision=highest)
    spot_inner = jnp.sum(predicted * target, axis=1)
    pred_scale = lax.rsqrt(jnp.sum(predicted * predicted, axis=1) + EPSILON)
    true_scale = lax.rsqrt(jnp.sum(target * target, axis=1) + EPSILON)
    spot_sum = jnp.sum(spot_inner * pred_scale * true_scale)
    counts_real = spot_counts[0].astype(F32)
    exp_mass = jnp.exp(log_mass)
    local_mass = jnp.dot(member_all.T, exp_mass, precision=highest)
    local_count = jnp.dot(member_all.T, counts_real, precision=highest)
    local_clog = jnp.dot(member_all.T, counts_real * jnp.log(counts_real), precision=highest)
    local_clse = jnp.dot(member_all.T, counts_real * log_mass, precision=highest)
    slide_mass, slide_count, count_log, count_lse = lax.psum(
        (local_mass, local_count, local_clog, local_clse), "spots"
    )
    gene_inner, gene_pred, gene_true, spot_total = lax.psum(
        (gene_inner, gene_pred, gene_true, spot_sum), ("cells", "spots")
    )
    gene_a = lax.rsqrt(gene_pred + EPSILON)
    gene_b = lax.rsqrt(gene_true + EPSILON)
    gene_cos = gene_inner * gene_a * gene_b
    total_spots = columns * nspots
    some = slide_count > 0.5
    slide_count = jnp.where(some, slide_count, 1.0)
    slide_mass = jnp.where(some, slide_mass, 1.0)
    kl_value = jnp.sum(
        jnp.where(
            some,
            (count_log - count_lse) / slide_count - jnp.log(slide_count) + jnp.log(slide_mass),
            0.0,
        )
    )
    loss = -jnp.mean(gene_cos) - spot_total / total_spots + kl_value
    gene_step = -1.0 / (2 * genes)
    inner_grad = gene_step * gene_a * gene_b
    square_grad = -0.5 * gene_step * gene_inner * gene_b * gene_a * gene_a * gene_a
    pred_grad = jnp.dot(member_rows, inner_grad, precision=highest) * target
    pred_grad = pred_grad + 2.0 * jnp.dot(member_rows, square_grad, precision=highest) * predicted
    spot_step = -1.0 / total_spots
    pred_grad = pred_grad + (spot_step * pred_scale * true_scale)[:, None] * target
    pred_grad = (
        pred_grad
        - (spot_step * spot_inner * pred_scale * pred_scale * pred_scale * true_scale)[:, None]
        * predicted
    )
    grad_low = pred_grad.astype(BF16)
    mass_grad = exp_mass / jnp.dot(
        member_all, slide_mass, precision=highest
    ) - counts_real / jnp.dot(member_all, slide_count, precision=highest)
    contract_genes = (((1,), (1,)), ((), ()))
    grad_all = lax.all_gather(grad_low, "cells", axis=0, tiled=True)
    expr_part = jnp.dot(weights_low, grad_all, preferred_element_type=F32)
    weight_grad = lax.dot_general(
        expr_low, grad_all, contract_genes, preferred_element_type=F32
    )
    col_inner = lax.psum(jnp.sum(weights * weight_grad, axis=0), "cells")
    logit_grad = weights * (weight_grad - col_inner + mass_grad)
    expr_grad = lax.psum(expr_part, "spots")
    return (predicted[None], loss, logit_grad, expr_grad)


def solution(mesh):
    ncells, nx = mesh.shape["cells"], mesh.shape["spots"]

    def per_device(*args):
        if fits(ncells, nx, *args[:3]):
            return kernel_step(ncells, nx, *args)
        return plain_step(*args)

    return jax.shard_map(
        per_device,
        mesh=mesh,
        in_specs=(
            P("cells", "spots"),
            P("cells", None),
            P("spots", "cells", None),
            P("spots", None),
            P("spots", None),
        ),
        out_specs=(P("spots", "cells", None), P(), P("cells", "spots"), P("cells", None)),
        check_vma=False,
    )
```

```python
import functools

import jax
import jax.numpy as jnp
from jax import lax
from jax.experimental import pallas as pl
from jax.experimental.pallas import tpu as pltpu
from jax.sharding import PartitionSpec as P

EPSILON = 1e-06
MESH = pl.DeviceIdType.MESH
F32 = jnp.float32
BF16 = jnp.bfloat16
YK = 4


def forward_kernel(
    nz,
    nx,
    lg_hbm, ex_hbm, sp_hbm, ids_hbm, cnt_hbm,
    wv, g, eg, lgrad, lgv, vec, p_out, loss_out,
    lgo, et, exv, xl, pf, psib, ysend, yrecv, zsend, zrecv, tgt, prd,
    s_own, s_sib, s_pair, s_y, s_quad, s_z, aux, gtrue, strue, gsum, ssum, st1, st2, ids_ref, cnt_ref,
    loc, snd, rcv,
):
    cells, cols = lgv.shape
    rows, wide = pf.shape[2:]
    part = rows // YK
    c = lax.axis_index("cells")
    x = lax.axis_index("spots")
    z = c // YK
    yk = c % YK
    y = yk // 2
    k = yk % 2
    yo, ko, xo = 1 - y, 1 - k, (x + 1) % nx
    me = x * nz + z
    here, there = pl.ds(x * nz, nz), pl.ds(xo * nz, nz)

    def dev(zz, yy, kk, xx):
        return (zz * YK + yy * 2 + kk, xx)

    sib, yp, dia, xp = dev(z, y, ko, x), dev(z, yo, k, x), dev(z, yo, ko, x), dev(z, y, k, xo)
    yk_peers = ((sib, y * 2 + ko), (yp, yo * 2 + k), (dia, yo * 2 + ko))
    others = [(z + r) % nz for r in range(1, nz)]
    others = others[1:2] + others[:1] + others[2:]
    z_peers = [dev(q, y, k, x) for q in others]
    xz_peers = [dev(q, y, k, xo) for q in others] + z_peers + [xp]

    taken = {"send": 0, "recv": 0, "local": 0}
    kept = {"send": 0, "recv": 0}
    size = {"send": snd.shape[0], "recv": rcv.shape[0]}
    sends, late_sends = [], []

    def sems(kind, n=1):
        taken[kind] += n
        return taken[kind] - n

    def keep(kind):
        kept[kind] += 1
        return size[kind] - kept[kind]

    def put(src, dst, device, send, recv):
        pltpu.make_async_remote_copy(
            src_ref=src, dst_ref=dst, send_sem=snd.at[send], recv_sem=rcv.at[recv],
            device_id=device, device_id_type=MESH,
        ).start()

    def landed(ref, recv):
        pltpu.make_async_remote_copy(
            src_ref=ref, dst_ref=ref, send_sem=snd.at[0], recv_sem=rcv.at[recv],
            device_id=sib, device_id_type=MESH,
        ).wait_recv()

    def left(ref, send):
        pltpu.make_async_remote_copy(
            src_ref=ref, dst_ref=ref, send_sem=snd.at[send], recv_sem=rcv.at[0],
            device_id=sib, device_id_type=MESH,
        ).wait_send()

    def remote(src, dst, device, late=False):
        return spread_to([(src, dst, device)], lambda n: dst, late)

    def spread_to(pairs, size, late=False):
        take = keep if late else sems
        i, j = take("send"), take("recv")
        for src, dst, device in pairs:
            put(src, dst, device, i, j)
        (late_sends if late else sends).append((size(len(pairs)), i))
        return lambda: landed(size(len(pairs)), j)

    def local(src, dst):
        cp = pltpu.make_async_copy(src, dst, loc.at[sems("local")])
        cp.start()
        return cp

    barrier = pltpu.get_barrier_semaphore()
    for d in [p[0] for p in yk_peers] + xz_peers:
        pl.semaphore_signal(barrier, inc=1, device_id=d, device_id_type=MESH)

    def genes_of(ref, b):
        return ref.at[..., pl.ds(pl.multiple_of(b * wide, wide), wide)]

    blocks = (yo * 2 + ko, yo * 2 + k, y * 2 + ko, yk)
    lg_copy = local(lg_hbm, lgv)
    ex_copies = [local(genes_of(ex_hbm, b), exv.at[i]) for i, b in enumerate(blocks)]
    late = [
        local(genes_of(sp_hbm.at[0], yk), tgt.at[yk]),
        local(ids_hbm, ids_ref),
        local(cnt_hbm, cnt_ref),
    ]

    lg_copy.wait()
    piece = 128
    total = jnp.zeros((1, cols), F32)
    total_low = jnp.zeros((1, cols), F32)
    for i in range(cells // piece):
        e = jnp.exp(lgv[pl.ds(i * piece, piece), :].astype(F32))
        low = e.astype(BF16).astype(F32)
        total = total + jnp.sum(e, axis=0, keepdims=True)
        total_low = total_low + jnp.sum(low, axis=0, keepdims=True)
        et[:, pl.ds(i * piece, piece)] = low.T.astype(BF16)
    s_own[0:1, :] = total
    s_own[1:2, :] = total_low

    half = wide // 2

    def forward(i):
        ex_copies[i].wait()
        for n in range(2):
            lanes = pl.ds(n * half, half)
            low = exv[i, :, lanes].astype(BF16)
            xl[blocks[i], :, lanes] = low
            pf[i, :, :, lanes] = jnp.dot(et[...], low, preferred_element_type=F32).reshape(
                nz, rows, half
            )

    cut = rows * 3 // 8
    r1, r2 = pl.ds(0, cut), pl.ds(cut, rows - cut)
    most = cells * 13 // 16
    early, last = pl.ds(0, most), pl.ds(most, cells - most)

    forward(0)
    forward(1)
    pl.semaphore_wait(barrier, len(yk_peers) + len(xz_peers))
    s_sib_in = remote(s_own, s_sib, sib)
    sib_r1 = [remote(pf.at[0, q, r1], psib.at[0, q, r1], sib) for q in others + [z]]
    sib_r2 = remote(pf.at[0, :, r2], psib.at[0, :, r2], sib)
    lg_in = [remote(lg_hbm.at[early], lgo.at[early], xp, late=True)]
    forward(2)
    s_sib_in()
    s_pair[...] = s_own[...] + s_sib[...]
    s_y_in = remote(s_pair, s_y, yp)

    y_send = sems("send")
    y_in = {}

    def send_y(i, r, q):
        if r is r1:
            sib_r1[i]()
        ysend[q, r] = (pf[1, q, r] + psib[0, q, r]).astype(BF16)
        y_in[r.start, i] = sems("recv")
        put(ysend.at[q, r], yrecv.at[q, r], yp, y_send, y_in[r.start, i])

    for i, q in enumerate(others[:2]):
        send_y(i, r1, q)
    forward(3)
    sib_rest = remote(pf.at[2], psib.at[1], sib)
    send_y(2, r1, others[2])
    sib_r2()
    for i, q in enumerate(others):
        send_y(i, r2, q)
    t_in = spread_to(
        [(genes_of(sp_hbm.at[0], b), tgt.at[yk], d) for d, b in yk_peers],
        lambda n: tgt.at[pl.ds(0, n)],
    )
    send_y(nz - 1, r1, z)
    send_y(nz - 1, r2, z)
    sends.append((ysend, y_send))

    s_y_in()
    s_quad[...] = s_pair[...] + s_y[...]
    s_z[z] = s_quad[...]
    s_z_in = spread_to(
        [(s_quad, s_z.at[z], d) for d in z_peers], lambda n: s_z.at[pl.ds(0, n)]
    )

    z_send, z_recv = sems("send"), sems("recv")

    def add_y(i, r, q):
        landed(yrecv.at[q, r], y_in[r.start, i])
        return pf[3, q, r] + psib[1, q, r] + yrecv[q, r].astype(F32)

    sib_rest()
    for r in (r1, r2):
        for i, q in enumerate(others):
            zsend[q, r] = add_y(i, r, q).astype(BF16)
            put(zsend.at[q, r], zrecv.at[z, r], z_peers[i], z_send, z_recv)
    sends.append((zsend.at[pl.ds(0, nz - 1)], z_send))

    for cp in late:
        cp.wait()
    t_in()
    eye = lax.broadcasted_iota(jnp.int32, (rows, rows), 0) == lax.broadcasted_iota(
        jnp.int32, (rows, rows), 1
    )

    def to_col(v):
        return jnp.sum(jnp.where(eye, jnp.broadcast_to(v, (rows, rows)), 0.0), axis=1, keepdims=True)

    def to_row(v):
        return jnp.sum(jnp.where(eye, jnp.broadcast_to(v, (rows, rows)), 0.0), axis=0, keepdims=True)

    mine_cols = pl.ds(pl.multiple_of(z * rows, rows), rows)
    slide = to_col(ids_ref[:, mine_cols].astype(F32))
    second = jnp.broadcast_to(slide > 0.5, (rows, wide))

    def by_slide(v):
        a = jnp.sum(jnp.where(second, 0.0, v), axis=0, keepdims=True)
        b = jnp.sum(jnp.where(second, v, 0.0), axis=0, keepdims=True)
        return a, b

    target = tgt[...].reshape(rows, wide)
    square = target * target
    for s, v in enumerate(by_slide(square)):
        gtrue[me, s : s + 1, :] = v
    strue[yk] = to_row(jnp.sum(square, axis=1, keepdims=True))

    def share(by_gene, by_spot):
        a = spread_to(
            [(by_gene.at[me], by_gene.at[me], d) for d in xz_peers], lambda n: by_gene.at[pl.ds(0, n)], late=True
        )
        b = spread_to(
            [(by_spot.at[yk], by_spot.at[yk], d) for d, _ in yk_peers],
            lambda n: by_spot.at[pl.ds(0, n)],
            late=True,
        )
        return a, b

    true_in = share(gtrue, strue)

    own_1 = add_y(nz - 1, r1, z)
    own_2 = add_y(nz - 1, r2, z)

    s_z_in()
    whole_sum = s_z[0]
    for q in range(1, nz):
        whole_sum = whole_sum + s_z[q]
    mass = whole_sum[0:1, :]
    inv_mass = 1.0 / mass
    slides = ids_ref[...].astype(F32)
    counts = cnt_ref[...].astype(F32)
    aux[x, 0:1, :] = mass
    aux[x, 1:2, :] = slides
    aux[x, 2:3, :] = counts
    aux[x, 3:4, :] = jnp.zeros((1, cols), F32)
    aux_in = remote(aux.at[x], aux.at[x], xp, late=True)
    low_sum = s_z[0, 1:2, mine_cols]
    for q in range(1, nz):
        low_sum = low_sum + s_z[q, 1:2, mine_cols]
    inv_low = 1.0 / to_col(low_sum)

    landed(zrecv.at[pl.ds(0, nz - 1)], z_recv)
    pred = jnp.concatenate([own_1, own_2], axis=0)
    for q in others:
        pred = pred + zrecv[q].astype(F32)
    pred = pred * inv_low
    both = pred * target
    pair = pred * pred
    for r, v in enumerate((both, pair)):
        for s, w in enumerate(by_slide(v)):
            gsum[me, 2 * r + s : 2 * r + s + 1, :] = w
        ssum[yk, r : r + 1, :] = to_row(jnp.sum(v, axis=1, keepdims=True))
    sum_in = share(gsum, ssum)
    lg_in.append(remote(lg_hbm.at[last], lgo.at[last], xp, late=True))
    prd[...] = pred.reshape(YK, part, wide)
    p_in = spread_to(
        [(prd.at[b], p_out.at[yk], d) for d, b in yk_peers], lambda n: p_out.at[pl.ds(0, n)], late=True
    )
    p_out[yk] = prd[yk]

    def weights(src, scale, to):
        for i in range(cells // piece):
            r = pl.ds(i * piece, piece)
            wv[to, r, :] = (jnp.exp(src[r, :].astype(F32)) * scale).astype(BF16)

    weights(lgv, inv_mass, x)
    for wait in true_in + sum_in:
        wait()
    for ref, i in sends:
        left(ref, i)
    used = dict(taken)
    taken.update(send=0, recv=0)
    sends.clear()

    def added(ref, n):
        v = ref[0]
        for q in range(1, n):
            v = v + ref[q]
        return v

    genes = YK * wide
    spots = nx * cols
    gene_step = -1.0 / (2 * genes)
    spot_step = -1.0 / spots
    gs = added(gsum, nx * nz)
    gene_a = lax.rsqrt(gs[2:4] + EPSILON)
    gene_b = lax.rsqrt(added(gtrue, nx * nz) + EPSILON)
    gene_cos = gs[0:2] * gene_a * gene_b
    t_gene = gene_step * gene_a * gene_b
    p_gene = -gene_step * gs[0:2] * gene_b * gene_a * gene_a * gene_a
    ss = added(ssum, YK)
    pred_scale = lax.rsqrt(ss[1:2] + EPSILON)
    true_scale = lax.rsqrt(added(strue, YK) + EPSILON)
    spot_cos = ss[0:1] * pred_scale * true_scale
    t_spot = to_col(spot_step * pred_scale * true_scale)
    p_spot = to_col(-spot_step * ss[0:1] * pred_scale * pred_scale * pred_scale * true_scale)

    def of_slide(v):
        return jnp.where(
            second, jnp.broadcast_to(v[1:2], (rows, wide)), jnp.broadcast_to(v[0:1], (rows, wide))
        )

    grad = (of_slide(t_gene) + t_spot) * target + (of_slide(p_gene) + p_spot) * pred
    low = grad.astype(BF16)
    g[me, y, k] = low

    part_a, part_b, part_c = pl.ds(0, cut), pl.ds(cut, cut), pl.ds(2 * cut, rows - 2 * cut)
    part_ab = pl.ds(0, 2 * cut)
    z_out, c_out = sems("send"), sems("send")
    y_out, x_out, cy_out, cx_out, cd_out, a_out, b_out, core_out = (sems("send") for _ in range(8))
    from_z, from_y, from_x = (sems("recv", 2 * nz) for _ in range(3))
    from_a, from_b = (sems("recv", nz) for _ in range(2))
    cy_in, cx_in, cd_in = (sems("recv") for _ in range(3))
    from_c, core_in = sems("recv", 4 * nz), sems("recv", 4)
    kinds = ((x, y, 0), (xo, y, 2), (x, yo, 1), (xo, yo, 3))

    def to_core(shard, region):
        put(shard, shard, sib, core_out, core_in + region)

    def pass_on(shard, upward, send, recv):
        @pl.when(z < nz - 1 if upward else z > 0)
        def _():
            put(shard, shard, dev(z + 1 if upward else z - 1, y, k, x), send, recv)

    def own_z():
        for h, r in enumerate((part_a, part_b)):
            shard = g.at[me, y, k, r]
            pass_on(shard, True, z_out, from_z + 2 * z + h)
            pass_on(shard, False, z_out, from_z + 2 * z + h)

    def own_c():
        shard = g.at[me, y, k, part_c]
        put(shard, shard, yp, cy_out, cy_in)
        put(shard, shard, xp, cx_out, cx_in)

    def own_y():
        for h, r in enumerate((part_a, part_b)):
            shard = g.at[me, y, k, r]
            put(shard, shard, yp, y_out, from_y + 2 * z + h)

    def own_x():
        for h, r in ((1, part_b), (0, part_a)):
            shard = g.at[me, y, k, r]
            put(shard, shard, xp, x_out, from_x + 2 * z + h)

    def own_core():
        to_core(g.at[me, y, k], 0)

    def start_c(kind):
        plane, yy, _ = kinds[kind]
        shard = g.at[plane * nz + z, yy, k, part_c]
        pass_on(shard, True, c_out, from_c + 4 * z + kind)
        pass_on(shard, False, c_out, from_c + 4 * z + kind)

    def wait_cy():
        shard = g.at[me, yo, k, part_c]
        landed(shard, cy_in)
        put(shard, shard, xp, cd_out, cd_in)
        to_core(shard, 1)

    def wait_cx():
        shard = g.at[xo * nz + z, y, k, part_c]
        landed(shard, cx_in)
        to_core(shard, 2)

    def wait_cd():
        shard = g.at[xo * nz + z, yo, k, part_c]
        landed(shard, cd_in)
        to_core(shard, 3)

    def at_distance(d, act):
        if d == 0:
            act(z, False)
            return

        @pl.when(z >= d)
        def _():
            act(z - d, False)

        @pl.when(z < nz - d)
        def _():
            act(z + d, True)

    def take_z(q, above):
        for h, r in enumerate((part_a, part_b)):
            shard = g.at[x * nz + q, y, k, r]
            landed(shard, from_z + 2 * q + h)
            pass_on(shard, not above, z_out, from_z + 2 * q + h)
            put(shard, shard, yp, y_out, from_y + 2 * q + h)
            put(shard, shard, xp, x_out, from_x + 2 * q + h)
            to_core(shard, 0)

    def take_c(kind):
        def act(q, above):
            plane, yy, region = kinds[kind]
            shard = g.at[plane * nz + q, yy, k, part_c]
            landed(shard, from_c + 4 * q + kind)
            pass_on(shard, not above, c_out, from_c + 4 * q + kind)
            to_core(shard, region)

        return act

    def take_y(q, above):
        for h, r in enumerate((part_a, part_b)):
            shard = g.at[x * nz + q, yo, k, r]
            landed(shard, from_y + 2 * q + h)
            if h == 0:
                put(shard, shard, xp, a_out, from_a + q)
            to_core(shard, 1)

    def take_x(q, above):
        for h, r in ((1, part_b), (0, part_a)):
            shard = g.at[xo * nz + q, y, k, r]
            landed(shard, from_x + 2 * q + h)
            if h == 1:
                put(shard, shard, yp, b_out, from_b + q)
            to_core(shard, 2)

    def take_d(q, above):
        for recv, r in ((from_a, part_a), (from_b, part_b)):
            shard = g.at[xo * nz + q, yo, k, r]
            landed(shard, recv + q)
            to_core(shard, 3)

    def grad_of(plane, yy, kk):
        return g[plane, yy, kk].reshape(cols, wide)

    def weight_term(yy, kk):
        return lax.dot_general(
            xl[yy * 2 + kk], grad_of(here, yy, kk), (((1,), (1,)), ((), ())), preferred_element_type=F32
        )

    def expr_term(q, plane, yy, kk):
        return jnp.dot(wv[q], grad_of(plane, yy, kk), preferred_element_type=F32)

    lane = lax.broadcasted_iota(jnp.int32, (1, rows), 1)

    own_z()
    own_c()
    start_c(0)
    own_x()
    own_y()
    st1[yk, 0:1, :] = to_row(jnp.sum(low.astype(F32) * pred, axis=1, keepdims=True))
    st1[yk, 1:2, :] = jnp.where(lane == 0, jnp.sum(gene_cos), 0.0)
    st1_in = spread_to([(st1.at[yk], st1.at[yk], d) for d, _ in yk_peers], lambda n: st1.at[pl.ds(0, n)])
    wait_cx()
    start_c(1)
    wait_cy()
    start_c(2)
    at_distance(1, take_z)
    own_core()
    at_distance(1, take_c(0))
    wait_cd()
    at_distance(2, take_z)
    at_distance(2, take_c(0))
    start_c(3)
    at_distance(1, take_y)
    at_distance(1, take_x)
    at_distance(3, take_z)
    take_y(z, False)
    at_distance(1, take_c(2))
    at_distance(1, take_c(1))
    take_x(z, False)
    at_distance(3, take_c(0))
    st1_in()
    aux_in()
    for wait in lg_in:
        wait()
    weights(lgo, 1.0 / aux[xo, 0:1, :], xo)
    whole = added(st1, YK)
    st2[me, 0:1, :] = whole[0:1]
    st2[me, 1:2, :] = jnp.where(lane == 0, whole[1:2], jnp.where(lane == 1, jnp.sum(spot_cos), 0.0))
    st2_in = spread_to([(st2.at[me], st2.at[me], d) for d in xz_peers], lambda n: st2.at[pl.ds(0, n)])
    lgrad[...] = weight_term(y, k)
    eg[y, k] = expr_term(x, here, y, k)
    at_distance(1, take_c(3))
    at_distance(2, take_x)
    at_distance(2, take_y)
    at_distance(2, take_c(2))
    at_distance(2, take_c(1))
    at_distance(3, take_y)
    at_distance(3, take_x)
    landed(g.at[here, y, ko], core_in)
    lgrad[...] += weight_term(y, ko)
    eg[y, ko] = expr_term(x, here, y, ko)
    at_distance(3, take_c(2))
    at_distance(2, take_c(3))
    lgrad[...] += weight_term(yo, k)
    eg[yo, k] = expr_term(x, here, yo, k)
    take_d(z, False)
    at_distance(1, take_d)
    at_distance(3, take_c(1))
    at_distance(2, take_d)
    at_distance(3, take_c(3))
    at_distance(3, take_d)
    eg[y, k] += expr_term(xo, there, y, k)
    landed(g.at[here, yo, ko], core_in + 1)
    lgrad[...] += weight_term(yo, ko)

    kl = 0.0
    slide_mass, slide_count = [], []
    for s in range(2):
        m = n = cl = cm = 0.0
        for q in range(nx):
            of_s = jnp.abs(aux[q, 1:2, :] - s) < 0.5
            n_q = jnp.where(of_s, aux[q, 2:3, :], 0.0)
            m = m + jnp.sum(jnp.where(of_s, aux[q, 0:1, :], 0.0))
            n = n + jnp.sum(n_q)
            cl = cl + jnp.sum(n_q * jnp.log(aux[q, 2:3, :]))
            cm = cm + jnp.sum(n_q * jnp.log(aux[q, 0:1, :]))
        some = n > 0.5
        m = jnp.full((1, 128), jnp.where(some, m, 1.0), F32)
        n = jnp.full((1, 128), jnp.where(some, n, 1.0), F32)
        kl = kl + jnp.where(some, (cl - cm) / n - jnp.log(n) + jnp.log(m), 0.0)
        slide_mass.append(m[:, 0:1])
        slide_count.append(n[:, 0:1])
    is_second = slides > 0.5
    mass_grad = mass / jnp.where(is_second, slide_mass[1], slide_mass[0]) - counts / jnp.where(
        is_second, slide_count[1], slide_count[0]
    )
    st2_in()
    gene_total = whole[1:2]
    spot_total = added(st2, nx * nz)[1:2]
    loss_out[...] = (
        -jnp.sum(jnp.where(lane == 0, gene_total, 0.0)) / (2 * genes)
        - jnp.sum(jnp.where(lane == 1, spot_total, 0.0)) / spots
        + kl
    )
    vec[0:1, :] = inv_mass
    vec[1:2, :] = mass_grad - jnp.concatenate([st2[x * nz + q, 0:1, :] for q in range(nz)], axis=1)

    p_in()
    landed(g.at[there, y, ko], core_in + 2)
    landed(g.at[there, yo, ko], core_in + 3)
    for ref, i in sends + late_sends:
        left(ref, i)
    left(g.at[here, y, k, part_ab], y_out)
    left(g.at[here, y, k, part_ab], x_out)
    for i in (cy_out, cx_out, cd_out):
        left(g.at[me, y, k, part_c], i)
    left(g.at[here, yo, k, part_a], a_out)
    left(g.at[there, y, k, part_b], b_out)
    left(g.at[:, :, k], core_out)
    at_end = (z == 0) | (z == nz - 1)

    @pl.when(at_end)
    def _():
        left(g.at[me, y, k, part_ab], z_out)
        left(g.at[pl.ds(0, 4), y, k, part_c], c_out)

    @pl.when(jnp.logical_not(at_end))
    def _():
        left(g.at[pl.ds(0, nz + 1), y, k, part_ab], z_out)
        left(g.at[pl.ds(0, nz + 1), y, k], c_out)

    needed = {kind: max(used[kind], taken[kind]) + kept[kind] for kind in kept}
    assert needed == size, needed


def backward_kernel(
    nz, w_ref, g_ref, part_ref, lgrad_ref, lg_ref, vec_ref, p_ref, loss_ref,
    eg_hbm, lgrad_hbm, pred_ref, total_ref, eg, lgrad, done,
):
    c = lax.axis_index("cells")
    x = lax.axis_index("spots")
    y, k = (c % YK) // 2, c % 2
    nx, cells, cols = w_ref.shape
    wide = g_ref.shape[4]
    half = wide // 2
    xo = (x + 1) % nx
    copies = []

    def out(src, dst):
        cp = pltpu.make_async_copy(src, dst, done.at[len(copies)])
        cp.start()
        copies.append(cp)

    def genes_at(yy, kk, h, n):
        return eg_hbm.at[:, pl.ds(pl.multiple_of((yy * 2 + kk) * wide + h * half, half), n)]

    def term(q, yy, kk, lanes):
        block = g_ref[pl.ds(q * nz, nz), yy, kk, :, lanes].reshape(cols, half)
        return jnp.dot(w_ref[q], block, preferred_element_type=F32)

    out(part_ref.at[y, k], genes_at(y, k, 0, wide))
    for b in range(YK):
        out(p_ref.at[b], pred_ref.at[:, b * wide : (b + 1) * wide])
    for i, (yy, kk) in enumerate(((y, 1 - k), (1 - y, k), (1 - y, 1 - k))):
        for h in range(2):
            lanes = pl.ds(h * half, half)
            mine = part_ref[yy, kk, :, lanes] if i < 2 else term(x, yy, kk, lanes)
            eg[2 * i + h] = mine + term(xo, yy, kk, lanes)
            out(eg.at[2 * i + h], genes_at(yy, kk, h, half))
        if i == 0:
            lgrad[...] = (
                jnp.exp(lg_ref[...].astype(F32)) * vec_ref[0:1, :] * (lgrad_ref[...] + vec_ref[1:2, :])
            )
            out(lgrad, lgrad_hbm)
    total_ref[...] = loss_ref[:, 0:1]
    for cp in copies:
        cp.wait()


def step(ncells, nx, logits, expression, spatial, slide_ids, spot_counts):
    cells, cols = logits.shape
    genes = expression.shape[1]
    nz = ncells // YK
    rows = cols // nz
    wide = genes // YK
    part = rows // YK
    half = wide // 2
    anywhere = pl.BlockSpec(memory_space=pl.ANY)
    whole = pl.BlockSpec(memory_space=pltpu.VMEM)
    *held, p, loss = pl.pallas_call(
        functools.partial(forward_kernel, nz, nx),
        out_shape=(
            pltpu.VMEM((nx, cells, cols), BF16),
            pltpu.VMEM((nx * nz, 2, 2, rows, wide), BF16),
            pltpu.VMEM((2, 2, cells, wide), F32),
            pltpu.VMEM((cells, cols), F32),
            pltpu.VMEM((cells, cols), BF16),
            pltpu.VMEM((2, cols), F32),
            pltpu.VMEM((YK, part, wide), F32),
            pltpu.VMEM((1, 128), F32),
        ),
        in_specs=[anywhere] * 5,
        out_specs=(whole,) * 8,
        scratch_shapes=[
            pltpu.VMEM((cells, cols), BF16),
            pltpu.VMEM((cols, cells), BF16),
            pltpu.VMEM((YK, cells, wide), F32),
            pltpu.VMEM((YK, cells, wide), BF16),
            pltpu.VMEM((YK, nz, rows, wide), F32),
            pltpu.VMEM((2, nz, rows, wide), F32),
            pltpu.VMEM((nz, rows, wide), BF16),
            pltpu.VMEM((nz, rows, wide), BF16),
            pltpu.VMEM((nz, rows, wide), BF16),
            pltpu.VMEM((nz, rows, wide), BF16),
            pltpu.VMEM((YK, part, wide), F32),
            pltpu.VMEM((YK, part, wide), F32),
            pltpu.VMEM((2, cols), F32),
            pltpu.VMEM((2, cols), F32),
            pltpu.VMEM((2, cols), F32),
            pltpu.VMEM((2, cols), F32),
            pltpu.VMEM((2, cols), F32),
            pltpu.VMEM((nz, 2, cols), F32),
            pltpu.VMEM((nx, 4, cols), F32),
            pltpu.VMEM((nx * nz, 2, wide), F32),
            pltpu.VMEM((YK, 1, rows), F32),
            pltpu.VMEM((nx * nz, 4, wide), F32),
            pltpu.VMEM((YK, 2, rows), F32),
            pltpu.VMEM((YK, 2, rows), F32),
            pltpu.VMEM((nx * nz, 2, rows), F32),
            pltpu.VMEM((1, cols), jnp.int32),
            pltpu.VMEM((1, cols), jnp.int32),
            pltpu.SemaphoreType.DMA((8,)),
            pltpu.SemaphoreType.DMA((20,)),
            pltpu.SemaphoreType.DMA((17 + 12 * nz,)),
        ],
        compiler_params=pltpu.CompilerParams(
            collective_id=0, has_side_effects=True, vmem_limit_bytes=36 << 20
        ),
        name="forward_and_gather",
    )(
        *(
            pltpu.with_memory_space_constraint(v, pltpu.HBM)
            for v in (logits, expression, spatial, slide_ids, spot_counts)
        )
    )

    held = [pltpu.with_memory_space_constraint(v, pltpu.VMEM) for v in held]
    return pl.pallas_call(
        functools.partial(backward_kernel, nz),
        out_shape=(
            jax.ShapeDtypeStruct((cells, genes), F32),
            jax.ShapeDtypeStruct((cells, cols), F32),
            jax.ShapeDtypeStruct((part, genes), F32),
            jax.ShapeDtypeStruct((1, 1), F32),
        ),
        in_specs=[whole] * 8,
        out_specs=(anywhere, anywhere, anywhere, whole),
        scratch_shapes=[
            pltpu.VMEM((6, cells, half), F32),
            pltpu.VMEM((cells, cols), F32),
            pltpu.SemaphoreType.DMA((12,)),
        ],
        compiler_params=pltpu.CompilerParams(vmem_limit_bytes=24 << 20),
        name="backward",
    )(*held, p, loss)


def kernel_step(ncells, nx, *args):
    grad_expr, grad_logits, predicted, loss = step(ncells, nx, *args)
    return (predicted[None], loss[0, 0], grad_logits, grad_expr)


def fits(ncells, nx, logits, expression, spatial):
    cells, cols = logits.shape
    genes = expression.shape[1]
    if ncells != 4 * YK or nx != 2 or cols % (ncells // YK) or genes % (YK * 256):
        return False
    rows = cols // (ncells // YK)
    held = (cells + rows) * genes * 8 + cells * cols * 16 + cols * genes * 16
    return rows % 128 == 0 and cells % 128 == 0 and held < 50 << 20


def plain_step(logits, expression, spatial, slide_ids, spot_counts):
    highest = lax.Precision.HIGHEST
    ncells = lax.axis_size("cells")
    nspots = lax.axis_size("spots")
    columns = logits.shape[1]
    genes = expression.shape[1]
    out_rows = columns // ncells
    scores = logits.astype(F32)
    col_peak = lax.pmax(jnp.max(scores, axis=0), "cells")
    shifted = jnp.exp(scores - col_peak)
    col_total = lax.psum(jnp.sum(shifted, axis=0), "cells")
    weights = shifted / col_total
    log_mass = col_peak + jnp.log(col_total)
    weights_low = weights.astype(BF16)
    expr_low = expression.astype(BF16)
    contract_first = (((0,), (0,)), ((), ()))
    predicted = lax.psum_scatter(
        lax.dot_general(weights_low, expr_low, contract_first, preferred_element_type=F32),
        "cells",
        scatter_dimension=0,
        tiled=True,
    )
    target = spatial[0]
    member_all = (slide_ids[0][:, None] == jnp.arange(2, dtype=jnp.int32)[None, :]).astype(F32)
    first_row = lax.axis_index("cells") * out_rows
    member_rows = lax.dynamic_slice_in_dim(member_all, first_row, out_rows, 0)
    gene_inner = jnp.dot(member_rows.T, predicted * target, precision=highest)
    gene_pred = jnp.dot(member_rows.T, predicted * predicted, precision=highest)
    gene_true = jnp.dot(member_rows.T, target * target, precision=highest)
    spot_inner = jnp.sum(predicted * target, axis=1)
    pred_scale = lax.rsqrt(jnp.sum(predicted * predicted, axis=1) + EPSILON)
    true_scale = lax.rsqrt(jnp.sum(target * target, axis=1) + EPSILON)
    spot_sum = jnp.sum(spot_inner * pred_scale * true_scale)
    counts_real = spot_counts[0].astype(F32)
    exp_mass = jnp.exp(log_mass)
    local_mass = jnp.dot(member_all.T, exp_mass, precision=highest)
    local_count = jnp.dot(member_all.T, counts_real, precision=highest)
    local_clog = jnp.dot(member_all.T, counts_real * jnp.log(counts_real), precision=highest)
    local_clse = jnp.dot(member_all.T, counts_real * log_mass, precision=highest)
    slide_mass, slide_count, count_log, count_lse = lax.psum(
        (local_mass, local_count, local_clog, local_clse), "spots"
    )
    gene_inner, gene_pred, gene_true, spot_total = lax.psum(
        (gene_inner, gene_pred, gene_true, spot_sum), ("cells", "spots")
    )
    gene_a = lax.rsqrt(gene_pred + EPSILON)
    gene_b = lax.rsqrt(gene_true + EPSILON)
    gene_cos = gene_inner * gene_a * gene_b
    total_spots = columns * nspots
    some = slide_count > 0.5
    slide_count = jnp.where(some, slide_count, 1.0)
    slide_mass = jnp.where(some, slide_mass, 1.0)
    kl_value = jnp.sum(
        jnp.where(
            some,
            (count_log - count_lse) / slide_count - jnp.log(slide_count) + jnp.log(slide_mass),
            0.0,
        )
    )
    loss = -jnp.mean(gene_cos) - spot_total / total_spots + kl_value
    gene_step = -1.0 / (2 * genes)
    inner_grad = gene_step * gene_a * gene_b
    square_grad = -0.5 * gene_step * gene_inner * gene_b * gene_a * gene_a * gene_a
    pred_grad = jnp.dot(member_rows, inner_grad, precision=highest) * target
    pred_grad = pred_grad + 2.0 * jnp.dot(member_rows, square_grad, precision=highest) * predicted
    spot_step = -1.0 / total_spots
    pred_grad = pred_grad + (spot_step * pred_scale * true_scale)[:, None] * target
    pred_grad = (
        pred_grad
        - (spot_step * spot_inner * pred_scale * pred_scale * pred_scale * true_scale)[:, None]
        * predicted
    )
    grad_low = pred_grad.astype(BF16)
    mass_grad = exp_mass / jnp.dot(
        member_all, slide_mass, precision=highest
    ) - counts_real / jnp.dot(member_all, slide_count, precision=highest)
    contract_genes = (((1,), (1,)), ((), ()))
    grad_all = lax.all_gather(grad_low, "cells", axis=0, tiled=True)
    expr_part = jnp.dot(weights_low, grad_all, preferred_element_type=F32)
    weight_grad = lax.dot_general(
        expr_low, grad_all, contract_genes, preferred_element_type=F32
    )
    col_inner = lax.psum(jnp.sum(weights * weight_grad, axis=0), "cells")
    logit_grad = weights * (weight_grad - col_inner + mass_grad)
    expr_grad = lax.psum(expr_part, "spots")
    return (predicted[None], loss, logit_grad, expr_grad)


def solution(mesh):
    ncells, nx = mesh.shape["cells"], mesh.shape["spots"]

    def per_device(*args):
        if fits(ncells, nx, *args[:3]):
            return kernel_step(ncells, nx, *args)
        return plain_step(*args)

    return jax.shard_map(
        per_device,
        mesh=mesh,
        in_specs=(
            P("cells", "spots"),
            P("cells", None),
            P("spots", "cells", None),
            P("spots", None),
            P("spots", None),
        ),
        out_specs=(P("spots", "cells", None), P(), P("cells", "spots"), P("cells", None)),
        check_vma=False,
    )
```

```python
import functools

import jax
import jax.numpy as jnp
from jax import lax
from jax.experimental import pallas as pl
from jax.experimental.pallas import tpu as pltpu
from jax.sharding import PartitionSpec as P

EPSILON = 1e-06
MESH = pl.DeviceIdType.MESH
F32 = jnp.float32
BF16 = jnp.bfloat16
YK = 4


def forward_kernel(
    nz,
    nx,
    lg_hbm, ex_hbm, sp_hbm, ids_hbm, cnt_hbm,
    wv, g, eg, lgrad, lgv, vec, p_out, loss_out,
    lgo, et, exv, xl, pf, psib, ysend, yrecv, zsend, zrecv, tgt, prd,
    s_own, s_sib, s_pair, s_y, s_quad, s_z, aux, gtrue, strue, gsum, ssum, st1, st2, ids_ref, cnt_ref,
    loc, snd, rcv,
):
    cells, cols = lgv.shape
    rows, wide = pf.shape[2:]
    part = rows // YK
    c = lax.axis_index("cells")
    x = lax.axis_index("spots")
    z = c // YK
    yk = c % YK
    y = yk // 2
    k = yk % 2
    yo, ko, xo = 1 - y, 1 - k, (x + 1) % nx
    me = x * nz + z
    here, there = pl.ds(x * nz, nz), pl.ds(xo * nz, nz)

    def dev(zz, yy, kk, xx):
        return (zz * YK + yy * 2 + kk, xx)

    sib, yp, dia, xp = dev(z, y, ko, x), dev(z, yo, k, x), dev(z, yo, ko, x), dev(z, y, k, xo)
    yk_peers = ((sib, y * 2 + ko), (yp, yo * 2 + k), (dia, yo * 2 + ko))
    others = [(z + r) % nz for r in range(1, nz)]
    others = others[1:2] + others[:1] + others[2:]
    z_peers = [dev(q, y, k, x) for q in others]
    xz_peers = [dev(q, y, k, xo) for q in others] + z_peers + [xp]

    taken = {"send": 0, "recv": 0, "local": 0}
    kept = {"send": 0, "recv": 0}
    size = {"send": snd.shape[0], "recv": rcv.shape[0]}
    sends, late_sends = [], []

    def sems(kind, n=1):
        taken[kind] += n
        return taken[kind] - n

    def keep(kind):
        kept[kind] += 1
        return size[kind] - kept[kind]

    def put(src, dst, device, send, recv):
        pltpu.make_async_remote_copy(
            src_ref=src, dst_ref=dst, send_sem=snd.at[send], recv_sem=rcv.at[recv],
            device_id=device, device_id_type=MESH,
        ).start()

    def landed(ref, recv):
        pltpu.make_async_remote_copy(
            src_ref=ref, dst_ref=ref, send_sem=snd.at[0], recv_sem=rcv.at[recv],
            device_id=sib, device_id_type=MESH,
        ).wait_recv()

    def left(ref, send):
        pltpu.make_async_remote_copy(
            src_ref=ref, dst_ref=ref, send_sem=snd.at[send], recv_sem=rcv.at[0],
            device_id=sib, device_id_type=MESH,
        ).wait_send()

    def remote(src, dst, device, late=False):
        return spread_to([(src, dst, device)], lambda n: dst, late)

    def spread_to(pairs, size, late=False):
        take = keep if late else sems
        i, j = take("send"), take("recv")
        for src, dst, device in pairs:
            put(src, dst, device, i, j)
        (late_sends if late else sends).append((size(len(pairs)), i))
        return lambda: landed(size(len(pairs)), j)

    def local(src, dst):
        cp = pltpu.make_async_copy(src, dst, loc.at[sems("local")])
        cp.start()
        return cp

    barrier = pltpu.get_barrier_semaphore()
    for d in [p[0] for p in yk_peers] + xz_peers:
        pl.semaphore_signal(barrier, inc=1, device_id=d, device_id_type=MESH)

    def genes_of(ref, b):
        return ref.at[..., pl.ds(pl.multiple_of(b * wide, wide), wide)]

    blocks = (yo * 2 + ko, yo * 2 + k, y * 2 + ko, yk)
    lg_copy = local(lg_hbm, lgv)
    ex_copies = [local(genes_of(ex_hbm, b), exv.at[i]) for i, b in enumerate(blocks)]
    late = [
        local(genes_of(sp_hbm.at[0], yk), tgt.at[yk]),
        local(ids_hbm, ids_ref),
        local(cnt_hbm, cnt_ref),
    ]

    lg_copy.wait()
    piece = 128
    total = jnp.zeros((1, cols), F32)
    total_low = jnp.zeros((1, cols), F32)
    for i in range(cells // piece):
        e = jnp.exp(lgv[pl.ds(i * piece, piece), :].astype(F32))
        low = e.astype(BF16).astype(F32)
        total = total + jnp.sum(e, axis=0, keepdims=True)
        total_low = total_low + jnp.sum(low, axis=0, keepdims=True)
        et[:, pl.ds(i * piece, piece)] = low.T.astype(BF16)
    s_own[0:1, :] = total
    s_own[1:2, :] = total_low

    half = wide // 2

    def forward(i):
        ex_copies[i].wait()
        for n in range(2):
            lanes = pl.ds(n * half, half)
            low = exv[i, :, lanes].astype(BF16)
            xl[blocks[i], :, lanes] = low
            pf[i, :, :, lanes] = jnp.dot(et[...], low, preferred_element_type=F32).reshape(
                nz, rows, half
            )

    cut = rows * 3 // 8
    r1, r2 = pl.ds(0, cut), pl.ds(cut, rows - cut)
    most, more = cells * 13 // 16, cells // 8
    early, gap, last = pl.ds(0, most), pl.ds(most, more), pl.ds(most + more, cells - most - more)

    forward(0)
    pl.semaphore_wait(barrier, len(yk_peers) + len(xz_peers))
    s_sib_in = remote(s_own, s_sib, sib)
    sib_r1 = [remote(pf.at[0, q, r1], psib.at[0, q, r1], sib) for q in others + [z]]
    sib_r2 = remote(pf.at[0, :, r2], psib.at[0, :, r2], sib)
    lg_in = [remote(lg_hbm.at[early], lgo.at[early], xp, late=True)]
    forward(1)
    s_sib_in()
    s_pair[...] = s_own[...] + s_sib[...]
    s_y_in = remote(s_pair, s_y, yp)

    y_send = sems("send")
    y_in = {}

    def send_y(i, r, q):
        if r is r1:
            sib_r1[i]()
        ysend[q, r] = (pf[1, q, r] + psib[0, q, r]).astype(BF16)
        y_in[r.start, i] = sems("recv")
        put(ysend.at[q, r], yrecv.at[q, r], yp, y_send, y_in[r.start, i])

    for i, q in enumerate(others):
        send_y(i, r1, q)
    forward(2)
    sib_rest = remote(pf.at[2], psib.at[1], sib)
    forward(3)
    sib_r2()
    for i, q in enumerate(others):
        send_y(i, r2, q)
    t_in = spread_to(
        [(genes_of(sp_hbm.at[0], b), tgt.at[yk], d) for d, b in yk_peers],
        lambda n: tgt.at[pl.ds(0, n)],
    )
    send_y(nz - 1, r1, z)
    send_y(nz - 1, r2, z)
    sends.append((ysend, y_send))

    s_y_in()
    s_quad[...] = s_pair[...] + s_y[...]
    s_z[z] = s_quad[...]
    s_z_in = spread_to(
        [(s_quad, s_z.at[z], d) for d in z_peers], lambda n: s_z.at[pl.ds(0, n)]
    )

    z_send, z_recv = sems("send"), sems("recv")

    def add_y(i, r, q):
        landed(yrecv.at[q, r], y_in[r.start, i])
        return pf[3, q, r] + psib[1, q, r] + yrecv[q, r].astype(F32)

    sib_rest()
    for r in (r1, r2):
        for i, q in enumerate(others):
            zsend[q, r] = add_y(i, r, q).astype(BF16)
            put(zsend.at[q, r], zrecv.at[z, r], z_peers[i], z_send, z_recv)
    sends.append((zsend.at[pl.ds(0, nz - 1)], z_send))

    for cp in late:
        cp.wait()
    t_in()
    eye = lax.broadcasted_iota(jnp.int32, (rows, rows), 0) == lax.broadcasted_iota(
        jnp.int32, (rows, rows), 1
    )

    def to_col(v):
        return jnp.sum(jnp.where(eye, jnp.broadcast_to(v, (rows, rows)), 0.0), axis=1, keepdims=True)

    def to_row(v):
        return jnp.sum(jnp.where(eye, jnp.broadcast_to(v, (rows, rows)), 0.0), axis=0, keepdims=True)

    mine_cols = pl.ds(pl.multiple_of(z * rows, rows), rows)
    slide = to_col(ids_ref[:, mine_cols].astype(F32))
    second = jnp.broadcast_to(slide > 0.5, (rows, wide))

    def by_slide(v):
        a = jnp.sum(jnp.where(second, 0.0, v), axis=0, keepdims=True)
        b = jnp.sum(jnp.where(second, v, 0.0), axis=0, keepdims=True)
        return a, b

    target = tgt[...].reshape(rows, wide)
    square = target * target
    for s, v in enumerate(by_slide(square)):
        gtrue[me, s : s + 1, :] = v
    strue[yk] = to_row(jnp.sum(square, axis=1, keepdims=True))

    def share(by_gene, by_spot):
        a = spread_to(
            [(by_gene.at[me], by_gene.at[me], d) for d in xz_peers], lambda n: by_gene.at[pl.ds(0, n)], late=True
        )
        b = spread_to(
            [(by_spot.at[yk], by_spot.at[yk], d) for d, _ in yk_peers],
            lambda n: by_spot.at[pl.ds(0, n)],
            late=True,
        )
        return a, b

    true_in = share(gtrue, strue)

    own_1 = add_y(nz - 1, r1, z)
    own_2 = add_y(nz - 1, r2, z)

    s_z_in()
    whole_sum = s_z[0]
    for q in range(1, nz):
        whole_sum = whole_sum + s_z[q]
    mass = whole_sum[0:1, :]
    inv_mass = 1.0 / mass
    slides = ids_ref[...].astype(F32)
    counts = cnt_ref[...].astype(F32)
    aux[x, 0:1, :] = mass
    aux[x, 1:2, :] = slides
    aux[x, 2:3, :] = counts
    aux[x, 3:4, :] = jnp.zeros((1, cols), F32)
    aux_in = remote(aux.at[x], aux.at[x], xp, late=True)
    low_sum = s_z[0, 1:2, mine_cols]
    for q in range(1, nz):
        low_sum = low_sum + s_z[q, 1:2, mine_cols]
    inv_low = 1.0 / to_col(low_sum)

    landed(zrecv.at[pl.ds(0, nz - 1)], z_recv)
    pred = jnp.concatenate([own_1, own_2], axis=0)
    for q in others:
        pred = pred + zrecv[q].astype(F32)
    pred = pred * inv_low
    both = pred * target
    pair = pred * pred
    for r, v in enumerate((both, pair)):
        for s, w in enumerate(by_slide(v)):
            gsum[me, 2 * r + s : 2 * r + s + 1, :] = w
        ssum[yk, r : r + 1, :] = to_row(jnp.sum(v, axis=1, keepdims=True))
    sum_in = share(gsum, ssum)
    lg_in.append(remote(lg_hbm.at[gap], lgo.at[gap], xp, late=True))
    prd[...] = pred.reshape(YK, part, wide)
    p_in = spread_to(
        [(prd.at[b], p_out.at[yk], d) for d, b in yk_peers], lambda n: p_out.at[pl.ds(0, n)], late=True
    )
    p_out[yk] = prd[yk]

    def weights(src, scale, to):
        for i in range(cells // piece):
            r = pl.ds(i * piece, piece)
            wv[to, r, :] = (jnp.exp(src[r, :].astype(F32)) * scale).astype(BF16)

    weights(lgv, inv_mass, x)
    for wait in true_in + sum_in:
        wait()
    for ref, i in sends:
        left(ref, i)
    used = dict(taken)
    taken.update(send=0, recv=0)
    sends.clear()

    def added(ref, n):
        v = ref[0]
        for q in range(1, n):
            v = v + ref[q]
        return v

    genes = YK * wide
    spots = nx * cols
    gene_step = -1.0 / (2 * genes)
    spot_step = -1.0 / spots
    gs = added(gsum, nx * nz)
    gene_a = lax.rsqrt(gs[2:4] + EPSILON)
    gene_b = lax.rsqrt(added(gtrue, nx * nz) + EPSILON)
    gene_cos = gs[0:2] * gene_a * gene_b
    t_gene = gene_step * gene_a * gene_b
    p_gene = -gene_step * gs[0:2] * gene_b * gene_a * gene_a * gene_a
    ss = added(ssum, YK)
    pred_scale = lax.rsqrt(ss[1:2] + EPSILON)
    true_scale = lax.rsqrt(added(strue, YK) + EPSILON)
    spot_cos = ss[0:1] * pred_scale * true_scale
    t_spot = to_col(spot_step * pred_scale * true_scale)
    p_spot = to_col(-spot_step * ss[0:1] * pred_scale * pred_scale * pred_scale * true_scale)

    def of_slide(v):
        return jnp.where(
            second, jnp.broadcast_to(v[1:2], (rows, wide)), jnp.broadcast_to(v[0:1], (rows, wide))
        )

    grad = (of_slide(t_gene) + t_spot) * target + (of_slide(p_gene) + p_spot) * pred
    low = grad.astype(BF16)
    g[me, y, k] = low

    part_a, part_b, part_c = pl.ds(0, cut), pl.ds(cut, cut), pl.ds(2 * cut, rows - 2 * cut)
    part_ab = pl.ds(0, 2 * cut)
    z_out, c_out = sems("send"), sems("send")
    y_out, x_out, cy_out, cx_out, cd_out, a_out, b_out, core_out = (sems("send") for _ in range(8))
    from_z, from_y, from_x = (sems("recv", 2 * nz) for _ in range(3))
    from_a, from_b = (sems("recv", nz) for _ in range(2))
    cy_in, cx_in, cd_in = (sems("recv") for _ in range(3))
    from_c, core_in = sems("recv", 4 * nz), sems("recv", 4)
    kinds = ((x, y, 0), (xo, y, 2), (x, yo, 1), (xo, yo, 3))

    def to_core(shard, region):
        put(shard, shard, sib, core_out, core_in + region)

    def pass_on(shard, upward, send, recv):
        @pl.when(z < nz - 1 if upward else z > 0)
        def _():
            put(shard, shard, dev(z + 1 if upward else z - 1, y, k, x), send, recv)

    def own_z():
        for h, r in enumerate((part_a, part_b)):
            shard = g.at[me, y, k, r]
            pass_on(shard, True, z_out, from_z + 2 * z + h)
            pass_on(shard, False, z_out, from_z + 2 * z + h)

    def own_c():
        shard = g.at[me, y, k, part_c]
        put(shard, shard, yp, cy_out, cy_in)
        put(shard, shard, xp, cx_out, cx_in)

    def own_y():
        for h, r in enumerate((part_a, part_b)):
            shard = g.at[me, y, k, r]
            put(shard, shard, yp, y_out, from_y + 2 * z + h)

    def own_x():
        for h, r in ((1, part_b), (0, part_a)):
            shard = g.at[me, y, k, r]
            put(shard, shard, xp, x_out, from_x + 2 * z + h)

    def own_core():
        to_core(g.at[me, y, k], 0)

    def start_c(kind):
        plane, yy, _ = kinds[kind]
        shard = g.at[plane * nz + z, yy, k, part_c]
        pass_on(shard, True, c_out, from_c + 4 * z + kind)
        pass_on(shard, False, c_out, from_c + 4 * z + kind)

    def wait_cy():
        shard = g.at[me, yo, k, part_c]
        landed(shard, cy_in)
        put(shard, shard, xp, cd_out, cd_in)
        to_core(shard, 1)

    def wait_cx():
        shard = g.at[xo * nz + z, y, k, part_c]
        landed(shard, cx_in)
        to_core(shard, 2)

    def wait_cd():
        shard = g.at[xo * nz + z, yo, k, part_c]
        landed(shard, cd_in)
        to_core(shard, 3)

    def at_distance(d, act):
        if d == 0:
            act(z, False)
            return

        @pl.when(z >= d)
        def _():
            act(z - d, False)

        @pl.when(z < nz - d)
        def _():
            act(z + d, True)

    def take_z(q, above):
        for h, r in enumerate((part_a, part_b)):
            shard = g.at[x * nz + q, y, k, r]
            landed(shard, from_z + 2 * q + h)
            pass_on(shard, not above, z_out, from_z + 2 * q + h)
            put(shard, shard, yp, y_out, from_y + 2 * q + h)
            put(shard, shard, xp, x_out, from_x + 2 * q + h)
            to_core(shard, 0)

    def take_c(kind):
        def act(q, above):
            plane, yy, region = kinds[kind]
            shard = g.at[plane * nz + q, yy, k, part_c]
            landed(shard, from_c + 4 * q + kind)
            pass_on(shard, not above, c_out, from_c + 4 * q + kind)
            to_core(shard, region)

        return act

    def take_y(q, above):
        for h, r in enumerate((part_a, part_b)):
            shard = g.at[x * nz + q, yo, k, r]
            landed(shard, from_y + 2 * q + h)
            if h == 0:
                put(shard, shard, xp, a_out, from_a + q)
            to_core(shard, 1)

    def take_x(q, above):
        for h, r in ((1, part_b), (0, part_a)):
            shard = g.at[xo * nz + q, y, k, r]
            landed(shard, from_x + 2 * q + h)
            if h == 1:
                put(shard, shard, yp, b_out, from_b + q)
            to_core(shard, 2)

    def take_d(q, above):
        for recv, r in ((from_a, part_a), (from_b, part_b)):
            shard = g.at[xo * nz + q, yo, k, r]
            landed(shard, recv + q)
            to_core(shard, 3)

    def grad_of(plane, yy, kk):
        return g[plane, yy, kk].reshape(cols, wide)

    def weight_term(yy, kk):
        return lax.dot_general(
            xl[yy * 2 + kk], grad_of(here, yy, kk), (((1,), (1,)), ((), ())), preferred_element_type=F32
        )

    def expr_term(q, plane, yy, kk):
        return jnp.dot(wv[q], grad_of(plane, yy, kk), preferred_element_type=F32)

    lane = lax.broadcasted_iota(jnp.int32, (1, rows), 1)

    own_z()
    own_c()
    own_x()
    own_y()
    lg_in.append(remote(lg_hbm.at[last], lgo.at[last], xp, late=True))
    st1[yk, 0:1, :] = to_row(jnp.sum(low.astype(F32) * pred, axis=1, keepdims=True))
    st1[yk, 1:2, :] = jnp.where(lane == 0, jnp.sum(gene_cos), 0.0)
    st1_in = spread_to([(st1.at[yk], st1.at[yk], d) for d, _ in yk_peers], lambda n: st1.at[pl.ds(0, n)])
    start_c(0)
    own_core()
    wait_cx()
    start_c(1)
    wait_cy()
    start_c(2)
    at_distance(1, take_z)
    wait_cd()
    at_distance(1, take_c(0))
    start_c(3)
    at_distance(2, take_z)
    aux_in()
    for wait in lg_in:
        wait()
    weights(lgo, 1.0 / aux[xo, 0:1, :], xo)
    take_x(z, False)
    at_distance(2, take_c(0))
    at_distance(1, take_c(2))
    take_y(z, False)
    at_distance(1, take_c(1))
    at_distance(3, take_z)
    at_distance(1, take_c(3))
    at_distance(1, take_y)
    at_distance(2, take_y)
    at_distance(1, take_x)
    at_distance(3, take_c(0))
    st1_in()
    whole = added(st1, YK)
    st2[me, 0:1, :] = whole[0:1]
    st2[me, 1:2, :] = jnp.where(lane == 0, whole[1:2], jnp.where(lane == 1, jnp.sum(spot_cos), 0.0))
    st2_in = spread_to([(st2.at[me], st2.at[me], d) for d in xz_peers], lambda n: st2.at[pl.ds(0, n)])
    lgrad[...] = weight_term(y, k)
    at_distance(2, take_x)
    at_distance(2, take_c(2))
    landed(g.at[here, y, ko], core_in)
    lgrad[...] += weight_term(y, ko)
    eg[y, ko] = expr_term(x, here, y, ko)
    take_d(z, False)
    at_distance(3, take_y)
    at_distance(3, take_x)
    at_distance(2, take_c(1))
    eg[y, k] = expr_term(x, here, y, k)
    at_distance(3, take_c(2))
    at_distance(2, take_c(3))
    lgrad[...] += weight_term(yo, k)
    eg[yo, k] = expr_term(x, here, yo, k)
    at_distance(3, take_c(1))
    at_distance(1, take_d)
    eg[y, k] += expr_term(xo, there, y, k)
    at_distance(3, take_c(3))
    at_distance(2, take_d)
    at_distance(3, take_d)
    landed(g.at[here, yo, ko], core_in + 1)
    lgrad[...] += weight_term(yo, ko)

    kl = 0.0
    slide_mass, slide_count = [], []
    for s in range(2):
        m = n = cl = cm = 0.0
        for q in range(nx):
            of_s = jnp.abs(aux[q, 1:2, :] - s) < 0.5
            n_q = jnp.where(of_s, aux[q, 2:3, :], 0.0)
            m = m + jnp.sum(jnp.where(of_s, aux[q, 0:1, :], 0.0))
            n = n + jnp.sum(n_q)
            cl = cl + jnp.sum(n_q * jnp.log(aux[q, 2:3, :]))
            cm = cm + jnp.sum(n_q * jnp.log(aux[q, 0:1, :]))
        some = n > 0.5
        m = jnp.full((1, 128), jnp.where(some, m, 1.0), F32)
        n = jnp.full((1, 128), jnp.where(some, n, 1.0), F32)
        kl = kl + jnp.where(some, (cl - cm) / n - jnp.log(n) + jnp.log(m), 0.0)
        slide_mass.append(m[:, 0:1])
        slide_count.append(n[:, 0:1])
    is_second = slides > 0.5
    mass_grad = mass / jnp.where(is_second, slide_mass[1], slide_mass[0]) - counts / jnp.where(
        is_second, slide_count[1], slide_count[0]
    )
    st2_in()
    gene_total = whole[1:2]
    spot_total = added(st2, nx * nz)[1:2]
    loss_out[...] = (
        -jnp.sum(jnp.where(lane == 0, gene_total, 0.0)) / (2 * genes)
        - jnp.sum(jnp.where(lane == 1, spot_total, 0.0)) / spots
        + kl
    )
    vec[0:1, :] = inv_mass
    vec[1:2, :] = mass_grad - jnp.concatenate([st2[x * nz + q, 0:1, :] for q in range(nz)], axis=1)

    p_in()
    landed(g.at[there, y, ko], core_in + 2)
    landed(g.at[there, yo, ko], core_in + 3)
    for ref, i in sends + late_sends:
        left(ref, i)
    left(g.at[here, y, k, part_ab], y_out)
    left(g.at[here, y, k, part_ab], x_out)
    for i in (cy_out, cx_out, cd_out):
        left(g.at[me, y, k, part_c], i)
    left(g.at[here, yo, k, part_a], a_out)
    left(g.at[there, y, k, part_b], b_out)
    left(g.at[:, :, k], core_out)
    at_end = (z == 0) | (z == nz - 1)

    @pl.when(at_end)
    def _():
        left(g.at[me, y, k, part_ab], z_out)
        left(g.at[pl.ds(0, 4), y, k, part_c], c_out)

    @pl.when(jnp.logical_not(at_end))
    def _():
        left(g.at[pl.ds(0, nz + 1), y, k, part_ab], z_out)
        left(g.at[pl.ds(0, nz + 1), y, k], c_out)

    needed = {kind: max(used[kind], taken[kind]) + kept[kind] for kind in kept}
    assert needed == size, needed


def backward_kernel(
    nz, w_ref, g_ref, part_ref, lgrad_ref, lg_ref, vec_ref, p_ref, loss_ref,
    eg_hbm, lgrad_hbm, pred_ref, total_ref, eg, lgrad, done,
):
    c = lax.axis_index("cells")
    x = lax.axis_index("spots")
    y, k = (c % YK) // 2, c % 2
    nx, cells, cols = w_ref.shape
    wide = g_ref.shape[4]
    tall = cells // 2
    xo = (x + 1) % nx
    copies = []

    def out(src, dst):
        cp = pltpu.make_async_copy(src, dst, done.at[len(copies)])
        cp.start()
        copies.append(cp)

    def genes_at(yy, kk):
        return eg_hbm.at[:, pl.ds(pl.multiple_of((yy * 2 + kk) * wide, wide), wide)]

    def term(q, yy, kk, r):
        block = g_ref[pl.ds(q * nz, nz), yy, kk].reshape(cols, wide)
        return jnp.dot(w_ref[q, r, :], block, preferred_element_type=F32)

    out(part_ref.at[y, k], genes_at(y, k))
    lgrad[...] = jnp.exp(lg_ref[...].astype(F32)) * vec_ref[0:1, :] * (lgrad_ref[...] + vec_ref[1:2, :])
    out(lgrad, lgrad_hbm)
    for i, (yy, kk) in enumerate(((y, 1 - k), (1 - y, k), (1 - y, 1 - k))):
        for n in range(2):
            r = pl.ds(n * tall, tall)
            mine = part_ref[yy, kk, r, :] if i < 2 else term(x, yy, kk, r)
            eg[i, r, :] = mine + term(xo, yy, kk, r)
            out(eg.at[i, r], genes_at(yy, kk).at[r])
    for b in range(YK):
        out(p_ref.at[b], pred_ref.at[:, b * wide : (b + 1) * wide])
    total_ref[...] = loss_ref[:, 0:1]
    for cp in copies:
        cp.wait()


def step(ncells, nx, logits, expression, spatial, slide_ids, spot_counts):
    cells, cols = logits.shape
    genes = expression.shape[1]
    nz = ncells // YK
    rows = cols // nz
    wide = genes // YK
    part = rows // YK
    half = wide // 2
    anywhere = pl.BlockSpec(memory_space=pl.ANY)
    whole = pl.BlockSpec(memory_space=pltpu.VMEM)
    *held, p, loss = pl.pallas_call(
        functools.partial(forward_kernel, nz, nx),
        out_shape=(
            pltpu.VMEM((nx, cells, cols), BF16),
            pltpu.VMEM((nx * nz, 2, 2, rows, wide), BF16),
            pltpu.VMEM((2, 2, cells, wide), F32),
            pltpu.VMEM((cells, cols), F32),
            pltpu.VMEM((cells, cols), BF16),
            pltpu.VMEM((2, cols), F32),
            pltpu.VMEM((YK, part, wide), F32),
            pltpu.VMEM((1, 128), F32),
        ),
        in_specs=[anywhere] * 5,
        out_specs=(whole,) * 8,
        scratch_shapes=[
            pltpu.VMEM((cells, cols), BF16),
            pltpu.VMEM((cols, cells), BF16),
            pltpu.VMEM((YK, cells, wide), F32),
            pltpu.VMEM((YK, cells, wide), BF16),
            pltpu.VMEM((YK, nz, rows, wide), F32),
            pltpu.VMEM((2, nz, rows, wide), F32),
            pltpu.VMEM((nz, rows, wide), BF16),
            pltpu.VMEM((nz, rows, wide), BF16),
            pltpu.VMEM((nz, rows, wide), BF16),
            pltpu.VMEM((nz, rows, wide), BF16),
            pltpu.VMEM((YK, part, wide), F32),
            pltpu.VMEM((YK, part, wide), F32),
            pltpu.VMEM((2, cols), F32),
            pltpu.VMEM((2, cols), F32),
            pltpu.VMEM((2, cols), F32),
            pltpu.VMEM((2, cols), F32),
            pltpu.VMEM((2, cols), F32),
            pltpu.VMEM((nz, 2, cols), F32),
            pltpu.VMEM((nx, 4, cols), F32),
            pltpu.VMEM((nx * nz, 2, wide), F32),
            pltpu.VMEM((YK, 1, rows), F32),
            pltpu.VMEM((nx * nz, 4, wide), F32),
            pltpu.VMEM((YK, 2, rows), F32),
            pltpu.VMEM((YK, 2, rows), F32),
            pltpu.VMEM((nx * nz, 2, rows), F32),
            pltpu.VMEM((1, cols), jnp.int32),
            pltpu.VMEM((1, cols), jnp.int32),
            pltpu.SemaphoreType.DMA((8,)),
            pltpu.SemaphoreType.DMA((21,)),
            pltpu.SemaphoreType.DMA((18 + 12 * nz,)),
        ],
        compiler_params=pltpu.CompilerParams(
            collective_id=0, has_side_effects=True, vmem_limit_bytes=36 << 20
        ),
        name="forward_and_gather",
    )(
        *(
            pltpu.with_memory_space_constraint(v, pltpu.HBM)
            for v in (logits, expression, spatial, slide_ids, spot_counts)
        )
    )

    held = [pltpu.with_memory_space_constraint(v, pltpu.VMEM) for v in held]
    return pl.pallas_call(
        functools.partial(backward_kernel, nz),
        out_shape=(
            jax.ShapeDtypeStruct((cells, genes), F32),
            jax.ShapeDtypeStruct((cells, cols), F32),
            jax.ShapeDtypeStruct((part, genes), F32),
            jax.ShapeDtypeStruct((1, 1), F32),
        ),
        in_specs=[whole] * 8,
        out_specs=(anywhere, anywhere, anywhere, whole),
        scratch_shapes=[
            pltpu.VMEM((3, cells, wide), F32),
            pltpu.VMEM((cells, cols), F32),
            pltpu.SemaphoreType.DMA((12,)),
        ],
        compiler_params=pltpu.CompilerParams(vmem_limit_bytes=24 << 20),
        name="backward",
    )(*held, p, loss)


def kernel_step(ncells, nx, *args):
    grad_expr, grad_logits, predicted, loss = step(ncells, nx, *args)
    return (predicted[None], loss[0, 0], grad_logits, grad_expr)


def fits(ncells, nx, logits, expression, spatial):
    cells, cols = logits.shape
    genes = expression.shape[1]
    if ncells != 4 * YK or nx != 2 or cols % (ncells // YK) or genes % (YK * 256):
        return False
    rows = cols // (ncells // YK)
    held = (cells + rows) * genes * 8 + cells * cols * 16 + cols * genes * 16
    return rows % 128 == 0 and cells % 128 == 0 and held < 50 << 20


def plain_step(logits, expression, spatial, slide_ids, spot_counts):
    highest = lax.Precision.HIGHEST
    ncells = lax.axis_size("cells")
    nspots = lax.axis_size("spots")
    columns = logits.shape[1]
    genes = expression.shape[1]
    out_rows = columns // ncells
    scores = logits.astype(F32)
    col_peak = lax.pmax(jnp.max(scores, axis=0), "cells")
    shifted = jnp.exp(scores - col_peak)
    col_total = lax.psum(jnp.sum(shifted, axis=0), "cells")
    weights = shifted / col_total
    log_mass = col_peak + jnp.log(col_total)
    weights_low = weights.astype(BF16)
    expr_low = expression.astype(BF16)
    contract_first = (((0,), (0,)), ((), ()))
    predicted = lax.psum_scatter(
        lax.dot_general(weights_low, expr_low, contract_first, preferred_element_type=F32),
        "cells",
        scatter_dimension=0,
        tiled=True,
    )
    target = spatial[0]
    member_all = (slide_ids[0][:, None] == jnp.arange(2, dtype=jnp.int32)[None, :]).astype(F32)
    first_row = lax.axis_index("cells") * out_rows
    member_rows = lax.dynamic_slice_in_dim(member_all, first_row, out_rows, 0)
    gene_inner = jnp.dot(member_rows.T, predicted * target, precision=highest)
    gene_pred = jnp.dot(member_rows.T, predicted * predicted, precision=highest)
    gene_true = jnp.dot(member_rows.T, target * target, precision=highest)
    spot_inner = jnp.sum(predicted * target, axis=1)
    pred_scale = lax.rsqrt(jnp.sum(predicted * predicted, axis=1) + EPSILON)
    true_scale = lax.rsqrt(jnp.sum(target * target, axis=1) + EPSILON)
    spot_sum = jnp.sum(spot_inner * pred_scale * true_scale)
    counts_real = spot_counts[0].astype(F32)
    exp_mass = jnp.exp(log_mass)
    local_mass = jnp.dot(member_all.T, exp_mass, precision=highest)
    local_count = jnp.dot(member_all.T, counts_real, precision=highest)
    local_clog = jnp.dot(member_all.T, counts_real * jnp.log(counts_real), precision=highest)
    local_clse = jnp.dot(member_all.T, counts_real * log_mass, precision=highest)
    slide_mass, slide_count, count_log, count_lse = lax.psum(
        (local_mass, local_count, local_clog, local_clse), "spots"
    )
    gene_inner, gene_pred, gene_true, spot_total = lax.psum(
        (gene_inner, gene_pred, gene_true, spot_sum), ("cells", "spots")
    )
    gene_a = lax.rsqrt(gene_pred + EPSILON)
    gene_b = lax.rsqrt(gene_true + EPSILON)
    gene_cos = gene_inner * gene_a * gene_b
    total_spots = columns * nspots
    some = slide_count > 0.5
    slide_count = jnp.where(some, slide_count, 1.0)
    slide_mass = jnp.where(some, slide_mass, 1.0)
    kl_value = jnp.sum(
        jnp.where(
            some,
            (count_log - count_lse) / slide_count - jnp.log(slide_count) + jnp.log(slide_mass),
            0.0,
        )
    )
    loss = -jnp.mean(gene_cos) - spot_total / total_spots + kl_value
    gene_step = -1.0 / (2 * genes)
    inner_grad = gene_step * gene_a * gene_b
    square_grad = -0.5 * gene_step * gene_inner * gene_b * gene_a * gene_a * gene_a
    pred_grad = jnp.dot(member_rows, inner_grad, precision=highest) * target
    pred_grad = pred_grad + 2.0 * jnp.dot(member_rows, square_grad, precision=highest) * predicted
    spot_step = -1.0 / total_spots
    pred_grad = pred_grad + (spot_step * pred_scale * true_scale)[:, None] * target
    pred_grad = (
        pred_grad
        - (spot_step * spot_inner * pred_scale * pred_scale * pred_scale * true_scale)[:, None]
        * predicted
    )
    grad_low = pred_grad.astype(BF16)
    mass_grad = exp_mass / jnp.dot(
        member_all, slide_mass, precision=highest
    ) - counts_real / jnp.dot(member_all, slide_count, precision=highest)
    contract_genes = (((1,), (1,)), ((), ()))
    grad_all = lax.all_gather(grad_low, "cells", axis=0, tiled=True)
    expr_part = jnp.dot(weights_low, grad_all, preferred_element_type=F32)
    weight_grad = lax.dot_general(
        expr_low, grad_all, contract_genes, preferred_element_type=F32
    )
    col_inner = lax.psum(jnp.sum(weights * weight_grad, axis=0), "cells")
    logit_grad = weights * (weight_grad - col_inner + mass_grad)
    expr_grad = lax.psum(expr_part, "spots")
    return (predicted[None], loss, logit_grad, expr_grad)


def solution(mesh):
    ncells, nx = mesh.shape["cells"], mesh.shape["spots"]

    def per_device(*args):
        if fits(ncells, nx, *args[:3]):
            return kernel_step(ncells, nx, *args)
        return plain_step(*args)

    return jax.shard_map(
        per_device,
        mesh=mesh,
        in_specs=(
            P("cells", "spots"),
            P("cells", None),
            P("spots", "cells", None),
            P("spots", None),
            P("spots", None),
        ),
        out_specs=(P("spots", "cells", None), P(), P("cells", "spots"), P("cells", None)),
        check_vma=False,
    )
```

```python
import functools

import jax
import jax.numpy as jnp
from jax import lax
from jax.experimental import pallas as pl
from jax.experimental.pallas import tpu as pltpu
from jax.sharding import PartitionSpec as P

EPSILON = 1e-06
MESH = pl.DeviceIdType.MESH
F32 = jnp.float32
BF16 = jnp.bfloat16
YK = 4


def forward_kernel(
    nz,
    nx,
    lg_hbm, ex_hbm, sp_hbm, ids_hbm, cnt_hbm,
    wv, g, eg, lgrad, lgv, vec, p_out, loss_out,
    lgo, et, exv, xl, pf, psib, ysend, yrecv, zsend, zrecv, tgt, prd,
    s_own, s_sib, s_pair, s_y, s_quad, s_z, aux, gtrue, strue, gsum, ssum, st1, st2, ids_ref, cnt_ref,
    loc, snd, rcv,
):
    cells, cols = lgv.shape
    rows, wide = pf.shape[2:]
    part = rows // YK
    c = lax.axis_index("cells")
    x = lax.axis_index("spots")
    z = c // YK
    yk = c % YK
    y = yk // 2
    k = yk % 2
    yo, ko, xo = 1 - y, 1 - k, (x + 1) % nx
    me = x * nz + z
    here, there = pl.ds(x * nz, nz), pl.ds(xo * nz, nz)

    def dev(zz, yy, kk, xx):
        return (zz * YK + yy * 2 + kk, xx)

    sib, yp, dia, xp = dev(z, y, ko, x), dev(z, yo, k, x), dev(z, yo, ko, x), dev(z, y, k, xo)
    yk_peers = ((sib, y * 2 + ko), (yp, yo * 2 + k), (dia, yo * 2 + ko))
    others = [(z + r) % nz for r in range(1, nz)]
    others = others[1:2] + others[:1] + others[2:]
    z_peers = [dev(q, y, k, x) for q in others]
    xz_peers = [dev(q, y, k, xo) for q in others] + z_peers + [xp]

    taken = {"send": 0, "recv": 0, "local": 0}
    kept = {"send": 0, "recv": 0}
    size = {"send": snd.shape[0], "recv": rcv.shape[0]}
    sends, late_sends = [], []

    def sems(kind, n=1):
        taken[kind] += n
        return taken[kind] - n

    def keep(kind):
        kept[kind] += 1
        return size[kind] - kept[kind]

    def put(src, dst, device, send, recv):
        pltpu.make_async_remote_copy(
            src_ref=src, dst_ref=dst, send_sem=snd.at[send], recv_sem=rcv.at[recv],
            device_id=device, device_id_type=MESH,
        ).start()

    def landed(ref, recv):
        pltpu.make_async_remote_copy(
            src_ref=ref, dst_ref=ref, send_sem=snd.at[0], recv_sem=rcv.at[recv],
            device_id=sib, device_id_type=MESH,
        ).wait_recv()

    def left(ref, send):
        pltpu.make_async_remote_copy(
            src_ref=ref, dst_ref=ref, send_sem=snd.at[send], recv_sem=rcv.at[0],
            device_id=sib, device_id_type=MESH,
        ).wait_send()

    def remote(src, dst, device, late=False):
        return spread_to([(src, dst, device)], lambda n: dst, late)

    def spread_to(pairs, size, late=False):
        take = keep if late else sems
        i, j = take("send"), take("recv")
        for src, dst, device in pairs:
            put(src, dst, device, i, j)
        (late_sends if late else sends).append((size(len(pairs)), i))
        return lambda: landed(size(len(pairs)), j)

    def local(src, dst):
        cp = pltpu.make_async_copy(src, dst, loc.at[sems("local")])
        cp.start()
        return cp

    barrier = pltpu.get_barrier_semaphore()
    for d in [p[0] for p in yk_peers] + xz_peers:
        pl.semaphore_signal(barrier, inc=1, device_id=d, device_id_type=MESH)

    def genes_of(ref, b):
        return ref.at[..., pl.ds(pl.multiple_of(b * wide, wide), wide)]

    blocks = (yo * 2 + ko, yo * 2 + k, y * 2 + ko, yk)
    lg_copy = local(lg_hbm, lgv)
    ex_copies = [local(genes_of(ex_hbm, b), exv.at[i]) for i, b in enumerate(blocks)]
    late = [
        local(genes_of(sp_hbm.at[0], yk), tgt.at[yk]),
        local(ids_hbm, ids_ref),
        local(cnt_hbm, cnt_ref),
    ]

    lg_copy.wait()
    piece = 128
    total = jnp.zeros((1, cols), F32)
    total_low = jnp.zeros((1, cols), F32)
    for i in range(cells // piece):
        e = jnp.exp(lgv[pl.ds(i * piece, piece), :].astype(F32))
        low = e.astype(BF16).astype(F32)
        total = total + jnp.sum(e, axis=0, keepdims=True)
        total_low = total_low + jnp.sum(low, axis=0, keepdims=True)
        et[:, pl.ds(i * piece, piece)] = low.T.astype(BF16)
    s_own[0:1, :] = total
    s_own[1:2, :] = total_low

    half = wide // 2

    def forward(i):
        ex_copies[i].wait()
        for n in range(2):
            lanes = pl.ds(n * half, half)
            low = exv[i, :, lanes].astype(BF16)
            xl[blocks[i], :, lanes] = low
            pf[i, :, :, lanes] = jnp.dot(et[...], low, preferred_element_type=F32).reshape(
                nz, rows, half
            )

    cut = rows * 3 // 8
    r1, r2 = pl.ds(0, cut), pl.ds(cut, rows - cut)
    most, more = cells * 13 // 16, cells // 8
    early, gap, last = pl.ds(0, most), pl.ds(most, more), pl.ds(most + more, cells - most - more)

    forward(0)
    pl.semaphore_wait(barrier, len(yk_peers) + len(xz_peers))
    s_sib_in = remote(s_own, s_sib, sib)
    sib_r1 = [remote(pf.at[0, q, r1], psib.at[0, q, r1], sib) for q in others + [z]]
    sib_r2 = remote(pf.at[0, :, r2], psib.at[0, :, r2], sib)
    lg_in = [remote(lg_hbm.at[early], lgo.at[early], xp, late=True)]
    forward(1)
    s_sib_in()
    s_pair[...] = s_own[...] + s_sib[...]
    s_y_in = remote(s_pair, s_y, yp)

    y_send = sems("send")
    y_in = {}

    def send_y(i, r, q):
        if r is r1:
            sib_r1[i]()
        ysend[q, r] = (pf[1, q, r] + psib[0, q, r]).astype(BF16)
        y_in[r.start, i] = sems("recv")
        put(ysend.at[q, r], yrecv.at[q, r], yp, y_send, y_in[r.start, i])

    for i, q in enumerate(others):
        send_y(i, r1, q)
    forward(2)
    sib_rest = remote(pf.at[2], psib.at[1], sib)
    forward(3)
    sib_r2()
    for i, q in enumerate(others):
        send_y(i, r2, q)
    t_in = spread_to(
        [(genes_of(sp_hbm.at[0], b), tgt.at[yk], d) for d, b in yk_peers],
        lambda n: tgt.at[pl.ds(0, n)],
    )
    send_y(nz - 1, r1, z)
    send_y(nz - 1, r2, z)
    sends.append((ysend, y_send))

    s_y_in()
    s_quad[...] = s_pair[...] + s_y[...]
    s_z[z] = s_quad[...]
    s_z_in = spread_to(
        [(s_quad, s_z.at[z], d) for d in z_peers], lambda n: s_z.at[pl.ds(0, n)]
    )

    z_send, z_recv = sems("send"), sems("recv")

    def add_y(i, r, q):
        landed(yrecv.at[q, r], y_in[r.start, i])
        return pf[3, q, r] + psib[1, q, r] + yrecv[q, r].astype(F32)

    sib_rest()
    for r in (r1, r2):
        for i, q in enumerate(others):
            zsend[q, r] = add_y(i, r, q).astype(BF16)
            put(zsend.at[q, r], zrecv.at[z, r], z_peers[i], z_send, z_recv)
    sends.append((zsend.at[pl.ds(0, nz - 1)], z_send))

    for cp in late:
        cp.wait()
    t_in()
    eye = lax.broadcasted_iota(jnp.int32, (rows, rows), 0) == lax.broadcasted_iota(
        jnp.int32, (rows, rows), 1
    )

    def to_col(v):
        return jnp.sum(jnp.where(eye, jnp.broadcast_to(v, (rows, rows)), 0.0), axis=1, keepdims=True)

    def to_row(v):
        return jnp.sum(jnp.where(eye, jnp.broadcast_to(v, (rows, rows)), 0.0), axis=0, keepdims=True)

    mine_cols = pl.ds(pl.multiple_of(z * rows, rows), rows)
    slide = to_col(ids_ref[:, mine_cols].astype(F32))
    second = jnp.broadcast_to(slide > 0.5, (rows, wide))

    def by_slide(v):
        a = jnp.sum(jnp.where(second, 0.0, v), axis=0, keepdims=True)
        b = jnp.sum(jnp.where(second, v, 0.0), axis=0, keepdims=True)
        return a, b

    target = tgt[...].reshape(rows, wide)
    square = target * target
    for s, v in enumerate(by_slide(square)):
        gtrue[me, s : s + 1, :] = v
    strue[yk] = to_row(jnp.sum(square, axis=1, keepdims=True))

    def share(by_gene, by_spot):
        a = spread_to(
            [(by_gene.at[me], by_gene.at[me], d) for d in xz_peers], lambda n: by_gene.at[pl.ds(0, n)], late=True
        )
        b = spread_to(
            [(by_spot.at[yk], by_spot.at[yk], d) for d, _ in yk_peers],
            lambda n: by_spot.at[pl.ds(0, n)],
            late=True,
        )
        return a, b

    true_in = share(gtrue, strue)

    own_1 = add_y(nz - 1, r1, z)
    own_2 = add_y(nz - 1, r2, z)

    s_z_in()
    whole_sum = s_z[0]
    for q in range(1, nz):
        whole_sum = whole_sum + s_z[q]
    mass = whole_sum[0:1, :]
    inv_mass = 1.0 / mass
    slides = ids_ref[...].astype(F32)
    counts = cnt_ref[...].astype(F32)
    aux[x, 0:1, :] = mass
    aux[x, 1:2, :] = slides
    aux[x, 2:3, :] = counts
    aux[x, 3:4, :] = jnp.zeros((1, cols), F32)
    aux_in = remote(aux.at[x], aux.at[x], xp, late=True)
    low_sum = s_z[0, 1:2, mine_cols]
    for q in range(1, nz):
        low_sum = low_sum + s_z[q, 1:2, mine_cols]
    inv_low = 1.0 / to_col(low_sum)

    landed(zrecv.at[pl.ds(0, nz - 1)], z_recv)
    pred = jnp.concatenate([own_1, own_2], axis=0)
    for q in others:
        pred = pred + zrecv[q].astype(F32)
    pred = pred * inv_low
    both = pred * target
    pair = pred * pred
    for r, v in enumerate((both, pair)):
        for s, w in enumerate(by_slide(v)):
            gsum[me, 2 * r + s : 2 * r + s + 1, :] = w
        ssum[yk, r : r + 1, :] = to_row(jnp.sum(v, axis=1, keepdims=True))
    sum_in = share(gsum, ssum)
    lg_in.append(remote(lg_hbm.at[gap], lgo.at[gap], xp, late=True))
    prd[...] = pred.reshape(YK, part, wide)
    p_in = spread_to(
        [(prd.at[b], p_out.at[yk], d) for d, b in yk_peers], lambda n: p_out.at[pl.ds(0, n)], late=True
    )
    p_out[yk] = prd[yk]

    def weights(src, scale, to):
        for i in range(cells // piece):
            r = pl.ds(i * piece, piece)
            wv[to, r, :] = (jnp.exp(src[r, :].astype(F32)) * scale).astype(BF16)

    weights(lgv, inv_mass, x)
    for wait in true_in + sum_in:
        wait()
    for ref, i in sends:
        left(ref, i)
    used = dict(taken)
    taken.update(send=0, recv=0)
    sends.clear()

    def added(ref, n):
        v = ref[0]
        for q in range(1, n):
            v = v + ref[q]
        return v

    genes = YK * wide
    spots = nx * cols
    gene_step = -1.0 / (2 * genes)
    spot_step = -1.0 / spots
    gs = added(gsum, nx * nz)
    gene_a = lax.rsqrt(gs[2:4] + EPSILON)
    gene_b = lax.rsqrt(added(gtrue, nx * nz) + EPSILON)
    gene_cos = gs[0:2] * gene_a * gene_b
    t_gene = gene_step * gene_a * gene_b
    p_gene = -gene_step * gs[0:2] * gene_b * gene_a * gene_a * gene_a
    ss = added(ssum, YK)
    pred_scale = lax.rsqrt(ss[1:2] + EPSILON)
    true_scale = lax.rsqrt(added(strue, YK) + EPSILON)
    spot_cos = ss[0:1] * pred_scale * true_scale
    t_spot = to_col(spot_step * pred_scale * true_scale)
    p_spot = to_col(-spot_step * ss[0:1] * pred_scale * pred_scale * pred_scale * true_scale)

    def of_slide(v):
        return jnp.where(
            second, jnp.broadcast_to(v[1:2], (rows, wide)), jnp.broadcast_to(v[0:1], (rows, wide))
        )

    grad = (of_slide(t_gene) + t_spot) * target + (of_slide(p_gene) + p_spot) * pred
    low = grad.astype(BF16)
    g[me, y, k] = low

    part_a, part_b, part_c = pl.ds(0, cut), pl.ds(cut, cut), pl.ds(2 * cut, rows - 2 * cut)
    part_ab = pl.ds(0, 2 * cut)
    z_out, c_out = sems("send"), sems("send")
    y_out, x_out, cy_out, cx_out, cd_out, a_out, b_out, core_out = (sems("send") for _ in range(8))
    from_z, from_y, from_x = (sems("recv", 2 * nz) for _ in range(3))
    from_a, from_b = (sems("recv", nz) for _ in range(2))
    cy_in, cx_in, cd_in = (sems("recv") for _ in range(3))
    from_c, core_in = sems("recv", 4 * nz), sems("recv", 4)
    kinds = ((x, y, 0), (xo, y, 2), (x, yo, 1), (xo, yo, 3))

    def to_core(shard, region):
        put(shard, shard, sib, core_out, core_in + region)

    def pass_on(shard, upward, send, recv):
        @pl.when(z < nz - 1 if upward else z > 0)
        def _():
            put(shard, shard, dev(z + 1 if upward else z - 1, y, k, x), send, recv)

    at_end = (z == 0) | (z == nz - 1)

    def own_z():
        for h, r in enumerate((part_a, part_b)):
            shard = g.at[me, y, k, r]
            pass_on(shard, True, z_out, from_z + 2 * z + h)
            pass_on(shard, False, z_out, from_z + 2 * z + h)

        @pl.when(at_end)
        def _():
            for h, r in enumerate((part_a, part_b)):
                shard = g.at[me, y, k, r]
                put(shard, shard, dev(nz - 1 - z, y, k, x), z_out, from_z + 2 * z + h)

    def own_c():
        shard = g.at[me, y, k, part_c]
        put(shard, shard, yp, cy_out, cy_in)
        put(shard, shard, xp, cx_out, cx_in)

    def own_y():
        for h, r in enumerate((part_a, part_b)):
            shard = g.at[me, y, k, r]
            put(shard, shard, yp, y_out, from_y + 2 * z + h)

    def own_x():
        for h, r in ((1, part_b), (0, part_a)):
            shard = g.at[me, y, k, r]
            put(shard, shard, xp, x_out, from_x + 2 * z + h)

    def own_core():
        to_core(g.at[me, y, k], 0)

    def start_c(kind):
        plane, yy, _ = kinds[kind]
        shard = g.at[plane * nz + z, yy, k, part_c]
        pass_on(shard, True, c_out, from_c + 4 * z + kind)
        pass_on(shard, False, c_out, from_c + 4 * z + kind)

        @pl.when(at_end)
        def _():
            put(shard, shard, dev(nz - 1 - z, y, k, x), c_out, from_c + 4 * z + kind)

    def wait_cy():
        shard = g.at[me, yo, k, part_c]
        landed(shard, cy_in)
        put(shard, shard, xp, cd_out, cd_in)
        to_core(shard, 1)

    def wait_cx():
        shard = g.at[xo * nz + z, y, k, part_c]
        landed(shard, cx_in)
        to_core(shard, 2)

    def wait_cd():
        shard = g.at[xo * nz + z, yo, k, part_c]
        landed(shard, cd_in)
        to_core(shard, 3)

    def at_distance(d, act):
        if d == 0:
            act(z, False)
            return

        @pl.when(z >= d)
        def _():
            act(z - d, False)

        @pl.when(z < nz - d)
        def _():
            act(z + d, True)

    def take_z(q, above, further=False):
        for h, r in enumerate((part_a, part_b)):
            shard = g.at[x * nz + q, y, k, r]
            landed(shard, from_z + 2 * q + h)
            if further:
                pass_on(shard, not above, z_out, from_z + 2 * q + h)
            put(shard, shard, yp, y_out, from_y + 2 * q + h)
            put(shard, shard, xp, x_out, from_x + 2 * q + h)
            to_core(shard, 0)

    def take_c(kind, further=False):
        def act(q, above):
            plane, yy, region = kinds[kind]
            shard = g.at[plane * nz + q, yy, k, part_c]
            landed(shard, from_c + 4 * q + kind)
            if further:
                pass_on(shard, not above, c_out, from_c + 4 * q + kind)
            to_core(shard, region)

        return act

    def take_y(q, above):
        for h, r in enumerate((part_a, part_b)):
            shard = g.at[x * nz + q, yo, k, r]
            landed(shard, from_y + 2 * q + h)
            if h == 0:
                put(shard, shard, xp, a_out, from_a + q)
            to_core(shard, 1)

    def take_x(q, above):
        for h, r in ((1, part_b), (0, part_a)):
            shard = g.at[xo * nz + q, y, k, r]
            landed(shard, from_x + 2 * q + h)
            if h == 1:
                put(shard, shard, yp, b_out, from_b + q)
            to_core(shard, 2)

    def take_d(q, above):
        for recv, r in ((from_a, part_a), (from_b, part_b)):
            shard = g.at[xo * nz + q, yo, k, r]
            landed(shard, recv + q)
            to_core(shard, 3)

    def grad_of(plane, yy, kk):
        return g[plane, yy, kk].reshape(cols, wide)

    def weight_term(yy, kk):
        return lax.dot_general(
            xl[yy * 2 + kk], grad_of(here, yy, kk), (((1,), (1,)), ((), ())), preferred_element_type=F32
        )

    def expr_term(q, plane, yy, kk):
        return jnp.dot(wv[q], grad_of(plane, yy, kk), preferred_element_type=F32)

    lane = lax.broadcasted_iota(jnp.int32, (1, rows), 1)

    own_x()
    own_z()
    own_c()
    own_y()
    lg_in.append(remote(lg_hbm.at[last], lgo.at[last], xp, late=True))
    st1[yk, 0:1, :] = to_row(jnp.sum(low.astype(F32) * pred, axis=1, keepdims=True))
    st1[yk, 1:2, :] = jnp.where(lane == 0, jnp.sum(gene_cos), 0.0)
    st1_in = spread_to([(st1.at[yk], st1.at[yk], d) for d, _ in yk_peers], lambda n: st1.at[pl.ds(0, n)])
    start_c(0)
    take_x(z, False)
    wait_cy()
    at_distance(1, functools.partial(take_z, further=True))
    wait_cx()
    at_distance(3, take_z)
    start_c(2)
    at_distance(1, take_c(0, True))
    at_distance(2, take_z)
    start_c(1)
    own_core()
    take_y(z, False)
    wait_cd()
    aux_in()
    for wait in lg_in:
        wait()
    weights(lgo, 1.0 / aux[xo, 0:1, :], xo)
    start_c(3)
    at_distance(3, take_y)
    at_distance(1, take_c(2, True))
    at_distance(3, take_x)
    at_distance(1, take_y)
    at_distance(2, take_c(0))
    at_distance(3, take_c(0))
    st1_in()
    whole = added(st1, YK)
    st2[me, 0:1, :] = whole[0:1]
    st2[me, 1:2, :] = jnp.where(lane == 0, whole[1:2], jnp.where(lane == 1, jnp.sum(spot_cos), 0.0))
    st2_in = spread_to([(st2.at[me], st2.at[me], d) for d in xz_peers], lambda n: st2.at[pl.ds(0, n)])
    eg[y, k] = expr_term(x, here, y, k)
    at_distance(1, take_x)
    lgrad[...] = weight_term(y, k)
    at_distance(2, take_y)
    at_distance(3, take_c(2))
    landed(g.at[here, y, ko], core_in)
    eg[y, ko] = expr_term(x, here, y, ko)
    at_distance(1, take_c(1, True))
    at_distance(1, take_c(3, True))
    at_distance(2, take_x)
    lgrad[...] += weight_term(y, ko)
    at_distance(2, take_c(2))
    take_d(z, False)
    eg[yo, k] = expr_term(x, here, yo, k)
    lgrad[...] += weight_term(yo, k)
    at_distance(3, take_c(3))
    at_distance(3, take_c(1))
    at_distance(1, take_d)
    landed(g.at[here, yo, ko], core_in + 1)
    lgrad[...] += weight_term(yo, ko)
    at_distance(3, take_d)
    at_distance(2, take_c(1))
    at_distance(2, take_c(3))
    at_distance(2, take_d)
    eg[y, k] += expr_term(xo, there, y, k)

    kl = 0.0
    slide_mass, slide_count = [], []
    for s in range(2):
        m = n = cl = cm = 0.0
        for q in range(nx):
            of_s = jnp.abs(aux[q, 1:2, :] - s) < 0.5
            n_q = jnp.where(of_s, aux[q, 2:3, :], 0.0)
            m = m + jnp.sum(jnp.where(of_s, aux[q, 0:1, :], 0.0))
            n = n + jnp.sum(n_q)
            cl = cl + jnp.sum(n_q * jnp.log(aux[q, 2:3, :]))
            cm = cm + jnp.sum(n_q * jnp.log(aux[q, 0:1, :]))
        some = n > 0.5
        m = jnp.full((1, 128), jnp.where(some, m, 1.0), F32)
        n = jnp.full((1, 128), jnp.where(some, n, 1.0), F32)
        kl = kl + jnp.where(some, (cl - cm) / n - jnp.log(n) + jnp.log(m), 0.0)
        slide_mass.append(m[:, 0:1])
        slide_count.append(n[:, 0:1])
    is_second = slides > 0.5
    mass_grad = mass / jnp.where(is_second, slide_mass[1], slide_mass[0]) - counts / jnp.where(
        is_second, slide_count[1], slide_count[0]
    )
    st2_in()
    gene_total = whole[1:2]
    spot_total = added(st2, nx * nz)[1:2]
    loss_out[...] = (
        -jnp.sum(jnp.where(lane == 0, gene_total, 0.0)) / (2 * genes)
        - jnp.sum(jnp.where(lane == 1, spot_total, 0.0)) / spots
        + kl
    )
    vec[0:1, :] = inv_mass
    vec[1:2, :] = mass_grad - jnp.concatenate([st2[x * nz + q, 0:1, :] for q in range(nz)], axis=1)

    p_in()
    landed(g.at[there, y, ko], core_in + 2)
    landed(g.at[there, yo, ko], core_in + 3)
    for ref, i in sends + late_sends:
        left(ref, i)
    left(g.at[here, y, k, part_ab], y_out)
    left(g.at[here, y, k, part_ab], x_out)
    for i in (cy_out, cx_out, cd_out):
        left(g.at[me, y, k, part_c], i)
    left(g.at[here, yo, k, part_a], a_out)
    left(g.at[there, y, k, part_b], b_out)
    left(g.at[:, :, k], core_out)

    @pl.when(at_end)
    def _():
        left(g.at[pl.ds(0, 2), y, k, part_ab], z_out)
        left(g.at[pl.ds(0, 8), y, k, part_c], c_out)

    @pl.when(jnp.logical_not(at_end))
    def _():
        left(g.at[pl.ds(0, nz), y, k, part_ab], z_out)
        left(g.at[pl.ds(0, nz), y, k], c_out)

    needed = {kind: max(used[kind], taken[kind]) + kept[kind] for kind in kept}
    assert needed == size, needed


def backward_kernel(
    nz, w_ref, g_ref, part_ref, lgrad_ref, lg_ref, vec_ref, p_ref, loss_ref,
    eg_hbm, lgrad_hbm, pred_ref, total_ref, eg, lgrad, done,
):
    c = lax.axis_index("cells")
    x = lax.axis_index("spots")
    y, k = (c % YK) // 2, c % 2
    nx, cells, cols = w_ref.shape
    wide = g_ref.shape[4]
    tall = cells // 2
    xo = (x + 1) % nx
    copies = []

    def out(src, dst):
        cp = pltpu.make_async_copy(src, dst, done.at[len(copies)])
        cp.start()
        copies.append(cp)

    def genes_at(yy, kk):
        return eg_hbm.at[:, pl.ds(pl.multiple_of((yy * 2 + kk) * wide, wide), wide)]

    def term(q, yy, kk, r):
        block = g_ref[pl.ds(q * nz, nz), yy, kk].reshape(cols, wide)
        return jnp.dot(w_ref[q, r, :], block, preferred_element_type=F32)

    out(part_ref.at[y, k], genes_at(y, k))
    lgrad[...] = jnp.exp(lg_ref[...].astype(F32)) * vec_ref[0:1, :] * (lgrad_ref[...] + vec_ref[1:2, :])
    out(lgrad, lgrad_hbm)
    for i, (yy, kk) in enumerate(((y, 1 - k), (1 - y, k), (1 - y, 1 - k))):
        for n in range(2):
            r = pl.ds(n * tall, tall)
            mine = part_ref[yy, kk, r, :] if i < 2 else term(x, yy, kk, r)
            eg[i, r, :] = mine + term(xo, yy, kk, r)
            out(eg.at[i, r], genes_at(yy, kk).at[r])
    for b in range(YK):
        out(p_ref.at[b], pred_ref.at[:, b * wide : (b + 1) * wide])
    total_ref[...] = loss_ref[:, 0:1]
    for cp in copies:
        cp.wait()


def step(ncells, nx, logits, expression, spatial, slide_ids, spot_counts):
    cells, cols = logits.shape
    genes = expression.shape[1]
    nz = ncells // YK
    rows = cols // nz
    wide = genes // YK
    part = rows // YK
    half = wide // 2
    anywhere = pl.BlockSpec(memory_space=pl.ANY)
    whole = pl.BlockSpec(memory_space=pltpu.VMEM)
    *held, p, loss = pl.pallas_call(
        functools.partial(forward_kernel, nz, nx),
        out_shape=(
            pltpu.VMEM((nx, cells, cols), BF16),
            pltpu.VMEM((nx * nz, 2, 2, rows, wide), BF16),
            pltpu.VMEM((2, 2, cells, wide), F32),
            pltpu.VMEM((cells, cols), F32),
            pltpu.VMEM((cells, cols), BF16),
            pltpu.VMEM((2, cols), F32),
            pltpu.VMEM((YK, part, wide), F32),
            pltpu.VMEM((1, 128), F32),
        ),
        in_specs=[anywhere] * 5,
        out_specs=(whole,) * 8,
        scratch_shapes=[
            pltpu.VMEM((cells, cols), BF16),
            pltpu.VMEM((cols, cells), BF16),
            pltpu.VMEM((YK, cells, wide), F32),
            pltpu.VMEM((YK, cells, wide), BF16),
            pltpu.VMEM((YK, nz, rows, wide), F32),
            pltpu.VMEM((2, nz, rows, wide), F32),
            pltpu.VMEM((nz, rows, wide), BF16),
            pltpu.VMEM((nz, rows, wide), BF16),
            pltpu.VMEM((nz, rows, wide), BF16),
            pltpu.VMEM((nz, rows, wide), BF16),
            pltpu.VMEM((YK, part, wide), F32),
            pltpu.VMEM((YK, part, wide), F32),
            pltpu.VMEM((2, cols), F32),
            pltpu.VMEM((2, cols), F32),
            pltpu.VMEM((2, cols), F32),
            pltpu.VMEM((2, cols), F32),
            pltpu.VMEM((2, cols), F32),
            pltpu.VMEM((nz, 2, cols), F32),
            pltpu.VMEM((nx, 4, cols), F32),
            pltpu.VMEM((nx * nz, 2, wide), F32),
            pltpu.VMEM((YK, 1, rows), F32),
            pltpu.VMEM((nx * nz, 4, wide), F32),
            pltpu.VMEM((YK, 2, rows), F32),
            pltpu.VMEM((YK, 2, rows), F32),
            pltpu.VMEM((nx * nz, 2, rows), F32),
            pltpu.VMEM((1, cols), jnp.int32),
            pltpu.VMEM((1, cols), jnp.int32),
            pltpu.SemaphoreType.DMA((8,)),
            pltpu.SemaphoreType.DMA((21,)),
            pltpu.SemaphoreType.DMA((18 + 12 * nz,)),
        ],
        compiler_params=pltpu.CompilerParams(
            collective_id=0, has_side_effects=True, vmem_limit_bytes=36 << 20
        ),
        name="forward_and_gather",
    )(
        *(
            pltpu.with_memory_space_constraint(v, pltpu.HBM)
            for v in (logits, expression, spatial, slide_ids, spot_counts)
        )
    )

    held = [pltpu.with_memory_space_constraint(v, pltpu.VMEM) for v in held]
    return pl.pallas_call(
        functools.partial(backward_kernel, nz),
        out_shape=(
            jax.ShapeDtypeStruct((cells, genes), F32),
            jax.ShapeDtypeStruct((cells, cols), F32),
            jax.ShapeDtypeStruct((part, genes), F32),
            jax.ShapeDtypeStruct((1, 1), F32),
        ),
        in_specs=[whole] * 8,
        out_specs=(anywhere, anywhere, anywhere, whole),
        scratch_shapes=[
            pltpu.VMEM((3, cells, wide), F32),
            pltpu.VMEM((cells, cols), F32),
            pltpu.SemaphoreType.DMA((12,)),
        ],
        compiler_params=pltpu.CompilerParams(vmem_limit_bytes=24 << 20),
        name="backward",
    )(*held, p, loss)


def kernel_step(ncells, nx, *args):
    grad_expr, grad_logits, predicted, loss = step(ncells, nx, *args)
    return (predicted[None], loss[0, 0], grad_logits, grad_expr)


def fits(ncells, nx, logits, expression, spatial):
    cells, cols = logits.shape
    genes = expression.shape[1]
    if ncells != 4 * YK or nx != 2 or cols % (ncells // YK) or genes % (YK * 256):
        return False
    rows = cols // (ncells // YK)
    held = (cells + rows) * genes * 8 + cells * cols * 16 + cols * genes * 16
    return rows % 128 == 0 and cells % 128 == 0 and held < 50 << 20


def plain_step(logits, expression, spatial, slide_ids, spot_counts):
    highest = lax.Precision.HIGHEST
    ncells = lax.axis_size("cells")
    nspots = lax.axis_size("spots")
    columns = logits.shape[1]
    genes = expression.shape[1]
    out_rows = columns // ncells
    scores = logits.astype(F32)
    col_peak = lax.pmax(jnp.max(scores, axis=0), "cells")
    shifted = jnp.exp(scores - col_peak)
    col_total = lax.psum(jnp.sum(shifted, axis=0), "cells")
    weights = shifted / col_total
    log_mass = col_peak + jnp.log(col_total)
    weights_low = weights.astype(BF16)
    expr_low = expression.astype(BF16)
    contract_first = (((0,), (0,)), ((), ()))
    predicted = lax.psum_scatter(
        lax.dot_general(weights_low, expr_low, contract_first, preferred_element_type=F32),
        "cells",
        scatter_dimension=0,
        tiled=True,
    )
    target = spatial[0]
    member_all = (slide_ids[0][:, None] == jnp.arange(2, dtype=jnp.int32)[None, :]).astype(F32)
    first_row = lax.axis_index("cells") * out_rows
    member_rows = lax.dynamic_slice_in_dim(member_all, first_row, out_rows, 0)
    gene_inner = jnp.dot(member_rows.T, predicted * target, precision=highest)
    gene_pred = jnp.dot(member_rows.T, predicted * predicted, precision=highest)
    gene_true = jnp.dot(member_rows.T, target * target, precision=highest)
    spot_inner = jnp.sum(predicted * target, axis=1)
    pred_scale = lax.rsqrt(jnp.sum(predicted * predicted, axis=1) + EPSILON)
    true_scale = lax.rsqrt(jnp.sum(target * target, axis=1) + EPSILON)
    spot_sum = jnp.sum(spot_inner * pred_scale * true_scale)
    counts_real = spot_counts[0].astype(F32)
    exp_mass = jnp.exp(log_mass)
    local_mass = jnp.dot(member_all.T, exp_mass, precision=highest)
    local_count = jnp.dot(member_all.T, counts_real, precision=highest)
    local_clog = jnp.dot(member_all.T, counts_real * jnp.log(counts_real), precision=highest)
    local_clse = jnp.dot(member_all.T, counts_real * log_mass, precision=highest)
    slide_mass, slide_count, count_log, count_lse = lax.psum(
        (local_mass, local_count, local_clog, local_clse), "spots"
    )
    gene_inner, gene_pred, gene_true, spot_total = lax.psum(
        (gene_inner, gene_pred, gene_true, spot_sum), ("cells", "spots")
    )
    gene_a = lax.rsqrt(gene_pred + EPSILON)
    gene_b = lax.rsqrt(gene_true + EPSILON)
    gene_cos = gene_inner * gene_a * gene_b
    total_spots = columns * nspots
    some = slide_count > 0.5
    slide_count = jnp.where(some, slide_count, 1.0)
    slide_mass = jnp.where(some, slide_mass, 1.0)
    kl_value = jnp.sum(
        jnp.where(
            some,
            (count_log - count_lse) / slide_count - jnp.log(slide_count) + jnp.log(slide_mass),
            0.0,
        )
    )
    loss = -jnp.mean(gene_cos) - spot_total / total_spots + kl_value
    gene_step = -1.0 / (2 * genes)
    inner_grad = gene_step * gene_a * gene_b
    square_grad = -0.5 * gene_step * gene_inner * gene_b * gene_a * gene_a * gene_a
    pred_grad = jnp.dot(member_rows, inner_grad, precision=highest) * target
    pred_grad = pred_grad + 2.0 * jnp.dot(member_rows, square_grad, precision=highest) * predicted
    spot_step = -1.0 / total_spots
    pred_grad = pred_grad + (spot_step * pred_scale * true_scale)[:, None] * target
    pred_grad = (
        pred_grad
        - (spot_step * spot_inner * pred_scale * pred_scale * pred_scale * true_scale)[:, None]
        * predicted
    )
    grad_low = pred_grad.astype(BF16)
    mass_grad = exp_mass / jnp.dot(
        member_all, slide_mass, precision=highest
    ) - counts_real / jnp.dot(member_all, slide_count, precision=highest)
    contract_genes = (((1,), (1,)), ((), ()))
    grad_all = lax.all_gather(grad_low, "cells", axis=0, tiled=True)
    expr_part = jnp.dot(weights_low, grad_all, preferred_element_type=F32)
    weight_grad = lax.dot_general(
        expr_low, grad_all, contract_genes, preferred_element_type=F32
    )
    col_inner = lax.psum(jnp.sum(weights * weight_grad, axis=0), "cells")
    logit_grad = weights * (weight_grad - col_inner + mass_grad)
    expr_grad = lax.psum(expr_part, "spots")
    return (predicted[None], loss, logit_grad, expr_grad)


def solution(mesh):
    ncells, nx = mesh.shape["cells"], mesh.shape["spots"]

    def per_device(*args):
        if fits(ncells, nx, *args[:3]):
            return kernel_step(ncells, nx, *args)
        return plain_step(*args)

    return jax.shard_map(
        per_device,
        mesh=mesh,
        in_specs=(
            P("cells", "spots"),
            P("cells", None),
            P("spots", "cells", None),
            P("spots", None),
            P("spots", None),
        ),
        out_specs=(P("spots", "cells", None), P(), P("cells", "spots"), P("cells", None)),
        check_vma=False,
    )
```

```python
import functools

import jax
import jax.numpy as jnp
from jax import lax
from jax.experimental import pallas as pl
from jax.experimental.pallas import tpu as pltpu
from jax.sharding import PartitionSpec as P

EPSILON = 1e-06
MESH = pl.DeviceIdType.MESH
F32 = jnp.float32
BF16 = jnp.bfloat16
YK = 4


def forward_kernel(
    nz,
    nx,
    lg_hbm, ex_hbm, sp_hbm, ids_hbm, cnt_hbm,
    wv, g, eg, lgrad, lgv, vec, p_out, loss_out,
    lgo, et, exv, xl, pf, psib, ysend, yrecv, zsend, zrecv, tgt, prd,
    s_own, s_sib, s_pair, s_y, s_quad, s_z, aux, gtrue, strue, gsum, ssum, st1, st2, ids_ref, cnt_ref,
    loc, snd, rcv,
):
    cells, cols = lgv.shape
    rows, wide = pf.shape[2:]
    part = rows // YK
    c = lax.axis_index("cells")
    x = lax.axis_index("spots")
    z = c // YK
    yk = c % YK
    y = yk // 2
    k = yk % 2
    yo, ko, xo = 1 - y, 1 - k, (x + 1) % nx
    me = x * nz + z
    here, there = pl.ds(x * nz, nz), pl.ds(xo * nz, nz)

    def dev(zz, yy, kk, xx):
        return (zz * YK + yy * 2 + kk, xx)

    sib, yp, dia, xp = dev(z, y, ko, x), dev(z, yo, k, x), dev(z, yo, ko, x), dev(z, y, k, xo)
    yk_peers = ((sib, y * 2 + ko), (yp, yo * 2 + k), (dia, yo * 2 + ko))
    others = [(z + r) % nz for r in range(1, nz)]
    others = others[1:2] + others[:1] + others[2:]
    z_peers = [dev(q, y, k, x) for q in others]
    xz_peers = [dev(q, y, k, xo) for q in others] + z_peers + [xp]

    taken = {"send": 0, "recv": 0, "local": 0}
    kept = {"send": 0, "recv": 0}
    size = {"send": snd.shape[0], "recv": rcv.shape[0]}
    sends, late_sends = [], []

    def sems(kind, n=1):
        taken[kind] += n
        return taken[kind] - n

    def keep(kind):
        kept[kind] += 1
        return size[kind] - kept[kind]

    def put(src, dst, device, send, recv):
        pltpu.make_async_remote_copy(
            src_ref=src, dst_ref=dst, send_sem=snd.at[send], recv_sem=rcv.at[recv],
            device_id=device, device_id_type=MESH,
        ).start()

    def landed(ref, recv):
        pltpu.make_async_remote_copy(
            src_ref=ref, dst_ref=ref, send_sem=snd.at[0], recv_sem=rcv.at[recv],
            device_id=sib, device_id_type=MESH,
        ).wait_recv()

    def left(ref, send):
        pltpu.make_async_remote_copy(
            src_ref=ref, dst_ref=ref, send_sem=snd.at[send], recv_sem=rcv.at[0],
            device_id=sib, device_id_type=MESH,
        ).wait_send()

    def remote(src, dst, device, late=False):
        return spread_to([(src, dst, device)], lambda n: dst, late)

    def spread_to(pairs, size, late=False):
        take = keep if late else sems
        i, j = take("send"), take("recv")
        for src, dst, device in pairs:
            put(src, dst, device, i, j)
        (late_sends if late else sends).append((size(len(pairs)), i))
        return lambda: landed(size(len(pairs)), j)

    def local(src, dst):
        cp = pltpu.make_async_copy(src, dst, loc.at[sems("local")])
        cp.start()
        return cp

    barrier = pltpu.get_barrier_semaphore()
    for d in [p[0] for p in yk_peers] + xz_peers:
        pl.semaphore_signal(barrier, inc=1, device_id=d, device_id_type=MESH)

    def genes_of(ref, b):
        return ref.at[..., pl.ds(pl.multiple_of(b * wide, wide), wide)]

    blocks = (yo * 2 + ko, yo * 2 + k, y * 2 + ko, yk)
    lg_copy = local(lg_hbm, lgv)
    ex_copies = [local(genes_of(ex_hbm, b), exv.at[i]) for i, b in enumerate(blocks)]
    late = [
        local(genes_of(sp_hbm.at[0], yk), tgt.at[yk]),
        local(ids_hbm, ids_ref),
        local(cnt_hbm, cnt_ref),
    ]

    lg_copy.wait()
    piece = 128
    total = jnp.zeros((1, cols), F32)
    total_low = jnp.zeros((1, cols), F32)
    for i in range(cells // piece):
        e = jnp.exp(lgv[pl.ds(i * piece, piece), :].astype(F32))
        low = e.astype(BF16).astype(F32)
        total = total + jnp.sum(e, axis=0, keepdims=True)
        total_low = total_low + jnp.sum(low, axis=0, keepdims=True)
        et[:, pl.ds(i * piece, piece)] = low.T.astype(BF16)
    s_own[0:1, :] = total
    s_own[1:2, :] = total_low

    half = wide // 2

    def forward(i):
        ex_copies[i].wait()
        for n in range(2):
            lanes = pl.ds(n * half, half)
            low = exv[i, :, lanes].astype(BF16)
            xl[blocks[i], :, lanes] = low
            pf[i, :, :, lanes] = jnp.dot(et[...], low, preferred_element_type=F32).reshape(
                nz, rows, half
            )

    cut = rows * 3 // 8
    r1, r2 = pl.ds(0, cut), pl.ds(cut, rows - cut)
    most, more = cells * 13 // 16, cells // 8
    early, gap, last = pl.ds(0, most), pl.ds(most, more), pl.ds(most + more, cells - most - more)

    forward(0)
    pl.semaphore_wait(barrier, len(yk_peers) + len(xz_peers))
    s_sib_in = remote(s_own, s_sib, sib)
    sib_r1 = [remote(pf.at[0, q, r1], psib.at[0, q, r1], sib) for q in others + [z]]
    sib_r2 = remote(pf.at[0, :, r2], psib.at[0, :, r2], sib)
    lg_in = [remote(lg_hbm.at[early], lgo.at[early], xp, late=True)]
    forward(1)
    s_sib_in()
    s_pair[...] = s_own[...] + s_sib[...]
    s_y_in = remote(s_pair, s_y, yp)

    y_send = sems("send")
    y_in = {}

    def send_y(i, r, q):
        if r is r1:
            sib_r1[i]()
        ysend[q, r] = (pf[1, q, r] + psib[0, q, r]).astype(BF16)
        y_in[r.start, i] = sems("recv")
        put(ysend.at[q, r], yrecv.at[q, r], yp, y_send, y_in[r.start, i])

    for i, q in enumerate(others):
        send_y(i, r1, q)
    forward(2)
    sib_rest = remote(pf.at[2], psib.at[1], sib)
    forward(3)
    sib_r2()
    for i, q in enumerate(others):
        send_y(i, r2, q)
    t_in = spread_to(
        [(genes_of(sp_hbm.at[0], b), tgt.at[yk], d) for d, b in yk_peers],
        lambda n: tgt.at[pl.ds(0, n)],
    )
    send_y(nz - 1, r1, z)
    send_y(nz - 1, r2, z)
    sends.append((ysend, y_send))

    s_y_in()
    s_quad[...] = s_pair[...] + s_y[...]
    s_z[z] = s_quad[...]
    s_z_in = spread_to(
        [(s_quad, s_z.at[z], d) for d in z_peers], lambda n: s_z.at[pl.ds(0, n)]
    )

    z_send, z_recv = sems("send"), sems("recv")

    def add_y(i, r, q):
        landed(yrecv.at[q, r], y_in[r.start, i])
        return pf[3, q, r] + psib[1, q, r] + yrecv[q, r].astype(F32)

    sib_rest()
    for r in (r1, r2):
        for i, q in enumerate(others):
            zsend[q, r] = add_y(i, r, q).astype(BF16)
            put(zsend.at[q, r], zrecv.at[z, r], z_peers[i], z_send, z_recv)
    sends.append((zsend.at[pl.ds(0, nz - 1)], z_send))

    for cp in late:
        cp.wait()
    t_in()
    eye = lax.broadcasted_iota(jnp.int32, (rows, rows), 0) == lax.broadcasted_iota(
        jnp.int32, (rows, rows), 1
    )

    def to_col(v):
        return jnp.sum(jnp.where(eye, jnp.broadcast_to(v, (rows, rows)), 0.0), axis=1, keepdims=True)

    def to_row(v):
        return jnp.sum(jnp.where(eye, jnp.broadcast_to(v, (rows, rows)), 0.0), axis=0, keepdims=True)

    mine_cols = pl.ds(pl.multiple_of(z * rows, rows), rows)
    slide = to_col(ids_ref[:, mine_cols].astype(F32))
    second = jnp.broadcast_to(slide > 0.5, (rows, wide))

    def by_slide(v):
        a = jnp.sum(jnp.where(second, 0.0, v), axis=0, keepdims=True)
        b = jnp.sum(jnp.where(second, v, 0.0), axis=0, keepdims=True)
        return a, b

    target = tgt[...].reshape(rows, wide)
    square = target * target
    for s, v in enumerate(by_slide(square)):
        gtrue[me, s : s + 1, :] = v
    strue[yk] = to_row(jnp.sum(square, axis=1, keepdims=True))

    def share(by_gene, by_spot):
        a = spread_to(
            [(by_gene.at[me], by_gene.at[me], d) for d in xz_peers], lambda n: by_gene.at[pl.ds(0, n)], late=True
        )
        b = spread_to(
            [(by_spot.at[yk], by_spot.at[yk], d) for d, _ in yk_peers],
            lambda n: by_spot.at[pl.ds(0, n)],
            late=True,
        )
        return a, b

    true_in = share(gtrue, strue)

    own_1 = add_y(nz - 1, r1, z)
    own_2 = add_y(nz - 1, r2, z)

    s_z_in()
    whole_sum = s_z[0]
    for q in range(1, nz):
        whole_sum = whole_sum + s_z[q]
    mass = whole_sum[0:1, :]
    inv_mass = 1.0 / mass
    slides = ids_ref[...].astype(F32)
    counts = cnt_ref[...].astype(F32)
    aux[x, 0:1, :] = mass
    aux[x, 1:2, :] = slides
    aux[x, 2:3, :] = counts
    aux[x, 3:4, :] = jnp.zeros((1, cols), F32)
    aux_in = remote(aux.at[x], aux.at[x], xp, late=True)
    low_sum = s_z[0, 1:2, mine_cols]
    for q in range(1, nz):
        low_sum = low_sum + s_z[q, 1:2, mine_cols]
    inv_low = 1.0 / to_col(low_sum)

    landed(zrecv.at[pl.ds(0, nz - 1)], z_recv)
    pred = jnp.concatenate([own_1, own_2], axis=0)
    for q in others:
        pred = pred + zrecv[q].astype(F32)
    pred = pred * inv_low
    both = pred * target
    pair = pred * pred
    for r, v in enumerate((both, pair)):
        for s, w in enumerate(by_slide(v)):
            gsum[me, 2 * r + s : 2 * r + s + 1, :] = w
        ssum[yk, r : r + 1, :] = to_row(jnp.sum(v, axis=1, keepdims=True))
    sum_in = share(gsum, ssum)
    lg_in.append(remote(lg_hbm.at[gap], lgo.at[gap], xp, late=True))
    prd[...] = pred.reshape(YK, part, wide)
    p_in = spread_to(
        [(prd.at[b], p_out.at[yk], d) for d, b in yk_peers], lambda n: p_out.at[pl.ds(0, n)], late=True
    )
    p_out[yk] = prd[yk]

    def weights(src, scale, to):
        for i in range(cells // piece):
            r = pl.ds(i * piece, piece)
            wv[to, r, :] = (jnp.exp(src[r, :].astype(F32)) * scale).astype(BF16)

    weights(lgv, inv_mass, x)
    for wait in true_in + sum_in:
        wait()
    for ref, i in sends:
        left(ref, i)
    used = dict(taken)
    taken.update(send=0, recv=0)
    sends.clear()

    def added(ref, n):
        v = ref[0]
        for q in range(1, n):
            v = v + ref[q]
        return v

    genes = YK * wide
    spots = nx * cols
    gene_step = -1.0 / (2 * genes)
    spot_step = -1.0 / spots
    gs = added(gsum, nx * nz)
    gene_a = lax.rsqrt(gs[2:4] + EPSILON)
    gene_b = lax.rsqrt(added(gtrue, nx * nz) + EPSILON)
    gene_cos = gs[0:2] * gene_a * gene_b
    t_gene = gene_step * gene_a * gene_b
    p_gene = -gene_step * gs[0:2] * gene_b * gene_a * gene_a * gene_a
    ss = added(ssum, YK)
    pred_scale = lax.rsqrt(ss[1:2] + EPSILON)
    true_scale = lax.rsqrt(added(strue, YK) + EPSILON)
    spot_cos = ss[0:1] * pred_scale * true_scale
    t_spot = to_col(spot_step * pred_scale * true_scale)
    p_spot = to_col(-spot_step * ss[0:1] * pred_scale * pred_scale * pred_scale * true_scale)

    def of_slide(v):
        return jnp.where(
            second, jnp.broadcast_to(v[1:2], (rows, wide)), jnp.broadcast_to(v[0:1], (rows, wide))
        )

    grad = (of_slide(t_gene) + t_spot) * target + (of_slide(p_gene) + p_spot) * pred
    low = grad.astype(BF16)
    g[me, y, k] = low

    part_a, part_b, part_c = pl.ds(0, cut), pl.ds(cut, cut), pl.ds(2 * cut, rows - 2 * cut)
    part_ab = pl.ds(0, 2 * cut)
    z_out, c_out = sems("send"), sems("send")
    y_out, x_out, cy_out, cx_out, cd_out, a_out, b_out, core_out = (sems("send") for _ in range(8))
    from_z, from_y, from_x = (sems("recv", 2 * nz) for _ in range(3))
    from_a, from_b = (sems("recv", nz) for _ in range(2))
    cy_in, cx_in, cd_in = (sems("recv") for _ in range(3))
    from_c, core_in = sems("recv", 4 * nz), sems("recv", 4)
    kinds = ((x, y, 0), (xo, y, 2), (x, yo, 1), (xo, yo, 3))

    def to_core(shard, region):
        put(shard, shard, sib, core_out, core_in + region)

    def pass_on(shard, upward, send, recv):
        @pl.when(z < nz - 1 if upward else z > 0)
        def _():
            put(shard, shard, dev(z + 1 if upward else z - 1, y, k, x), send, recv)

    at_end = (z == 0) | (z == nz - 1)

    def own_z():
        for h, r in enumerate((part_a, part_b)):
            shard = g.at[me, y, k, r]
            pass_on(shard, True, z_out, from_z + 2 * z + h)
            pass_on(shard, False, z_out, from_z + 2 * z + h)

        @pl.when(at_end)
        def _():
            for h, r in enumerate((part_a, part_b)):
                shard = g.at[me, y, k, r]
                put(shard, shard, dev(nz - 1 - z, y, k, x), z_out, from_z + 2 * z + h)

    def own_c():
        shard = g.at[me, y, k, part_c]
        put(shard, shard, yp, cy_out, cy_in)
        put(shard, shard, xp, cx_out, cx_in)

    def own_y():
        for h, r in enumerate((part_a, part_b)):
            shard = g.at[me, y, k, r]
            put(shard, shard, yp, y_out, from_y + 2 * z + h)

    def own_x():
        for h, r in ((1, part_b), (0, part_a)):
            shard = g.at[me, y, k, r]
            put(shard, shard, xp, x_out, from_x + 2 * z + h)

    def own_core():
        to_core(g.at[me, y, k], 0)

    def start_c(kind):
        plane, yy, _ = kinds[kind]
        shard = g.at[plane * nz + z, yy, k, part_c]
        pass_on(shard, True, c_out, from_c + 4 * z + kind)
        pass_on(shard, False, c_out, from_c + 4 * z + kind)

        @pl.when(at_end)
        def _():
            put(shard, shard, dev(nz - 1 - z, y, k, x), c_out, from_c + 4 * z + kind)

    def wait_cy():
        shard = g.at[me, yo, k, part_c]
        landed(shard, cy_in)
        put(shard, shard, xp, cd_out, cd_in)
        to_core(shard, 1)

    def wait_cx():
        shard = g.at[xo * nz + z, y, k, part_c]
        landed(shard, cx_in)
        to_core(shard, 2)

    def wait_cd():
        shard = g.at[xo * nz + z, yo, k, part_c]
        landed(shard, cd_in)
        to_core(shard, 3)

    def at_distance(d, act):
        if d == 0:
            act(z, False)
            return

        @pl.when(z >= d)
        def _():
            act(z - d, False)

        @pl.when(z < nz - d)
        def _():
            act(z + d, True)

    def take_z(q, above, further=False):
        for h, r in enumerate((part_a, part_b)):
            shard = g.at[x * nz + q, y, k, r]
            landed(shard, from_z + 2 * q + h)
            if further:
                pass_on(shard, not above, z_out, from_z + 2 * q + h)
            put(shard, shard, yp, y_out, from_y + 2 * q + h)
            put(shard, shard, xp, x_out, from_x + 2 * q + h)
            to_core(shard, 0)

    def take_c(kind, further=False):
        def act(q, above):
            plane, yy, region = kinds[kind]
            shard = g.at[plane * nz + q, yy, k, part_c]
            landed(shard, from_c + 4 * q + kind)
            if further:
                pass_on(shard, not above, c_out, from_c + 4 * q + kind)
            to_core(shard, region)

        return act

    def take_y(q, above):
        for h, r in enumerate((part_a, part_b)):
            shard = g.at[x * nz + q, yo, k, r]
            landed(shard, from_y + 2 * q + h)
            if h == 0:
                put(shard, shard, xp, a_out, from_a + q)
            to_core(shard, 1)

    def take_x(q, above):
        for h, r in ((1, part_b), (0, part_a)):
            shard = g.at[xo * nz + q, y, k, r]
            landed(shard, from_x + 2 * q + h)
            if h == 1:
                put(shard, shard, yp, b_out, from_b + q)
            to_core(shard, 2)

    def take_d(q, above):
        for recv, r in ((from_a, part_a), (from_b, part_b)):
            shard = g.at[xo * nz + q, yo, k, r]
            landed(shard, recv + q)
            to_core(shard, 3)

    def grad_of(plane, yy, kk):
        return g[plane, yy, kk].reshape(cols, wide)

    def weight_term(yy, kk):
        return lax.dot_general(
            xl[yy * 2 + kk], grad_of(here, yy, kk), (((1,), (1,)), ((), ())), preferred_element_type=F32
        )

    def expr_term(q, plane, yy, kk):
        return jnp.dot(wv[q], grad_of(plane, yy, kk), preferred_element_type=F32)

    lane = lax.broadcasted_iota(jnp.int32, (1, rows), 1)

    own_z()
    own_x()
    own_c()
    own_core()
    own_y()
    lg_in.append(remote(lg_hbm.at[last], lgo.at[last], xp, late=True))
    st1[yk, 0:1, :] = to_row(jnp.sum(low.astype(F32) * pred, axis=1, keepdims=True))
    st1[yk, 1:2, :] = jnp.where(lane == 0, jnp.sum(gene_cos), 0.0)
    st1_in = spread_to([(st1.at[yk], st1.at[yk], d) for d, _ in yk_peers], lambda n: st1.at[pl.ds(0, n)])
    start_c(0)
    wait_cy()
    take_x(z, False)
    at_distance(1, functools.partial(take_z, further=True))
    at_distance(3, take_z)
    wait_cd()
    at_distance(1, take_c(0, True))
    start_c(2)
    wait_cx()
    at_distance(2, take_z)
    start_c(3)
    aux_in()
    for wait in lg_in:
        wait()
    weights(lgo, 1.0 / aux[xo, 0:1, :], xo)
    take_y(z, False)
    start_c(1)
    at_distance(1, take_c(2, True))
    at_distance(3, take_x)
    at_distance(3, take_y)
    at_distance(2, take_c(0))
    at_distance(3, take_c(0))
    at_distance(1, take_y)
    at_distance(1, take_x)
    st1_in()
    whole = added(st1, YK)
    st2[me, 0:1, :] = whole[0:1]
    st2[me, 1:2, :] = jnp.where(lane == 0, whole[1:2], jnp.where(lane == 1, jnp.sum(spot_cos), 0.0))
    st2_in = spread_to([(st2.at[me], st2.at[me], d) for d in xz_peers], lambda n: st2.at[pl.ds(0, n)])
    eg[y, k] = expr_term(x, here, y, k)
    at_distance(2, take_y)
    lgrad[...] = weight_term(y, k)
    at_distance(1, take_c(3, True))
    at_distance(3, take_c(2))
    at_distance(2, take_x)
    at_distance(1, take_c(1, True))
    landed(g.at[here, y, ko], core_in)
    lgrad[...] += weight_term(y, ko)
    at_distance(2, take_c(2))
    eg[yo, k] = expr_term(x, here, yo, k)
    lgrad[...] += weight_term(yo, k)
    take_d(z, False)
    at_distance(3, take_c(1))
    landed(g.at[here, yo, ko], core_in + 1)
    lgrad[...] += weight_term(yo, ko)
    at_distance(2, take_c(3))
    at_distance(1, take_d)
    at_distance(3, take_c(3))
    at_distance(2, take_d)
    at_distance(3, take_d)
    at_distance(2, take_c(1))
    eg[y, k] += expr_term(xo, there, y, k)
    eg[y, ko] = expr_term(x, here, y, ko)

    kl = 0.0
    slide_mass, slide_count = [], []
    for s in range(2):
        m = n = cl = cm = 0.0
        for q in range(nx):
            of_s = jnp.abs(aux[q, 1:2, :] - s) < 0.5
            n_q = jnp.where(of_s, aux[q, 2:3, :], 0.0)
            m = m + jnp.sum(jnp.where(of_s, aux[q, 0:1, :], 0.0))
            n = n + jnp.sum(n_q)
            cl = cl + jnp.sum(n_q * jnp.log(aux[q, 2:3, :]))
            cm = cm + jnp.sum(n_q * jnp.log(aux[q, 0:1, :]))
        some = n > 0.5
        m = jnp.full((1, 128), jnp.where(some, m, 1.0), F32)
        n = jnp.full((1, 128), jnp.where(some, n, 1.0), F32)
        kl = kl + jnp.where(some, (cl - cm) / n - jnp.log(n) + jnp.log(m), 0.0)
        slide_mass.append(m[:, 0:1])
        slide_count.append(n[:, 0:1])
    is_second = slides > 0.5
    mass_grad = mass / jnp.where(is_second, slide_mass[1], slide_mass[0]) - counts / jnp.where(
        is_second, slide_count[1], slide_count[0]
    )
    st2_in()
    gene_total = whole[1:2]
    spot_total = added(st2, nx * nz)[1:2]
    loss_out[...] = (
        -jnp.sum(jnp.where(lane == 0, gene_total, 0.0)) / (2 * genes)
        - jnp.sum(jnp.where(lane == 1, spot_total, 0.0)) / spots
        + kl
    )
    vec[0:1, :] = inv_mass
    vec[1:2, :] = mass_grad - jnp.concatenate([st2[x * nz + q, 0:1, :] for q in range(nz)], axis=1)

    p_in()
    landed(g.at[there, y, ko], core_in + 2)
    landed(g.at[there, yo, ko], core_in + 3)
    for ref, i in sends + late_sends:
        left(ref, i)
    left(g.at[here, y, k, part_ab], y_out)
    left(g.at[here, y, k, part_ab], x_out)
    for i in (cy_out, cx_out, cd_out):
        left(g.at[me, y, k, part_c], i)
    left(g.at[here, yo, k, part_a], a_out)
    left(g.at[there, y, k, part_b], b_out)
    left(g.at[:, :, k], core_out)

    @pl.when(at_end)
    def _():
        left(g.at[pl.ds(0, 2), y, k, part_ab], z_out)
        left(g.at[pl.ds(0, 8), y, k, part_c], c_out)

    @pl.when(jnp.logical_not(at_end))
    def _():
        left(g.at[pl.ds(0, nz), y, k, part_ab], z_out)
        left(g.at[pl.ds(0, nz), y, k], c_out)

    needed = {kind: max(used[kind], taken[kind]) + kept[kind] for kind in kept}
    assert needed == size, needed


def backward_kernel(
    nz, w_ref, g_ref, part_ref, lgrad_ref, lg_ref, vec_ref, p_ref, loss_ref,
    eg_hbm, lgrad_hbm, pred_ref, total_ref, eg, lgrad, done,
):
    c = lax.axis_index("cells")
    x = lax.axis_index("spots")
    y, k = (c % YK) // 2, c % 2
    nx, cells, cols = w_ref.shape
    wide = g_ref.shape[4]
    tall = cells // 4
    xo = (x + 1) % nx
    copies = []

    def out(src, dst):
        cp = pltpu.make_async_copy(src, dst, done.at[len(copies)])
        cp.start()
        copies.append(cp)

    def genes_at(yy, kk):
        return eg_hbm.at[:, pl.ds(pl.multiple_of((yy * 2 + kk) * wide, wide), wide)]

    def term(q, yy, kk, r):
        block = g_ref[pl.ds(q * nz, nz), yy, kk].reshape(cols, wide)
        return jnp.dot(w_ref[q, r, :], block, preferred_element_type=F32)

    out(part_ref.at[y, k], genes_at(y, k))
    lgrad[...] = jnp.exp(lg_ref[...].astype(F32)) * vec_ref[0:1, :] * (lgrad_ref[...] + vec_ref[1:2, :])
    out(lgrad, lgrad_hbm)
    for i, (yy, kk) in enumerate(((y, 1 - k), (1 - y, k), (1 - y, 1 - k))):
        for n in range(4):
            r = pl.ds(n * tall, tall)
            mine = part_ref[yy, kk, r, :] if i < 2 else term(x, yy, kk, r)
            eg[i, r, :] = mine + term(xo, yy, kk, r)
            out(eg.at[i, r], genes_at(yy, kk).at[r])
    for b in range(YK):
        out(p_ref.at[b], pred_ref.at[:, b * wide : (b + 1) * wide])
    total_ref[...] = loss_ref[:, 0:1]
    for cp in copies:
        cp.wait()


def step(ncells, nx, logits, expression, spatial, slide_ids, spot_counts):
    cells, cols = logits.shape
    genes = expression.shape[1]
    nz = ncells // YK
    rows = cols // nz
    wide = genes // YK
    part = rows // YK
    half = wide // 2
    anywhere = pl.BlockSpec(memory_space=pl.ANY)
    whole = pl.BlockSpec(memory_space=pltpu.VMEM)
    *held, p, loss = pl.pallas_call(
        functools.partial(forward_kernel, nz, nx),
        out_shape=(
            pltpu.VMEM((nx, cells, cols), BF16),
            pltpu.VMEM((nx * nz, 2, 2, rows, wide), BF16),
            pltpu.VMEM((2, 2, cells, wide), F32),
            pltpu.VMEM((cells, cols), F32),
            pltpu.VMEM((cells, cols), BF16),
            pltpu.VMEM((2, cols), F32),
            pltpu.VMEM((YK, part, wide), F32),
            pltpu.VMEM((1, 128), F32),
        ),
        in_specs=[anywhere] * 5,
        out_specs=(whole,) * 8,
        scratch_shapes=[
            pltpu.VMEM((cells, cols), BF16),
            pltpu.VMEM((cols, cells), BF16),
            pltpu.VMEM((YK, cells, wide), F32),
            pltpu.VMEM((YK, cells, wide), BF16),
            pltpu.VMEM((YK, nz, rows, wide), F32),
            pltpu.VMEM((2, nz, rows, wide), F32),
            pltpu.VMEM((nz, rows, wide), BF16),
            pltpu.VMEM((nz, rows, wide), BF16),
            pltpu.VMEM((nz, rows, wide), BF16),
            pltpu.VMEM((nz, rows, wide), BF16),
            pltpu.VMEM((YK, part, wide), F32),
            pltpu.VMEM((YK, part, wide), F32),
            pltpu.VMEM((2, cols), F32),
            pltpu.VMEM((2, cols), F32),
            pltpu.VMEM((2, cols), F32),
            pltpu.VMEM((2, cols), F32),
            pltpu.VMEM((2, cols), F32),
            pltpu.VMEM((nz, 2, cols), F32),
            pltpu.VMEM((nx, 4, cols), F32),
            pltpu.VMEM((nx * nz, 2, wide), F32),
            pltpu.VMEM((YK, 1, rows), F32),
            pltpu.VMEM((nx * nz, 4, wide), F32),
            pltpu.VMEM((YK, 2, rows), F32),
            pltpu.VMEM((YK, 2, rows), F32),
            pltpu.VMEM((nx * nz, 2, rows), F32),
            pltpu.VMEM((1, cols), jnp.int32),
            pltpu.VMEM((1, cols), jnp.int32),
            pltpu.SemaphoreType.DMA((8,)),
            pltpu.SemaphoreType.DMA((21,)),
            pltpu.SemaphoreType.DMA((18 + 12 * nz,)),
        ],
        compiler_params=pltpu.CompilerParams(
            collective_id=0, has_side_effects=True, vmem_limit_bytes=36 << 20
        ),
        name="forward_and_gather",
    )(
        *(
            pltpu.with_memory_space_constraint(v, pltpu.HBM)
            for v in (logits, expression, spatial, slide_ids, spot_counts)
        )
    )

    held = [pltpu.with_memory_space_constraint(v, pltpu.VMEM) for v in held]
    return pl.pallas_call(
        functools.partial(backward_kernel, nz),
        out_shape=(
            jax.ShapeDtypeStruct((cells, genes), F32),
            jax.ShapeDtypeStruct((cells, cols), F32),
            jax.ShapeDtypeStruct((part, genes), F32),
            jax.ShapeDtypeStruct((1, 1), F32),
        ),
        in_specs=[whole] * 8,
        out_specs=(anywhere, anywhere, anywhere, whole),
        scratch_shapes=[
            pltpu.VMEM((3, cells, wide), F32),
            pltpu.VMEM((cells, cols), F32),
            pltpu.SemaphoreType.DMA((18,)),
        ],
        compiler_params=pltpu.CompilerParams(vmem_limit_bytes=24 << 20),
        name="backward",
    )(*held, p, loss)


def kernel_step(ncells, nx, *args):
    grad_expr, grad_logits, predicted, loss = step(ncells, nx, *args)
    return (predicted[None], loss[0, 0], grad_logits, grad_expr)


def fits(ncells, nx, logits, expression, spatial):
    cells, cols = logits.shape
    genes = expression.shape[1]
    if ncells != 4 * YK or nx != 2 or cols % (ncells // YK) or genes % (YK * 256):
        return False
    rows = cols // (ncells // YK)
    held = (cells + rows) * genes * 8 + cells * cols * 16 + cols * genes * 16
    return rows % 128 == 0 and cells % 128 == 0 and held < 50 << 20


def plain_step(logits, expression, spatial, slide_ids, spot_counts):
    highest = lax.Precision.HIGHEST
    ncells = lax.axis_size("cells")
    nspots = lax.axis_size("spots")
    columns = logits.shape[1]
    genes = expression.shape[1]
    out_rows = columns // ncells
    scores = logits.astype(F32)
    col_peak = lax.pmax(jnp.max(scores, axis=0), "cells")
    shifted = jnp.exp(scores - col_peak)
    col_total = lax.psum(jnp.sum(shifted, axis=0), "cells")
    weights = shifted / col_total
    log_mass = col_peak + jnp.log(col_total)
    weights_low = weights.astype(BF16)
    expr_low = expression.astype(BF16)
    contract_first = (((0,), (0,)), ((), ()))
    predicted = lax.psum_scatter(
        lax.dot_general(weights_low, expr_low, contract_first, preferred_element_type=F32),
        "cells",
        scatter_dimension=0,
        tiled=True,
    )
    target = spatial[0]
    member_all = (slide_ids[0][:, None] == jnp.arange(2, dtype=jnp.int32)[None, :]).astype(F32)
    first_row = lax.axis_index("cells") * out_rows
    member_rows = lax.dynamic_slice_in_dim(member_all, first_row, out_rows, 0)
    gene_inner = jnp.dot(member_rows.T, predicted * target, precision=highest)
    gene_pred = jnp.dot(member_rows.T, predicted * predicted, precision=highest)
    gene_true = jnp.dot(member_rows.T, target * target, precision=highest)
    spot_inner = jnp.sum(predicted * target, axis=1)
    pred_scale = lax.rsqrt(jnp.sum(predicted * predicted, axis=1) + EPSILON)
    true_scale = lax.rsqrt(jnp.sum(target * target, axis=1) + EPSILON)
    spot_sum = jnp.sum(spot_inner * pred_scale * true_scale)
    counts_real = spot_counts[0].astype(F32)
    exp_mass = jnp.exp(log_mass)
    local_mass = jnp.dot(member_all.T, exp_mass, precision=highest)
    local_count = jnp.dot(member_all.T, counts_real, precision=highest)
    local_clog = jnp.dot(member_all.T, counts_real * jnp.log(counts_real), precision=highest)
    local_clse = jnp.dot(member_all.T, counts_real * log_mass, precision=highest)
    slide_mass, slide_count, count_log, count_lse = lax.psum(
        (local_mass, local_count, local_clog, local_clse), "spots"
    )
    gene_inner, gene_pred, gene_true, spot_total = lax.psum(
        (gene_inner, gene_pred, gene_true, spot_sum), ("cells", "spots")
    )
    gene_a = lax.rsqrt(gene_pred + EPSILON)
    gene_b = lax.rsqrt(gene_true + EPSILON)
    gene_cos = gene_inner * gene_a * gene_b
    total_spots = columns * nspots
    some = slide_count > 0.5
    slide_count = jnp.where(some, slide_count, 1.0)
    slide_mass = jnp.where(some, slide_mass, 1.0)
    kl_value = jnp.sum(
        jnp.where(
            some,
            (count_log - count_lse) / slide_count - jnp.log(slide_count) + jnp.log(slide_mass),
            0.0,
        )
    )
    loss = -jnp.mean(gene_cos) - spot_total / total_spots + kl_value
    gene_step = -1.0 / (2 * genes)
    inner_grad = gene_step * gene_a * gene_b
    square_grad = -0.5 * gene_step * gene_inner * gene_b * gene_a * gene_a * gene_a
    pred_grad = jnp.dot(member_rows, inner_grad, precision=highest) * target
    pred_grad = pred_grad + 2.0 * jnp.dot(member_rows, square_grad, precision=highest) * predicted
    spot_step = -1.0 / total_spots
    pred_grad = pred_grad + (spot_step * pred_scale * true_scale)[:, None] * target
    pred_grad = (
        pred_grad
        - (spot_step * spot_inner * pred_scale * pred_scale * pred_scale * true_scale)[:, None]
        * predicted
    )
    grad_low = pred_grad.astype(BF16)
    mass_grad = exp_mass / jnp.dot(
        member_all, slide_mass, precision=highest
    ) - counts_real / jnp.dot(member_all, slide_count, precision=highest)
    contract_genes = (((1,), (1,)), ((), ()))
    grad_all = lax.all_gather(grad_low, "cells", axis=0, tiled=True)
    expr_part = jnp.dot(weights_low, grad_all, preferred_element_type=F32)
    weight_grad = lax.dot_general(
        expr_low, grad_all, contract_genes, preferred_element_type=F32
    )
    col_inner = lax.psum(jnp.sum(weights * weight_grad, axis=0), "cells")
    logit_grad = weights * (weight_grad - col_inner + mass_grad)
    expr_grad = lax.psum(expr_part, "spots")
    return (predicted[None], loss, logit_grad, expr_grad)


def solution(mesh):
    ncells, nx = mesh.shape["cells"], mesh.shape["spots"]

    def per_device(*args):
        if fits(ncells, nx, *args[:3]):
            return kernel_step(ncells, nx, *args)
        return plain_step(*args)

    return jax.shard_map(
        per_device,
        mesh=mesh,
        in_specs=(
            P("cells", "spots"),
            P("cells", None),
            P("spots", "cells", None),
            P("spots", None),
            P("spots", None),
        ),
        out_specs=(P("spots", "cells", None), P(), P("cells", "spots"), P("cells", None)),
        check_vma=False,
    )
```

```python
import functools

import jax
import jax.numpy as jnp
from jax import lax
from jax.experimental import pallas as pl
from jax.experimental.pallas import tpu as pltpu
from jax.sharding import PartitionSpec as P

EPSILON = 1e-06
MESH = pl.DeviceIdType.MESH
F32 = jnp.float32
BF16 = jnp.bfloat16
YK = 4


def forward_kernel(
    nz,
    nx,
    lg_hbm, ex_hbm, sp_hbm, ids_hbm, cnt_hbm,
    wv, g, eg, lgrad, lgv, vec, p_out, loss_out,
    lgo, et, exv, xl, pf, psib, ysend, yrecv, zsend, zrecv, zrelay, tgt, prd,
    s_own, s_sib, s_pair, s_y, s_quad, s_z, aux, gtrue, strue, gsum, ssum, st1, st2, ids_ref, cnt_ref,
    loc, snd, rcv,
):
    cells, cols = lgv.shape
    rows, wide = pf.shape[2:]
    part = rows // YK
    c = lax.axis_index("cells")
    x = lax.axis_index("spots")
    z = c // YK
    yk = c % YK
    y = yk // 2
    k = yk % 2
    yo, ko, xo = 1 - y, 1 - k, (x + 1) % nx
    me = x * nz + z
    here, there = pl.ds(x * nz, nz), pl.ds(xo * nz, nz)

    def dev(zz, yy, kk, xx):
        return (zz * YK + yy * 2 + kk, xx)

    sib, yp, dia, xp = dev(z, y, ko, x), dev(z, yo, k, x), dev(z, yo, ko, x), dev(z, y, k, xo)
    yk_peers = ((sib, y * 2 + ko), (yp, yo * 2 + k), (dia, yo * 2 + ko))
    others = [(z + r) % nz for r in range(1, nz)]
    others = others[1:2] + others[:1] + others[2:]
    z_peers = [dev(q, y, k, x) for q in others]
    xz_peers = [dev(q, y, k, xo) for q in others] + z_peers + [xp]

    taken = {"send": 0, "recv": 0, "local": 0}
    kept = {"send": 0, "recv": 0}
    size = {"send": snd.shape[0], "recv": rcv.shape[0]}
    sends, late_sends = [], []

    def sems(kind, n=1):
        taken[kind] += n
        return taken[kind] - n

    def keep(kind):
        kept[kind] += 1
        return size[kind] - kept[kind]

    def put(src, dst, device, send, recv):
        pltpu.make_async_remote_copy(
            src_ref=src, dst_ref=dst, send_sem=snd.at[send], recv_sem=rcv.at[recv],
            device_id=device, device_id_type=MESH,
        ).start()

    def landed(ref, recv):
        pltpu.make_async_remote_copy(
            src_ref=ref, dst_ref=ref, send_sem=snd.at[0], recv_sem=rcv.at[recv],
            device_id=sib, device_id_type=MESH,
        ).wait_recv()

    def left(ref, send):
        pltpu.make_async_remote_copy(
            src_ref=ref, dst_ref=ref, send_sem=snd.at[send], recv_sem=rcv.at[0],
            device_id=sib, device_id_type=MESH,
        ).wait_send()

    def remote(src, dst, device, late=False):
        return spread_to([(src, dst, device)], lambda n: dst, late)

    def spread_to(pairs, size, late=False):
        take = keep if late else sems
        i, j = take("send"), take("recv")
        for src, dst, device in pairs:
            put(src, dst, device, i, j)
        (late_sends if late else sends).append((size(len(pairs)), i))
        return lambda: landed(size(len(pairs)), j)

    def local(src, dst):
        cp = pltpu.make_async_copy(src, dst, loc.at[sems("local")])
        cp.start()
        return cp

    barrier = pltpu.get_barrier_semaphore()
    for d in [p[0] for p in yk_peers] + xz_peers:
        pl.semaphore_signal(barrier, inc=1, device_id=d, device_id_type=MESH)

    def genes_of(ref, b):
        return ref.at[..., pl.ds(pl.multiple_of(b * wide, wide), wide)]

    blocks = (yo * 2 + ko, yo * 2 + k, y * 2 + ko, yk)
    lg_copy = local(lg_hbm, lgv)
    ex_copies = [local(genes_of(ex_hbm, b), exv.at[i]) for i, b in enumerate(blocks)]
    late = [
        local(genes_of(sp_hbm.at[0], yk), tgt.at[yk]),
        local(ids_hbm, ids_ref),
        local(cnt_hbm, cnt_ref),
    ]

    lg_copy.wait()
    piece = 128
    total = jnp.zeros((1, cols), F32)
    total_low = jnp.zeros((1, cols), F32)
    for i in range(cells // piece):
        e = jnp.exp(lgv[pl.ds(i * piece, piece), :].astype(F32))
        low = e.astype(BF16).astype(F32)
        total = total + jnp.sum(e, axis=0, keepdims=True)
        total_low = total_low + jnp.sum(low, axis=0, keepdims=True)
        et[:, pl.ds(i * piece, piece)] = low.T.astype(BF16)
    s_own[0:1, :] = total
    s_own[1:2, :] = total_low

    half = wide // 2

    def forward(i):
        ex_copies[i].wait()
        for n in range(2):
            lanes = pl.ds(n * half, half)
            low = exv[i, :, lanes].astype(BF16)
            xl[blocks[i], :, lanes] = low
            pf[i, :, :, lanes] = jnp.dot(et[...], low, preferred_element_type=F32).reshape(
                nz, rows, half
            )

    cut = rows * 3 // 8
    r1, r2 = pl.ds(0, cut), pl.ds(cut, rows - cut)
    most, more = cells * 13 // 16, cells // 8
    early, gap, last = pl.ds(0, most), pl.ds(most, more), pl.ds(most + more, cells - most - more)

    forward(0)
    pl.semaphore_wait(barrier, len(yk_peers) + len(xz_peers))
    s_sib_in = remote(s_own, s_sib, sib)
    order = [(r1, 0), (r2, 0)] + [(r, i) for r in (r1, r2) for i in range(1, nz - 1)]
    rows_of = others + [z]
    sib_in = {
        (r.start, i): remote(pf.at[0, rows_of[i], r], psib.at[0, rows_of[i], r], sib)
        for r, i in order + [(r1, nz - 1), (r2, nz - 1)]
    }
    lg_in = [remote(lg_hbm.at[early], lgo.at[early], xp, late=True)]
    forward(1)
    s_sib_in()
    s_pair[...] = s_own[...] + s_sib[...]
    s_y_in = remote(s_pair, s_y, yp)

    y_send = sems("send")
    y_in = {}

    def send_y(r, i):
        q = rows_of[i]
        sib_in[r.start, i]()
        ysend[q, r] = (pf[1, q, r] + psib[0, q, r]).astype(BF16)
        y_in[r.start, i] = sems("recv")
        put(ysend.at[q, r], yrecv.at[q, r], yp, y_send, y_in[r.start, i])

    for r, i in order[:3]:
        send_y(r, i)
    forward(2)
    sib_rest = remote(pf.at[2], psib.at[1], sib)
    forward(3)
    for r, i in order[3:]:
        send_y(r, i)
    t_in = spread_to(
        [(genes_of(sp_hbm.at[0], b), tgt.at[yk], d) for d, b in yk_peers],
        lambda n: tgt.at[pl.ds(0, n)],
    )
    send_y(r1, nz - 1)
    send_y(r2, nz - 1)
    sends.append((ysend, y_send))

    s_y_in()
    s_quad[...] = s_pair[...] + s_y[...]
    s_z[z] = s_quad[...]
    s_z_in = spread_to(
        [(s_quad, s_z.at[z], d) for d in z_peers], lambda n: s_z.at[pl.ds(0, n)]
    )

    z_send, z_recv = sems("send"), sems("recv")

    relay_in = {r.start: sems("recv", nz) for r in (r1, r2)}
    at_end = (z == 0) | (z == nz - 1)
    between = dev(z + 1 - 2 * (z // (nz // 2)), y, k, x)

    def add_y(r, i):
        q = rows_of[i]
        landed(yrecv.at[q, r], y_in[r.start, i])
        return pf[3, q, r] + psib[1, q, r] + yrecv[q, r].astype(F32)

    sib_rest()
    for r, i in order:
        q = rows_of[i]
        term = add_y(r, i)
        if i == 0:
            zsend[q, r] = term.astype(BF16)
            put(zsend.at[q, r], zrelay.at[q, r], between, z_send, relay_in[r.start] + q)
            continue

        @pl.when(at_end)
        def _():
            zsend[q, r] = term.astype(BF16)

        @pl.when(jnp.logical_not(at_end))
        def _():
            landed(zrelay.at[q, r], relay_in[r.start] + q)
            zsend[q, r] = (term + zrelay[q, r].astype(F32)).astype(BF16)

        put(zsend.at[q, r], zrecv.at[z, r], z_peers[i], z_send, z_recv)
    sends.append((zsend.at[pl.ds(0, nz - 1)], z_send))

    for cp in late:
        cp.wait()
    t_in()
    eye = lax.broadcasted_iota(jnp.int32, (rows, rows), 0) == lax.broadcasted_iota(
        jnp.int32, (rows, rows), 1
    )

    def to_col(v):
        return jnp.sum(jnp.where(eye, jnp.broadcast_to(v, (rows, rows)), 0.0), axis=1, keepdims=True)

    def to_row(v):
        return jnp.sum(jnp.where(eye, jnp.broadcast_to(v, (rows, rows)), 0.0), axis=0, keepdims=True)

    mine_cols = pl.ds(pl.multiple_of(z * rows, rows), rows)
    slide = to_col(ids_ref[:, mine_cols].astype(F32))
    second = jnp.broadcast_to(slide > 0.5, (rows, wide))

    def by_slide(v):
        a = jnp.sum(jnp.where(second, 0.0, v), axis=0, keepdims=True)
        b = jnp.sum(jnp.where(second, v, 0.0), axis=0, keepdims=True)
        return a, b

    target = tgt[...].reshape(rows, wide)
    square = target * target
    for s, v in enumerate(by_slide(square)):
        gtrue[me, s : s + 1, :] = v
    strue[yk] = to_row(jnp.sum(square, axis=1, keepdims=True))

    def share(by_gene, by_spot):
        a = spread_to(
            [(by_gene.at[me], by_gene.at[me], d) for d in xz_peers], lambda n: by_gene.at[pl.ds(0, n)], late=True
        )
        b = spread_to(
            [(by_spot.at[yk], by_spot.at[yk], d) for d, _ in yk_peers],
            lambda n: by_spot.at[pl.ds(0, n)],
            late=True,
        )
        return a, b

    true_in = share(gtrue, strue)

    own_1 = add_y(r1, nz - 1)
    own_2 = add_y(r2, nz - 1)

    s_z_in()
    whole_sum = s_z[0]
    for q in range(1, nz):
        whole_sum = whole_sum + s_z[q]
    mass = whole_sum[0:1, :]
    inv_mass = 1.0 / mass
    slides = ids_ref[...].astype(F32)
    counts = cnt_ref[...].astype(F32)
    aux[x, 0:1, :] = mass
    aux[x, 1:2, :] = slides
    aux[x, 2:3, :] = counts
    aux[x, 3:4, :] = jnp.zeros((1, cols), F32)
    aux_in = remote(aux.at[x], aux.at[x], xp, late=True)
    low_sum = s_z[0, 1:2, mine_cols]
    for q in range(1, nz):
        low_sum = low_sum + s_z[q, 1:2, mine_cols]
    inv_low = 1.0 / to_col(low_sum)

    landed(zrecv.at[pl.ds(0, nz - 2)], z_recv)
    pred = jnp.concatenate([own_1, own_2], axis=0)
    for q in others[1:]:
        pred = pred + zrecv[q].astype(F32)
    pred = pred * inv_low
    both = pred * target
    pair = pred * pred
    for r, v in enumerate((both, pair)):
        for s, w in enumerate(by_slide(v)):
            gsum[me, 2 * r + s : 2 * r + s + 1, :] = w
        ssum[yk, r : r + 1, :] = to_row(jnp.sum(v, axis=1, keepdims=True))
    sum_in = share(gsum, ssum)
    lg_in.append(remote(lg_hbm.at[gap], lgo.at[gap], xp, late=True))
    prd[...] = pred.reshape(YK, part, wide)
    p_in = spread_to(
        [(prd.at[b], p_out.at[yk], d) for d, b in yk_peers], lambda n: p_out.at[pl.ds(0, n)], late=True
    )
    p_out[yk] = prd[yk]

    def weights(src, scale, to):
        for i in range(cells // piece):
            r = pl.ds(i * piece, piece)
            wv[to, r, :] = (jnp.exp(src[r, :].astype(F32)) * scale).astype(BF16)

    weights(lgv, inv_mass, x)
    for wait in true_in + sum_in:
        wait()
    for ref, i in sends:
        left(ref, i)
    used = dict(taken)
    taken.update(send=0, recv=0)
    sends.clear()

    def added(ref, n):
        v = ref[0]
        for q in range(1, n):
            v = v + ref[q]
        return v

    genes = YK * wide
    spots = nx * cols
    gene_step = -1.0 / (2 * genes)
    spot_step = -1.0 / spots
    gs = added(gsum, nx * nz)
    gene_a = lax.rsqrt(gs[2:4] + EPSILON)
    gene_b = lax.rsqrt(added(gtrue, nx * nz) + EPSILON)
    gene_cos = gs[0:2] * gene_a * gene_b
    t_gene = gene_step * gene_a * gene_b
    p_gene = -gene_step * gs[0:2] * gene_b * gene_a * gene_a * gene_a
    ss = added(ssum, YK)
    pred_scale = lax.rsqrt(ss[1:2] + EPSILON)
    true_scale = lax.rsqrt(added(strue, YK) + EPSILON)
    spot_cos = ss[0:1] * pred_scale * true_scale
    t_spot = to_col(spot_step * pred_scale * true_scale)
    p_spot = to_col(-spot_step * ss[0:1] * pred_scale * pred_scale * pred_scale * true_scale)

    def of_slide(v):
        return jnp.where(
            second, jnp.broadcast_to(v[1:2], (rows, wide)), jnp.broadcast_to(v[0:1], (rows, wide))
        )

    grad = (of_slide(t_gene) + t_spot) * target + (of_slide(p_gene) + p_spot) * pred
    low = grad.astype(BF16)
    g[me, y, k] = low

    part_a, part_b, part_c = pl.ds(0, cut), pl.ds(cut, cut), pl.ds(2 * cut, rows - 2 * cut)
    part_ab = pl.ds(0, 2 * cut)
    z_out, c_out = sems("send"), sems("send")
    y_out, x_out, cy_out, cx_out, cd_out, a_out, b_out, core_out = (sems("send") for _ in range(8))
    from_z, from_y, from_x = (sems("recv", 2 * nz) for _ in range(3))
    from_a, from_b = (sems("recv", nz) for _ in range(2))
    cy_in, cx_in, cd_in = (sems("recv") for _ in range(3))
    from_c, core_in = sems("recv", 4 * nz), sems("recv", 4)
    kinds = ((x, y, 0), (xo, y, 2), (x, yo, 1), (xo, yo, 3))

    def to_core(shard, region):
        put(shard, shard, sib, core_out, core_in + region)

    def pass_on(shard, upward, send, recv):
        @pl.when(z < nz - 1 if upward else z > 0)
        def _():
            put(shard, shard, dev(z + 1 if upward else z - 1, y, k, x), send, recv)

    def own_z():
        for h, r in enumerate((part_a, part_b)):
            shard = g.at[me, y, k, r]
            pass_on(shard, True, z_out, from_z + 2 * z + h)
            pass_on(shard, False, z_out, from_z + 2 * z + h)

        @pl.when(at_end)
        def _():
            for h, r in enumerate((part_a, part_b)):
                shard = g.at[me, y, k, r]
                put(shard, shard, dev(nz - 1 - z, y, k, x), z_out, from_z + 2 * z + h)

    def own_c():
        shard = g.at[me, y, k, part_c]
        put(shard, shard, yp, cy_out, cy_in)
        put(shard, shard, xp, cx_out, cx_in)

    def own_y():
        for h, r in enumerate((part_a, part_b)):
            shard = g.at[me, y, k, r]
            put(shard, shard, yp, y_out, from_y + 2 * z + h)

    def own_x():
        for h, r in ((1, part_b), (0, part_a)):
            shard = g.at[me, y, k, r]
            put(shard, shard, xp, x_out, from_x + 2 * z + h)

    def own_core():
        to_core(g.at[me, y, k], 0)

    def start_c(kind):
        plane, yy, _ = kinds[kind]
        shard = g.at[plane * nz + z, yy, k, part_c]
        pass_on(shard, True, c_out, from_c + 4 * z + kind)
        pass_on(shard, False, c_out, from_c + 4 * z + kind)

        @pl.when(at_end)
        def _():
            put(shard, shard, dev(nz - 1 - z, y, k, x), c_out, from_c + 4 * z + kind)

    def wait_cy():
        shard = g.at[me, yo, k, part_c]
        landed(shard, cy_in)
        put(shard, shard, xp, cd_out, cd_in)
        to_core(shard, 1)

    def wait_cx():
        shard = g.at[xo * nz + z, y, k, part_c]
        landed(shard, cx_in)
        to_core(shard, 2)

    def wait_cd():
        shard = g.at[xo * nz + z, yo, k, part_c]
        landed(shard, cd_in)
        to_core(shard, 3)

    def at_distance(d, act):
        if d == 0:
            act(z, False)
            return

        @pl.when(z >= d)
        def _():
            act(z - d, False)

        @pl.when(z < nz - d)
        def _():
            act(z + d, True)

    def take_z(q, above, further=False):
        for h, r in enumerate((part_a, part_b)):
            shard = g.at[x * nz + q, y, k, r]
            landed(shard, from_z + 2 * q + h)
            if further:
                pass_on(shard, not above, z_out, from_z + 2 * q + h)
            put(shard, shard, yp, y_out, from_y + 2 * q + h)
            put(shard, shard, xp, x_out, from_x + 2 * q + h)
            to_core(shard, 0)

    def take_c(kind, further=False):
        def act(q, above):
            plane, yy, region = kinds[kind]
            shard = g.at[plane * nz + q, yy, k, part_c]
            landed(shard, from_c + 4 * q + kind)
            if further:
                pass_on(shard, not above, c_out, from_c + 4 * q + kind)
            to_core(shard, region)

        return act

    def take_y(q, above):
        for h, r in enumerate((part_a, part_b)):
            shard = g.at[x * nz + q, yo, k, r]
            landed(shard, from_y + 2 * q + h)
            if h == 0:
                put(shard, shard, xp, a_out, from_a + q)
            to_core(shard, 1)

    def take_x(q, above):
        for h, r in ((1, part_b), (0, part_a)):
            shard = g.at[xo * nz + q, y, k, r]
            landed(shard, from_x + 2 * q + h)
            if h == 1:
                put(shard, shard, yp, b_out, from_b + q)
            to_core(shard, 2)

    def take_d(q, above):
        for recv, r in ((from_a, part_a), (from_b, part_b)):
            shard = g.at[xo * nz + q, yo, k, r]
            landed(shard, recv + q)
            to_core(shard, 3)

    def grad_of(plane, yy, kk):
        return g[plane, yy, kk].reshape(cols, wide)

    def weight_term(yy, kk):
        return lax.dot_general(
            xl[yy * 2 + kk], grad_of(here, yy, kk), (((1,), (1,)), ((), ())), preferred_element_type=F32
        )

    def expr_term(q, plane, yy, kk):
        return jnp.dot(wv[q], grad_of(plane, yy, kk), preferred_element_type=F32)

    lane = lax.broadcasted_iota(jnp.int32, (1, rows), 1)

    own_x()
    own_z()
    own_c()
    own_y()
    lg_in.append(remote(lg_hbm.at[last], lgo.at[last], xp, late=True))
    st1[yk, 0:1, :] = to_row(jnp.sum(low.astype(F32) * pred, axis=1, keepdims=True))
    st1[yk, 1:2, :] = jnp.where(lane == 0, jnp.sum(gene_cos), 0.0)
    st1_in = spread_to([(st1.at[yk], st1.at[yk], d) for d, _ in yk_peers], lambda n: st1.at[pl.ds(0, n)])
    start_c(0)
    take_x(z, False)
    wait_cy()
    at_distance(1, functools.partial(take_z, further=True))
    wait_cx()
    at_distance(3, take_z)
    start_c(2)
    at_distance(1, take_c(0, True))
    at_distance(2, take_z)
    start_c(1)
    own_core()
    take_y(z, False)
    wait_cd()
    aux_in()
    for wait in lg_in:
        wait()
    weights(lgo, 1.0 / aux[xo, 0:1, :], xo)
    start_c(3)
    at_distance(3, take_y)
    at_distance(1, take_c(2, True))
    at_distance(3, take_x)
    at_distance(1, take_y)
    at_distance(2, take_c(0))
    at_distance(3, take_c(0))
    st1_in()
    whole = added(st1, YK)
    st2[me, 0:1, :] = whole[0:1]
    st2[me, 1:2, :] = jnp.where(lane == 0, whole[1:2], jnp.where(lane == 1, jnp.sum(spot_cos), 0.0))
    st2_in = spread_to([(st2.at[me], st2.at[me], d) for d in xz_peers], lambda n: st2.at[pl.ds(0, n)])
    eg[y, k] = expr_term(x, here, y, k)
    at_distance(1, take_x)
    lgrad[...] = weight_term(y, k)
    at_distance(2, take_y)
    at_distance(3, take_c(2))
    landed(g.at[here, y, ko], core_in)
    eg[y, ko] = expr_term(x, here, y, ko)
    at_distance(1, take_c(1, True))
    at_distance(1, take_c(3, True))
    at_distance(2, take_x)
    lgrad[...] += weight_term(y, ko)
    at_distance(2, take_c(2))
    take_d(z, False)
    eg[yo, k] = expr_term(x, here, yo, k)
    lgrad[...] += weight_term(yo, k)
    at_distance(3, take_c(3))
    at_distance(3, take_c(1))
    at_distance(1, take_d)
    landed(g.at[here, yo, ko], core_in + 1)
    lgrad[...] += weight_term(yo, ko)
    at_distance(3, take_d)
    at_distance(2, take_c(1))
    at_distance(2, take_c(3))
    at_distance(2, take_d)
    eg[y, k] += expr_term(xo, there, y, k)

    kl = 0.0
    slide_mass, slide_count = [], []
    for s in range(2):
        m = n = cl = cm = 0.0
        for q in range(nx):
            of_s = jnp.abs(aux[q, 1:2, :] - s) < 0.5
            n_q = jnp.where(of_s, aux[q, 2:3, :], 0.0)
            m = m + jnp.sum(jnp.where(of_s, aux[q, 0:1, :], 0.0))
            n = n + jnp.sum(n_q)
            cl = cl + jnp.sum(n_q * jnp.log(aux[q, 2:3, :]))
            cm = cm + jnp.sum(n_q * jnp.log(aux[q, 0:1, :]))
        some = n > 0.5
        m = jnp.full((1, 128), jnp.where(some, m, 1.0), F32)
        n = jnp.full((1, 128), jnp.where(some, n, 1.0), F32)
        kl = kl + jnp.where(some, (cl - cm) / n - jnp.log(n) + jnp.log(m), 0.0)
        slide_mass.append(m[:, 0:1])
        slide_count.append(n[:, 0:1])
    is_second = slides > 0.5
    mass_grad = mass / jnp.where(is_second, slide_mass[1], slide_mass[0]) - counts / jnp.where(
        is_second, slide_count[1], slide_count[0]
    )
    st2_in()
    gene_total = whole[1:2]
    spot_total = added(st2, nx * nz)[1:2]
    loss_out[...] = (
        -jnp.sum(jnp.where(lane == 0, gene_total, 0.0)) / (2 * genes)
        - jnp.sum(jnp.where(lane == 1, spot_total, 0.0)) / spots
        + kl
    )
    vec[0:1, :] = inv_mass
    vec[1:2, :] = mass_grad - jnp.concatenate([st2[x * nz + q, 0:1, :] for q in range(nz)], axis=1)

    p_in()
    landed(g.at[there, y, ko], core_in + 2)
    landed(g.at[there, yo, ko], core_in + 3)
    for ref, i in sends + late_sends:
        left(ref, i)
    left(g.at[here, y, k, part_ab], y_out)
    left(g.at[here, y, k, part_ab], x_out)
    for i in (cy_out, cx_out, cd_out):
        left(g.at[me, y, k, part_c], i)
    left(g.at[here, yo, k, part_a], a_out)
    left(g.at[there, y, k, part_b], b_out)
    left(g.at[:, :, k], core_out)

    @pl.when(at_end)
    def _():
        left(g.at[pl.ds(0, 2), y, k, part_ab], z_out)
        left(g.at[pl.ds(0, 8), y, k, part_c], c_out)

    @pl.when(jnp.logical_not(at_end))
    def _():
        left(g.at[pl.ds(0, nz), y, k, part_ab], z_out)
        left(g.at[pl.ds(0, nz), y, k], c_out)

    needed = {kind: max(used[kind], taken[kind]) + kept[kind] for kind in kept}
    assert needed == size, needed


def backward_kernel(
    nz, w_ref, g_ref, part_ref, lgrad_ref, lg_ref, vec_ref, p_ref, loss_ref,
    eg_hbm, lgrad_hbm, pred_ref, total_ref, eg, lgrad, done,
):
    c = lax.axis_index("cells")
    x = lax.axis_index("spots")
    y, k = (c % YK) // 2, c % 2
    nx, cells, cols = w_ref.shape
    wide = g_ref.shape[4]
    tall = cells // 2
    xo = (x + 1) % nx
    copies = []

    def out(src, dst):
        cp = pltpu.make_async_copy(src, dst, done.at[len(copies)])
        cp.start()
        copies.append(cp)

    def genes_at(yy, kk):
        return eg_hbm.at[:, pl.ds(pl.multiple_of((yy * 2 + kk) * wide, wide), wide)]

    def term(q, yy, kk, r):
        block = g_ref[pl.ds(q * nz, nz), yy, kk].reshape(cols, wide)
        return jnp.dot(w_ref[q, r, :], block, preferred_element_type=F32)

    out(part_ref.at[y, k], genes_at(y, k))
    lgrad[...] = jnp.exp(lg_ref[...].astype(F32)) * vec_ref[0:1, :] * (lgrad_ref[...] + vec_ref[1:2, :])
    out(lgrad, lgrad_hbm)
    for i, (yy, kk) in enumerate(((y, 1 - k), (1 - y, k), (1 - y, 1 - k))):
        for n in range(2):
            r = pl.ds(n * tall, tall)
            mine = part_ref[yy, kk, r, :] if i < 2 else term(x, yy, kk, r)
            eg[i, r, :] = mine + term(xo, yy, kk, r)
            out(eg.at[i, r], genes_at(yy, kk).at[r])
    for b in range(YK):
        out(p_ref.at[b], pred_ref.at[:, b * wide : (b + 1) * wide])
    total_ref[...] = loss_ref[:, 0:1]
    for cp in copies:
        cp.wait()


def step(ncells, nx, logits, expression, spatial, slide_ids, spot_counts):
    cells, cols = logits.shape
    genes = expression.shape[1]
    nz = ncells // YK
    rows = cols // nz
    wide = genes // YK
    part = rows // YK
    half = wide // 2
    anywhere = pl.BlockSpec(memory_space=pl.ANY)
    whole = pl.BlockSpec(memory_space=pltpu.VMEM)
    *held, p, loss = pl.pallas_call(
        functools.partial(forward_kernel, nz, nx),
        out_shape=(
            pltpu.VMEM((nx, cells, cols), BF16),
            pltpu.VMEM((nx * nz, 2, 2, rows, wide), BF16),
            pltpu.VMEM((2, 2, cells, wide), F32),
            pltpu.VMEM((cells, cols), F32),
            pltpu.VMEM((cells, cols), BF16),
            pltpu.VMEM((2, cols), F32),
            pltpu.VMEM((YK, part, wide), F32),
            pltpu.VMEM((1, 128), F32),
        ),
        in_specs=[anywhere] * 5,
        out_specs=(whole,) * 8,
        scratch_shapes=[
            pltpu.VMEM((cells, cols), BF16),
            pltpu.VMEM((cols, cells), BF16),
            pltpu.VMEM((YK, cells, wide), F32),
            pltpu.VMEM((YK, cells, wide), BF16),
            pltpu.VMEM((YK, nz, rows, wide), F32),
            pltpu.VMEM((2, nz, rows, wide), F32),
            pltpu.VMEM((nz, rows, wide), BF16),
            pltpu.VMEM((nz, rows, wide), BF16),
            pltpu.VMEM((nz, rows, wide), BF16),
            pltpu.VMEM((nz, rows, wide), BF16),
            pltpu.VMEM((nz, rows, wide), BF16),
            pltpu.VMEM((YK, part, wide), F32),
            pltpu.VMEM((YK, part, wide), F32),
            pltpu.VMEM((2, cols), F32),
            pltpu.VMEM((2, cols), F32),
            pltpu.VMEM((2, cols), F32),
            pltpu.VMEM((2, cols), F32),
            pltpu.VMEM((2, cols), F32),
            pltpu.VMEM((nz, 2, cols), F32),
            pltpu.VMEM((nx, 4, cols), F32),
            pltpu.VMEM((nx * nz, 2, wide), F32),
            pltpu.VMEM((YK, 1, rows), F32),
            pltpu.VMEM((nx * nz, 4, wide), F32),
            pltpu.VMEM((YK, 2, rows), F32),
            pltpu.VMEM((YK, 2, rows), F32),
            pltpu.VMEM((nx * nz, 2, rows), F32),
            pltpu.VMEM((1, cols), jnp.int32),
            pltpu.VMEM((1, cols), jnp.int32),
            pltpu.SemaphoreType.DMA((8,)),
            pltpu.SemaphoreType.DMA((24,)),
            pltpu.SemaphoreType.DMA((18 + 12 * nz,)),
        ],
        compiler_params=pltpu.CompilerParams(
            collective_id=0, has_side_effects=True, vmem_limit_bytes=36 << 20
        ),
        name="forward_and_gather",
    )(
        *(
            pltpu.with_memory_space_constraint(v, pltpu.HBM)
            for v in (logits, expression, spatial, slide_ids, spot_counts)
        )
    )

    held = [pltpu.with_memory_space_constraint(v, pltpu.VMEM) for v in held]
    return pl.pallas_call(
        functools.partial(backward_kernel, nz),
        out_shape=(
            jax.ShapeDtypeStruct((cells, genes), F32),
            jax.ShapeDtypeStruct((cells, cols), F32),
            jax.ShapeDtypeStruct((part, genes), F32),
            jax.ShapeDtypeStruct((1, 1), F32),
        ),
        in_specs=[whole] * 8,
        out_specs=(anywhere, anywhere, anywhere, whole),
        scratch_shapes=[
            pltpu.VMEM((3, cells, wide), F32),
            pltpu.VMEM((cells, cols), F32),
            pltpu.SemaphoreType.DMA((12,)),
        ],
        compiler_params=pltpu.CompilerParams(vmem_limit_bytes=24 << 20),
        name="backward",
    )(*held, p, loss)


def kernel_step(ncells, nx, *args):
    grad_expr, grad_logits, predicted, loss = step(ncells, nx, *args)
    return (predicted[None], loss[0, 0], grad_logits, grad_expr)


def fits(ncells, nx, logits, expression, spatial):
    cells, cols = logits.shape
    genes = expression.shape[1]
    if ncells != 4 * YK or nx != 2 or cols % (ncells // YK) or genes % (YK * 256):
        return False
    rows = cols // (ncells // YK)
    held = (cells + rows) * genes * 8 + cells * cols * 16 + cols * genes * 16
    return rows % 128 == 0 and cells % 128 == 0 and held < 50 << 20


def plain_step(logits, expression, spatial, slide_ids, spot_counts):
    highest = lax.Precision.HIGHEST
    ncells = lax.axis_size("cells")
    nspots = lax.axis_size("spots")
    columns = logits.shape[1]
    genes = expression.shape[1]
    out_rows = columns // ncells
    scores = logits.astype(F32)
    col_peak = lax.pmax(jnp.max(scores, axis=0), "cells")
    shifted = jnp.exp(scores - col_peak)
    col_total = lax.psum(jnp.sum(shifted, axis=0), "cells")
    weights = shifted / col_total
    log_mass = col_peak + jnp.log(col_total)
    weights_low = weights.astype(BF16)
    expr_low = expression.astype(BF16)
    contract_first = (((0,), (0,)), ((), ()))
    predicted = lax.psum_scatter(
        lax.dot_general(weights_low, expr_low, contract_first, preferred_element_type=F32),
        "cells",
        scatter_dimension=0,
        tiled=True,
    )
    target = spatial[0]
    member_all = (slide_ids[0][:, None] == jnp.arange(2, dtype=jnp.int32)[None, :]).astype(F32)
    first_row = lax.axis_index("cells") * out_rows
    member_rows = lax.dynamic_slice_in_dim(member_all, first_row, out_rows, 0)
    gene_inner = jnp.dot(member_rows.T, predicted * target, precision=highest)
    gene_pred = jnp.dot(member_rows.T, predicted * predicted, precision=highest)
    gene_true = jnp.dot(member_rows.T, target * target, precision=highest)
    spot_inner = jnp.sum(predicted * target, axis=1)
    pred_scale = lax.rsqrt(jnp.sum(predicted * predicted, axis=1) + EPSILON)
    true_scale = lax.rsqrt(jnp.sum(target * target, axis=1) + EPSILON)
    spot_sum = jnp.sum(spot_inner * pred_scale * true_scale)
    counts_real = spot_counts[0].astype(F32)
    exp_mass = jnp.exp(log_mass)
    local_mass = jnp.dot(member_all.T, exp_mass, precision=highest)
    local_count = jnp.dot(member_all.T, counts_real, precision=highest)
    local_clog = jnp.dot(member_all.T, counts_real * jnp.log(counts_real), precision=highest)
    local_clse = jnp.dot(member_all.T, counts_real * log_mass, precision=highest)
    slide_mass, slide_count, count_log, count_lse = lax.psum(
        (local_mass, local_count, local_clog, local_clse), "spots"
    )
    gene_inner, gene_pred, gene_true, spot_total = lax.psum(
        (gene_inner, gene_pred, gene_true, spot_sum), ("cells", "spots")
    )
    gene_a = lax.rsqrt(gene_pred + EPSILON)
    gene_b = lax.rsqrt(gene_true + EPSILON)
    gene_cos = gene_inner * gene_a * gene_b
    total_spots = columns * nspots
    some = slide_count > 0.5
    slide_count = jnp.where(some, slide_count, 1.0)
    slide_mass = jnp.where(some, slide_mass, 1.0)
    kl_value = jnp.sum(
        jnp.where(
            some,
            (count_log - count_lse) / slide_count - jnp.log(slide_count) + jnp.log(slide_mass),
            0.0,
        )
    )
    loss = -jnp.mean(gene_cos) - spot_total / total_spots + kl_value
    gene_step = -1.0 / (2 * genes)
    inner_grad = gene_step * gene_a * gene_b
    square_grad = -0.5 * gene_step * gene_inner * gene_b * gene_a * gene_a * gene_a
    pred_grad = jnp.dot(member_rows, inner_grad, precision=highest) * target
    pred_grad = pred_grad + 2.0 * jnp.dot(member_rows, square_grad, precision=highest) * predicted
    spot_step = -1.0 / total_spots
    pred_grad = pred_grad + (spot_step * pred_scale * true_scale)[:, None] * target
    pred_grad = (
        pred_grad
        - (spot_step * spot_inner * pred_scale * pred_scale * pred_scale * true_scale)[:, None]
        * predicted
    )
    grad_low = pred_grad.astype(BF16)
    mass_grad = exp_mass / jnp.dot(
        member_all, slide_mass, precision=highest
    ) - counts_real / jnp.dot(member_all, slide_count, precision=highest)
    contract_genes = (((1,), (1,)), ((), ()))
    grad_all = lax.all_gather(grad_low, "cells", axis=0, tiled=True)
    expr_part = jnp.dot(weights_low, grad_all, preferred_element_type=F32)
    weight_grad = lax.dot_general(
        expr_low, grad_all, contract_genes, preferred_element_type=F32
    )
    col_inner = lax.psum(jnp.sum(weights * weight_grad, axis=0), "cells")
    logit_grad = weights * (weight_grad - col_inner + mass_grad)
    expr_grad = lax.psum(expr_part, "spots")
    return (predicted[None], loss, logit_grad, expr_grad)


def solution(mesh):
    ncells, nx = mesh.shape["cells"], mesh.shape["spots"]

    def per_device(*args):
        if fits(ncells, nx, *args[:3]):
            return kernel_step(ncells, nx, *args)
        return plain_step(*args)

    return jax.shard_map(
        per_device,
        mesh=mesh,
        in_specs=(
            P("cells", "spots"),
            P("cells", None),
            P("spots", "cells", None),
            P("spots", None),
            P("spots", None),
        ),
        out_specs=(P("spots", "cells", None), P(), P("cells", "spots"), P("cells", None)),
        check_vma=False,
    )
```
